128 devices in a mesh: az: 8 (over z, x_lo), rg: 16 (over x_hi, y, core).
Axes of the slice: x: 4 (x_hi: 2, x_lo: 2; x = x_hi * 2 + x_lo), y: 4, z: 4, core: 2. Of those that a mesh axis runs over, the one named last changes fastest.
Arguments:
- echo: float32 [2, 2048, 4096], P(None, 'az', 'rg'), may hold values from -6 to 6
- range_row: int32 [4096], replicated, may hold values from 0 to 63
- aperture: int32 [4096], replicated, may hold values from 640 to 1280
- centroid_table: int32 [64], replicated, may hold values from -160 to 160
- rate_table: float32 [64], replicated, may hold values from 10 to 60
Outputs:
- focused: float32 [2, 2048, 4096], P(None, 'az', 'rg')
The draws below stay inside these ranges and needn't reach their ends.
All inputs are finite; a program needn't handle non-finite values.
Results may differ from the reference program's by a relative error of at most 0.0003.
Values sent between devices are 32-bit elements; how exact they have to be, the bound alone decides.
A program may use at most 128 MiB of HBM per device.

```python
import math
import jax
import jax.numpy as jnp
from jax import lax

SEG = 256
NRG = 4096
NTAB = 64
BLOCK = 1280
NAZ = 2048
N_AZ = 8


def place_ends(array, stream_key, smallest, largest):
    longest = array.shape.index(max(array.shape))
    spots = []
    for shift in (0, 1):
        where = [jax.random.randint(jax.random.fold_in(stream_key, axis), (), 0, length) for axis, length in enumerate(array.shape)]
        where[longest] = (where[longest] + shift) % array.shape[longest]
        spots.append(tuple(where))
    return array.at[spots[0]].set(smallest).at[spots[1]].set(largest)


def block_scale(own_key, dims, pieces, smallest, top_value):
    loudness, own = 1.0, jax.random.fold_in(own_key, 6)
    for dim, parts in pieces:
        steps = jnp.exp(jax.random.uniform(jax.random.fold_in(own, dim), (parts,), jnp.float32, smallest / len(pieces), top_value / len(pieces)))
        loudness = loudness * jnp.repeat(steps, dims[dim] // parts).reshape([-1 if axis == dim else 1 for axis in range(len(dims))])
    return loudness


def noise(own_key, extent, width, reach, shards=(), kind=jnp.bfloat16):
    factor_of = block_scale(own_key, extent, shards, -0.22, 0.18) if shards else 1.0
    result = jax.random.normal(own_key, extent, jnp.float32) * width * factor_of
    return jnp.minimum(jnp.maximum(result, -reach), reach).astype(kind)


def setup_inputs(seed: int = 0) -> dict:
    streams_of = jax.random.split(jax.random.key(seed), 6)
    echo = noise(streams_of[0], (2, NAZ, NRG), 1.0, 6.0, ((1, 8), (2, 16)), jnp.float32)
    range_row = place_ends(jax.random.randint(streams_of[1], (NRG,), 0, NTAB), jax.random.fold_in(streams_of[1], 1), 0, NTAB - 1).astype(jnp.int32)
    aperture = place_ends(jax.random.randint(streams_of[2], (NRG,), BLOCK // 2, BLOCK + 1), jax.random.fold_in(streams_of[2], 1), BLOCK // 2, BLOCK).astype(jnp.int32)
    centroid_table = place_ends(jax.random.randint(streams_of[3], (NTAB,), 0 - BLOCK // 8, BLOCK // 8 + 1), jax.random.fold_in(streams_of[3], 1), 0 - BLOCK // 8, (BLOCK // 8 + 1) - 1).astype(jnp.int32)
    rate_table = jnp.clip(jnp.exp(jax.random.uniform(streams_of[4], (NTAB,), jnp.float32, math.log(10.0), math.log(60.0))), 10.0, 60.0)
    return {"echo": echo, "range_row": range_row, "aperture": aperture, "centroid_table": centroid_table, "rate_table": rate_table}


chirp_cycles = 300.0
beta_factor = 1.5
shift_gain = 0.2
migration_gain = 0.05

def doppler_terms(doppler_bin, centroid, length):
    offset = (doppler_bin - centroid + length // 2) % length - length // 2
    doppler = (centroid + offset).astype(jnp.float32) / length
    migration = jnp.sqrt(1.0 - beta_factor * doppler * doppler)
    scaling = 1.0 / migration - 1.0
    return (offset, migration, scaling)

def phase_one(scaling, range_time):
    lagged = range_time - shift_gain * scaling
    return -math.pi * chirp_cycles * scaling * lagged * lagged

def phase_two(migration, scaling, frequency, total):
    fraction = frequency.astype(jnp.float32) / total
    return math.pi * chirp_cycles * fraction * fraction * migration / (1.0 + scaling) + 2.0 * math.pi * migration_gain * scaling * frequency.astype(jnp.float32)

def phase_three(migration, scaling, pulse_rate, range_time):
    return 2.0 * math.pi * pulse_rate * (migration - 1.0) + math.pi * chirp_cycles * scaling * (1.0 + scaling) * range_time * range_time

def unit_turn(angle):
    return lax.complex(jnp.cos(angle), jnp.sin(angle))

def reference(echo, range_row, aperture, centroid_table, rate_table):
    length = 5 * SEG
    centroid = jnp.take(centroid_table, range_row).astype(jnp.int32)
    pulse_rate = jnp.take(rate_table, range_row)
    range_bins = jnp.arange(NRG, dtype=jnp.int32)
    range_time = (range_bins.astype(jnp.float32) + 0.5) / NRG - 0.5
    doppler_bins = jnp.arange(length, dtype=jnp.int32)
    offset, migration, scaling = doppler_terms(doppler_bins[:, None], centroid[None, :], length)
    unused, migration_zero, scaling_zero = doppler_terms(doppler_bins, jnp.zeros_like(doppler_bins), length)
    frequency = (range_bins + NRG // 2) % NRG - NRG // 2
    turn_one = unit_turn(phase_one(scaling, range_time[None, :]))
    turn_two = unit_turn(phase_two(migration_zero[:, None], scaling_zero[:, None], frequency[None, :], NRG))
    turn_three = unit_turn(phase_three(migration, scaling, pulse_rate[None, :], range_time[None, :]))
    keep = 2 * jnp.abs(offset) < aperture[None, :]
    padded = jnp.pad(echo, ((0, 0), (2 * SEG, 2 * SEG), (0, 0)))

    def one_block(index):
        block = lax.dynamic_slice_in_dim(padded, index * SEG, length, 1)
        field = lax.complex(block[0], block[1])
        field = jnp.fft.fft(field, axis=0, norm='ortho') * turn_one
        field = jnp.fft.fft(field, axis=1, norm='ortho') * turn_two
        field = jnp.fft.ifft(field, axis=1, norm='ortho') * turn_three
        field = jnp.where(keep, field, jnp.zeros_like(field))
        field = jnp.fft.ifft(field, axis=0, norm='ortho')[2 * SEG:3 * SEG]
        return jnp.stack([jnp.real(field), jnp.imag(field)])
    blocks = lax.map(one_block, jnp.arange(N_AZ, dtype=jnp.int32))
    return jnp.transpose(blocks, (1, 0, 2, 3)).reshape(2, N_AZ * SEG, NRG)
```

```python
from functools import partial
import math

import jax
import jax.numpy as jnp
import numpy as np
from jax import lax
from jax.experimental import pallas as pl
from jax.experimental.pallas import tpu as pltpu
from jax.sharding import PartitionSpec as P
import ml_dtypes

F32 = jnp.float32
BF16 = jnp.bfloat16
MESH = pl.DeviceIdType.MESH

SEG = 256
CLASSES = 5
LENGTH = SEG * CLASSES
GROUPS = 16
WIDTH = 256
TOTAL = GROUPS * WIDTH
LINES = SEG // GROUPS
HALF = 128
OTHERS = GROUPS - 1

STEPS = [
    (dx, dy, dc)
    for dc in (0, 1)
    for dx, dy in ((1, 2), (0, 2), (1, 1), (1, 3), (0, 1), (0, 3), (1, 0), (0, 0))
    if (dx, dy, dc) != (0, 0, 0)
]


def pair_split(values):
    high = values.astype(ml_dtypes.bfloat16)
    low = (values - high.astype(np.float64)).astype(ml_dtypes.bfloat16)
    return np.stack([high, low])


def azimuth_tables():
    p = np.arange(SEG)[None, :, None]
    m = np.arange(SEG)[None, None, :]
    q = np.arange(CLASSES)[:, None, None]
    turns = ((2 * SEG + p) * (CLASSES * m + q)) % LENGTH
    angle = turns * (2.0 * np.pi / LENGTH)
    scale = 1.0 / math.sqrt(LENGTH)
    cosine, sine = np.cos(angle) * scale, np.sin(angle) * scale
    inverse = np.concatenate([cosine, sine], axis=2)
    forward = np.concatenate([cosine.transpose(0, 2, 1), sine.transpose(0, 2, 1)], axis=2)
    return pair_split(forward).transpose(1, 0, 2, 3), pair_split(inverse).transpose(1, 0, 2, 3)


def range_tables():
    index = np.arange(WIDTH)
    angle = (index[:, None] * index[None, :] % WIDTH) * (2.0 * np.pi / WIDTH)
    cosine, sine = np.cos(angle), np.sin(angle)
    forward = np.block([[cosine, -sine], [sine, cosine]])
    inverse = np.block([[cosine, sine], [-sine, cosine]])
    fine = np.arange(GROUPS)[:, None] * index[None, :] * (2.0 * np.pi / TOTAL)
    twiddle = np.stack([np.cos(fine), np.sin(fine)]).astype(np.float32)
    return np.stack([pair_split(forward), pair_split(inverse)]), twiddle


def segment_weights():
    q = np.arange(CLASSES)[:, None]
    step = np.arange(1, 3)[None, :]
    angle = (q * step % CLASSES) * (2.0 * np.pi / CLASSES)
    return np.concatenate([np.cos(angle), np.sin(angle)], axis=1).astype(np.float32)


def split(value):
    high = value.astype(BF16)
    return high, (value - high.astype(F32)).astype(BF16)


def fitted(function, powers):
    nodes = np.cos((np.arange(400) + 0.5) * np.pi / 400) * 0.5
    nodes = nodes[nodes > 0]
    basis = np.stack([(2 * nodes) ** p for p in powers], axis=1)
    solved = np.linalg.lstsq(basis, function(2.0 * np.pi * nodes), rcond=None)[0]
    return [float(value * 2.0**p) for value, p in zip(solved, powers)]


SINE = fitted(np.sin, [1, 3, 5, 7, 9, 11])
COSINE = fitted(np.cos, [0, 2, 4, 6, 8, 10, 12])


def turn(cycles):
    left = cycles - jnp.floor(cycles + 0.5)
    square = left * left
    sine, cosine = SINE[-1], COSINE[-1]
    for value in SINE[-2::-1]:
        sine = sine * square + value
    for value in COSINE[-2::-1]:
        cosine = cosine * square + value
    return cosine, sine * left


def times_turn(value, quarter):
    real, imag = value
    quarter %= 4
    if quarter == 0:
        return real, imag
    if quarter == 1:
        return -imag, real
    if quarter == 2:
        return -real, -imag
    return imag, -real


def four(values, sign):
    a, b, c, d = values
    ac = (a[0] + c[0], a[1] + c[1])
    am = (a[0] - c[0], a[1] - c[1])
    bd = (b[0] + d[0], b[1] + d[1])
    bm = times_turn((b[0] - d[0], b[1] - d[1]), sign)
    return [
        (ac[0] + bd[0], ac[1] + bd[1]),
        (am[0] + bm[0], am[1] + bm[1]),
        (ac[0] - bd[0], ac[1] - bd[1]),
        (am[0] - bm[0], am[1] - bm[1]),
    ]


def sixteen(values, sign):
    inner = [four(values[low::4], sign) for low in range(4)]
    result = [None] * 16
    for first in range(4):
        column = []
        for low in range(4):
            real, imag = inner[low][first]
            step = low * first
            if step % 4 == 0:
                column.append(times_turn((real, imag), sign * (step // 4)))
            else:
                angle = sign * 2.0 * math.pi * step / 16
                cosine, sine = math.cos(angle), math.sin(angle)
                if step % 2 == 0:
                    root = math.sqrt(0.5)
                    up = 1.0 if cosine > 0 else -1.0
                    side = 1.0 if sine > 0 else -1.0
                    if up == side:
                        column.append(((real - imag) * (up * root), (real + imag) * (up * root)))
                    else:
                        column.append(((real + imag) * (up * root), (imag - real) * (up * root)))
                else:
                    column.append((real * cosine - imag * sine, real * sine + imag * cosine))
        outer = four(column, sign)
        for second in range(4):
            result[first + 4 * second] = outer[second]
    return result


def dot(left, right):
    return jnp.dot(left, right, preferred_element_type=F32)


def kernel(
    echo,
    range_row,
    aperture,
    twiddle,
    centroid_table,
    rate_table,
    weights,
    forward_hbm,
    inverse_hbm,
    range_hbm,
    out,
    forward,
    inverse,
    dense,
    halo,
    sums,
    made,
    got,
    back,
    home,
    one,
    two,
    three,
    centroid,
    rate,
    left,
    mixed,
    total,
    const_sem,
    halo_send,
    halo_recv,
    made_send,
    made_recv,
    back_send,
    back_recv,
):
    az = lax.axis_index("az")
    me = lax.axis_index("rg")
    high, middle, core = me // 8, (me // 2) % 4, me % 2
    partners = [
        ((high + dx) % 2) * 8 + ((middle + dy) % 4) * 2 + (core + dc) % 2 for dx, dy, dc in STEPS
    ]
    around = [(az + step) % 8 for step in (2, 6, 1, 7)]

    barrier = pltpu.get_barrier_semaphore()
    for other in around:
        pl.semaphore_signal(barrier, inc=1, device_id=(other, me), device_id_type=MESH)
    for partner in partners:
        pl.semaphore_signal(barrier, inc=1, device_id=(az, partner), device_id_type=MESH)
    consts = [
        pltpu.make_async_copy(range_hbm, dense, const_sem.at[0]),
        pltpu.make_async_copy(forward_hbm, forward, const_sem.at[1]),
        pltpu.make_async_copy(inverse_hbm, inverse, const_sem.at[2]),
    ]
    for copy in consts:
        copy.start()
    pl.semaphore_wait(barrier, len(around) + OTHERS)

    halo_copies = []
    for side in range(2):
        columns = pl.ds(side * HALF, HALF)
        for slot, other in enumerate(around):
            copy = pltpu.make_async_remote_copy(
                src_ref=echo.at[:, :, columns],
                dst_ref=halo.at[side, slot],
                send_sem=halo_send.at[side, slot],
                recv_sem=halo_recv.at[side, slot],
                device_id=(other, me),
                device_id_type=MESH,
            )
            copy.start()
            halo_copies.append(copy)

    rows = range_row[...]
    centers = jnp.zeros((GROUPS, WIDTH), jnp.int32)
    rates = jnp.zeros((GROUPS, WIDTH), F32)
    for entry in range(64):
        hit = rows == entry
        centers = jnp.where(hit, centroid_table[entry], centers)
        rates = jnp.where(hit, rate_table[entry], rates)
    centroid[...] = centers
    rate[...] = rates

    lane = lax.broadcasted_iota(jnp.int32, (LINES, WIDTH), 1)
    line = lax.broadcasted_iota(jnp.int32, (LINES, WIDTH), 0)

    def doppler(bins):
        fraction = bins.astype(F32) * (1.0 / LENGTH)
        squared = jnp.maximum(1.0 - 1.5 * fraction * fraction, 0.1)
        migration = jnp.sqrt(squared)
        return squared, migration, 1.0 / migration - 1.0

    def phases(q, carry):
        bins = CLASSES * (LINES * me + line) + q
        unused, low_migration, low_scaling = doppler(bins)
        unused, high_migration, high_scaling = doppler(bins - LENGTH)
        squared, unused, zero_scaling = doppler(jnp.where(bins < LENGTH // 2, bins, bins - LENGTH))
        square_gain = squared * (150.0 / (TOTAL * TOTAL))
        linear_gain = zero_scaling * 0.05

        def each_group(g, inner):
            here = pl.ds(g, 1)
            center = centroid[here, :]
            time = (g * WIDTH + lane).astype(F32) * (1.0 / TOTAL) + (0.5 / TOTAL - 0.5)
            low = bins <= center + (LENGTH // 2 - 1)
            migration = jnp.where(low, low_migration, high_migration)
            scaling = jnp.where(low, low_scaling, high_scaling)
            offset = jnp.where(low, bins, bins - LENGTH) - center
            lagged = time - 0.2 * scaling
            cosine, sine = turn(-150.0 * scaling * lagged * lagged)
            one[0, q, g] = cosine
            one[1, q, g] = sine
            cosine, sine = turn(
                rate[here, :] * (migration - 1.0) + 150.0 * scaling * (1.0 + scaling) * time * time
            )
            keep = jnp.where(2 * jnp.abs(offset) < aperture[here, :], 1.0 / TOTAL, 0.0)
            three[0, q, g] = cosine * keep
            three[1, q, g] = sine * keep
            frequency = (GROUPS * lane + g - jnp.where(lane >= HALF, TOTAL, 0)).astype(F32)
            cosine, sine = turn((square_gain * frequency + linear_gain) * frequency)
            two[0, q, g] = cosine
            two[1, q, g] = sine
            return inner

        return lax.fori_loop(0, GROUPS, each_group, carry)

    lax.fori_loop(0, CLASSES, phases, 0)

    consts[1].wait()
    valid = [
        jnp.where(az >= 2, 1.0, 0.0).astype(F32),
        jnp.where(az < 6, 1.0, 0.0).astype(F32),
        jnp.where(az >= 1, 1.0, 0.0).astype(F32),
        jnp.where(az < 7, 1.0, 0.0).astype(F32),
    ]
    mine = pl.ds(pl.multiple_of(me * LINES, LINES), LINES)
    for side in range(2):
        for slot in range(4):
            halo_copies[side * 4 + slot].wait_recv()
        for part in range(2):
            before_two = halo[side, 0, part] * valid[0]
            after_two = halo[side, 1, part] * valid[1]
            before_one = halo[side, 2, part] * valid[2]
            after_one = halo[side, 3, part] * valid[3]
            sums[0, part] = after_one + before_one
            sums[1, part] = after_two + before_two
            sums[2, part] = after_one - before_one
            sums[3, part] = after_two - before_two

        def azimuth(q, carry):
            c_one, c_two, s_one, s_two = (weights[q, i] for i in range(4))
            real = (
                echo[0, :, side * HALF : (side + 1) * HALF]
                + c_one * sums[0, 0]
                + c_two * sums[1, 0]
                + (s_one * sums[2, 1] + s_two * sums[3, 1])
            )
            imag = (
                echo[1, :, side * HALF : (side + 1) * HALF]
                + c_one * sums[0, 1]
                + c_two * sums[1, 1]
                - (s_one * sums[2, 0] + s_two * sums[3, 0])
            )
            real_high, real_low = split(real)
            imag_high, imag_low = split(imag)
            block_high = jnp.concatenate(
                [
                    jnp.concatenate([real_high, imag_high], axis=1),
                    jnp.concatenate([imag_high, -real_high], axis=1),
                ],
                axis=0,
            )
            block_low = jnp.concatenate(
                [
                    jnp.concatenate([real_low, imag_low], axis=1),
                    jnp.concatenate([imag_low, -real_low], axis=1),
                ],
                axis=0,
            )
            spectrum = (
                dot(forward[q, 0], block_high)
                + dot(forward[q, 1], block_high)
                + dot(forward[q, 0], block_low)
            )
            made[q, side, 0] = spectrum[:, :HALF]
            made[q, side, 1] = spectrum[:, HALF:]
            for partner in partners:
                theirs = pl.ds(pl.multiple_of(partner * LINES, LINES), LINES)
                pltpu.make_async_remote_copy(
                    src_ref=made.at[q, side, :, theirs, :],
                    dst_ref=got.at[q, side, me],
                    send_sem=made_send.at[q, side],
                    recv_sem=made_recv.at[q, side],
                    device_id=(az, partner),
                    device_id_type=MESH,
                ).start()
            got[q, side, me] = made[q, side, :, mine, :]
            return carry

        lax.fori_loop(0, CLASSES, azimuth, 0)

    consts[0].wait()

    def range_work(q, carry):
        for side in range(2):
            lot = got.at[q, side, pl.ds(0, OTHERS)]
            pltpu.make_async_copy(lot, lot, made_recv.at[q, side]).wait()
        for upper in range(2):
            some = slice(upper * 8, upper * 8 + 8)
            for side in range(2):
                columns = slice(side * HALF, (side + 1) * HALF)
                values = []
                for g in range(GROUPS):
                    real, imag = got[q, side, g, 0, some, :], got[q, side, g, 1, some, :]
                    cosine, sine = one[0, q, g, some, columns], one[1, q, g, some, columns]
                    values.append((real * cosine - imag * sine, real * sine + imag * cosine))
                values = sixteen(values, -1)
                for g in range(GROUPS):
                    real, imag = values[g]
                    cosine, sine = twiddle[0, g : g + 1, columns], twiddle[1, g : g + 1, columns]
                    values[g] = (real * cosine + imag * sine, imag * cosine - real * sine)
                for g in range(0, GROUPS, 2):
                    place = slice(upper * HALF + g * 8, upper * HALF + g * 8 + 16)
                    for part in range(2):
                        both = jnp.concatenate([values[g][part], values[g + 1][part]], axis=0)
                        spot = slice(part * WIDTH + side * HALF, part * WIDTH + (side + 1) * HALF)
                        left[0, place, spot], left[1, place, spot] = split(both)
        for upper in range(2):
            area = slice(upper * HALF, (upper + 1) * HALF)
            mixed[area, :] = (
                dot(left[0, area, :], dense[0, 0])
                + dot(left[0, area, :], dense[0, 1])
                + dot(left[1, area, :], dense[0, 0])
            )
        for upper in range(2):
            some = slice(upper * 8, upper * 8 + 8)
            for g in range(0, GROUPS, 2):
                place = slice(upper * HALF + g * 8, upper * HALF + g * 8 + 16)
                real, imag = mixed[place, :WIDTH], mixed[place, WIDTH:]
                cosine = jnp.concatenate([two[0, q, g, some, :], two[0, q, g + 1, some, :]], axis=0)
                sine = jnp.concatenate([two[1, q, g, some, :], two[1, q, g + 1, some, :]], axis=0)
                left[0, place, :WIDTH], left[1, place, :WIDTH] = split(real * cosine - imag * sine)
                left[0, place, WIDTH:], left[1, place, WIDTH:] = split(real * sine + imag * cosine)
        for upper in range(2):
            area = slice(upper * HALF, (upper + 1) * HALF)
            mixed[area, :] = (
                dot(left[0, area, :], dense[1, 0])
                + dot(left[0, area, :], dense[1, 1])
                + dot(left[1, area, :], dense[1, 0])
            )
        for upper in range(2):
            some = slice(upper * 8, upper * 8 + 8)
            for side in range(2):
                columns = slice(side * HALF, (side + 1) * HALF)
                values = []
                for g in range(GROUPS):
                    place = slice(upper * HALF + g * 8, upper * HALF + g * 8 + 8)
                    real = mixed[place, side * HALF : (side + 1) * HALF]
                    imag = mixed[place, WIDTH + side * HALF : WIDTH + (side + 1) * HALF]
                    cosine, sine = twiddle[0, g : g + 1, columns], twiddle[1, g : g + 1, columns]
                    values.append((real * cosine - imag * sine, real * sine + imag * cosine))
                values = sixteen(values, 1)
                for g in range(GROUPS):
                    real, imag = values[g]
                    cosine, sine = three[0, q, g, some, columns], three[1, q, g, some, columns]
                    back[q, g, 0, some, columns] = real * cosine - imag * sine
                    back[q, g, 1, some, columns] = real * sine + imag * cosine
        for partner in partners:
            pltpu.make_async_remote_copy(
                src_ref=back.at[q, partner],
                dst_ref=home.at[q, :, mine, :],
                send_sem=back_send.at[q],
                recv_sem=back_recv.at[q],
                device_id=(az, partner),
                device_id_type=MESH,
            ).start()
        home[q, :, mine, :] = back[q, me]
        return carry

    lax.fori_loop(0, CLASSES, range_work, 0)

    consts[2].wait()
    total[...] = jnp.zeros_like(total)

    def focus(q, carry):
        lot = back.at[q, pl.ds(0, OTHERS)]
        pltpu.make_async_copy(lot, lot, back_recv.at[q]).wait()
        real_high, real_low = split(home[q, 0])
        imag_high, imag_low = split(home[q, 1])
        block_high = jnp.concatenate(
            [
                jnp.concatenate([real_high, imag_high], axis=1),
                jnp.concatenate([-imag_high, real_high], axis=1),
            ],
            axis=0,
        )
        block_low = jnp.concatenate(
            [
                jnp.concatenate([real_low, imag_low], axis=1),
                jnp.concatenate([-imag_low, real_low], axis=1),
            ],
            axis=0,
        )
        total[...] += (
            dot(inverse[q, 0], block_high)
            + dot(inverse[q, 1], block_high)
            + dot(inverse[q, 0], block_low)
        )
        return carry

    lax.fori_loop(0, CLASSES, focus, 0)
    out[0] = total[:, :WIDTH]
    out[1] = total[:, WIDTH:]

    for copy in halo_copies:
        copy.wait_send()

    def drain(q, carry):
        for side in range(2):
            lot = got.at[q, side, pl.ds(0, OTHERS)]
            pltpu.make_async_copy(lot, lot, made_send.at[q, side]).wait()
        lot = back.at[q, pl.ds(0, OTHERS)]
        pltpu.make_async_copy(lot, lot, back_send.at[q]).wait()
        return carry

    lax.fori_loop(0, CLASSES, drain, 0)


def per_device(tables, echo, range_row, aperture, centroid_table, rate_table):
    forward, inverse, dense, twiddle, weights = tables
    vmem = pl.BlockSpec(memory_space=pltpu.VMEM)
    smem = pl.BlockSpec(memory_space=pltpu.SMEM)
    anywhere = pl.BlockSpec(memory_space=pl.ANY)
    semaphore = pltpu.SemaphoreType.DMA
    return pl.pallas_call(
        kernel,
        out_shape=jax.ShapeDtypeStruct((2, SEG, WIDTH), F32),
        in_specs=[vmem, vmem, vmem, vmem, smem, smem, smem, anywhere, anywhere, anywhere],
        out_specs=vmem,
        scratch_shapes=[
            pltpu.VMEM((CLASSES, 2, SEG, 2 * SEG), BF16),
            pltpu.VMEM((CLASSES, 2, SEG, 2 * SEG), BF16),
            pltpu.VMEM((2, 2, 2 * WIDTH, 2 * WIDTH), BF16),
            pltpu.VMEM((2, 4, 2, SEG, HALF), F32),
            pltpu.VMEM((4, 2, SEG, HALF), F32),
            pltpu.VMEM((CLASSES, 2, 2, SEG, HALF), F32),
            pltpu.VMEM((CLASSES, 2, GROUPS, 2, LINES, HALF), F32),
            pltpu.VMEM((CLASSES, GROUPS, 2, LINES, WIDTH), F32),
            pltpu.VMEM((CLASSES, 2, SEG, WIDTH), F32),
            pltpu.VMEM((2, CLASSES, GROUPS, LINES, WIDTH), F32),
            pltpu.VMEM((2, CLASSES, GROUPS, LINES, WIDTH), F32),
            pltpu.VMEM((2, CLASSES, GROUPS, LINES, WIDTH), F32),
            pltpu.VMEM((GROUPS, WIDTH), jnp.int32),
            pltpu.VMEM((GROUPS, WIDTH), F32),
            pltpu.VMEM((2, SEG, 2 * WIDTH), BF16),
            pltpu.VMEM((SEG, 2 * WIDTH), F32),
            pltpu.VMEM((SEG, 2 * WIDTH), F32),
            semaphore((3,)),
            semaphore((2, 4)),
            semaphore((2, 4)),
            semaphore((CLASSES, 2)),
            semaphore((CLASSES, 2)),
            semaphore((CLASSES,)),
            semaphore((CLASSES,)),
        ],
        compiler_params=pltpu.CompilerParams(
            collective_id=0, has_side_effects=True, vmem_limit_bytes=48 * 1024 * 1024
        ),
    )(
        echo,
        range_row.reshape(GROUPS, WIDTH),
        aperture.reshape(GROUPS, WIDTH),
        twiddle,
        centroid_table,
        rate_table,
        weights,
        forward,
        inverse,
        dense,
    )


def solution(mesh):
    forward, inverse = azimuth_tables()
    dense, twiddle = range_tables()
    tables = tuple(
        jnp.asarray(table) for table in (forward, inverse, dense, twiddle, segment_weights())
    )
    in_specs = (P(None, "az", "rg"), P(), P(), P(), P())
    out_specs = P(None, "az", "rg")
    return jax.shard_map(
        partial(per_device, tables),
        mesh=mesh,
        in_specs=in_specs,
        out_specs=out_specs,
        check_vma=False,
    )
```

```python
from functools import partial
import math

import jax
import jax.numpy as jnp
import numpy as np
from jax import lax
from jax.experimental import pallas as pl
from jax.experimental.pallas import tpu as pltpu
from jax.sharding import PartitionSpec as P
import ml_dtypes

F32 = jnp.float32
BF16 = jnp.bfloat16
MESH = pl.DeviceIdType.MESH

SEG = 256
CLASSES = 5
LENGTH = SEG * CLASSES
GROUPS = 16
WIDTH = 256
TOTAL = GROUPS * WIDTH
CHIPS = 64
LINES = SEG // CHIPS
ROWS = 2 * LINES
PAIRS = 4
HALF = 128


def links_of(step):
    load = np.zeros(6)
    for axis, hops in enumerate(step[:3]):
        load[2 * axis] += hops in (1, 2)
        load[2 * axis + 1] += hops in (2, 3)
    return load


def spread(steps):
    load, remaining, ordered = np.zeros(6), list(steps), []
    while remaining:
        levels = [
            (np.ptp(load + links_of(step)), -links_of(step).sum(), step) for step in remaining
        ]
        chosen = min(levels)[2]
        ordered.append(chosen)
        remaining.remove(chosen)
        load = load + links_of(chosen)
    return ordered


RING = range(4)
OUTWARD = spread([(dz, dx, dy) for dz in RING for dx in RING for dy in RING])
HOMEWARD = spread(
    [(dz, dx, dy, dc) for dz in RING for dx in (0, 2) for dy in RING for dc in (0, 1)]
)


def pair_split(values):
    high = values.astype(ml_dtypes.bfloat16)
    low = (values - high.astype(np.float64)).astype(ml_dtypes.bfloat16)
    return np.stack([high, low])


def azimuth_tables():
    pulse = np.arange(SEG)
    bins = np.arange(SEG)[None, :] * CLASSES + np.arange(CLASSES)[:, None]
    turns = ((2 * SEG + pulse)[None, :, None] * bins[:, None, :]) % LENGTH
    angle = turns * (2.0 * np.pi / LENGTH)
    scale = 1.0 / math.sqrt(LENGTH)
    cosine, sine = np.cos(angle) * scale, np.sin(angle) * scale
    real = np.stack([cosine, -sine]).reshape(2, CLASSES, SEG, CHIPS, LINES)
    imag = np.stack([sine, cosine]).reshape(2, CLASSES, SEG, CHIPS, LINES)
    inverse = np.stack([real, imag]).transpose(2, 0, 3, 4, 1, 5)
    inverse = inverse.reshape(CLASSES, 2 * SEG, CHIPS * ROWS)
    forward = inverse.transpose(0, 2, 1)
    return pair_split(forward).transpose(1, 0, 2, 3), pair_split(inverse).transpose(1, 0, 2, 3)


def range_tables():
    index = np.arange(WIDTH)
    angle = (index[:, None] * index[None, :] % WIDTH) * (2.0 * np.pi / WIDTH)
    cosine, sine = np.cos(angle), np.sin(angle)
    forward = np.block([[cosine, -sine], [sine, cosine]])
    inverse = np.block([[cosine, sine], [-sine, cosine]])
    fine = np.arange(GROUPS)[:, None] * index[None, :] * (2.0 * np.pi / TOTAL)
    twiddle = np.stack([np.cos(fine), np.sin(fine)]).astype(np.float32)
    return np.stack([pair_split(forward), pair_split(inverse)]), twiddle


WEIGHTS = [
    [
        (math.cos(2.0 * math.pi * q * step / CLASSES), math.sin(2.0 * math.pi * q * step / CLASSES))
        for step in (1, 2)
    ]
    for q in range(CLASSES)
]


def weight(q, step, part):
    value = jnp.float32(WEIGHTS[0][step - 1][part])
    for other in range(1, CLASSES):
        value = jnp.where(q == other, jnp.float32(WEIGHTS[other][step - 1][part]), value)
    return value


def split(value):
    high = value.astype(BF16)
    return high, (value - high.astype(F32)).astype(BF16)


def fitted(function, powers):
    nodes = np.cos((np.arange(400) + 0.5) * np.pi / 400) * 0.5
    nodes = nodes[nodes > 0]
    basis = np.stack([(2 * nodes) ** p for p in powers], axis=1)
    solved = np.linalg.lstsq(basis, function(2.0 * np.pi * nodes), rcond=None)[0]
    return [float(value * 2.0**p) for value, p in zip(solved, powers)]


SINE = fitted(np.sin, [1, 3, 5, 7, 9, 11])
COSINE = fitted(np.cos, [0, 2, 4, 6, 8, 10, 12])


def turn(cycles):
    left = cycles - jnp.floor(cycles + 0.5)
    square = left * left
    sine, cosine = SINE[-1], COSINE[-1]
    for value in SINE[-2::-1]:
        sine = sine * square + value
    for value in COSINE[-2::-1]:
        cosine = cosine * square + value
    return cosine, sine * left


def times_turn(value, quarter):
    real, imag = value
    quarter %= 4
    if quarter == 0:
        return real, imag
    if quarter == 1:
        return -imag, real
    if quarter == 2:
        return -real, -imag
    return imag, -real


def four(values, sign):
    a, b, c, d = values
    ac = (a[0] + c[0], a[1] + c[1])
    am = (a[0] - c[0], a[1] - c[1])
    bd = (b[0] + d[0], b[1] + d[1])
    bm = times_turn((b[0] - d[0], b[1] - d[1]), sign)
    return [
        (ac[0] + bd[0], ac[1] + bd[1]),
        (am[0] + bm[0], am[1] + bm[1]),
        (ac[0] - bd[0], ac[1] - bd[1]),
        (am[0] - bm[0], am[1] - bm[1]),
    ]


def sixteen(values, sign):
    inner = [four(values[low::4], sign) for low in range(4)]
    result = [None] * 16
    for first in range(4):
        column = []
        for low in range(4):
            real, imag = inner[low][first]
            step = low * first
            if step % 4 == 0:
                column.append(times_turn((real, imag), sign * (step // 4)))
            else:
                angle = sign * 2.0 * math.pi * step / 16
                cosine, sine = math.cos(angle), math.sin(angle)
                if step % 2 == 0:
                    root = math.sqrt(0.5)
                    up = 1.0 if cosine > 0 else -1.0
                    side = 1.0 if sine > 0 else -1.0
                    if up == side:
                        column.append(((real - imag) * (up * root), (real + imag) * (up * root)))
                    else:
                        column.append(((real + imag) * (up * root), (imag - real) * (up * root)))
                else:
                    column.append((real * cosine - imag * sine, real * sine + imag * cosine))
        outer = four(column, sign)
        for second in range(4):
            result[first + 4 * second] = outer[second]
    return result


def dot(left, right):
    return jnp.dot(left, right, preferred_element_type=F32)


def kernel(
    echo_hbm,
    range_row_hbm,
    aperture_hbm,
    centroid_hbm,
    rate_hbm,
    forward_hbm,
    inverse_hbm,
    dense_hbm,
    twiddle_hbm,
    out,
    echo,
    pulses,
    range_row,
    aperture,
    centroid_table,
    rate_table,
    forward,
    inverse,
    dense,
    twiddle,
    made,
    got,
    back,
    home,
    one,
    two,
    three,
    centroid,
    rate,
    left,
    mixed,
    total,
    load_sem,
    forward_sem,
    made_send,
    made_recv,
    swap_send,
    swap_recv,
    back_send,
    back_recv,
):
    az = lax.axis_index("az")
    me = lax.axis_index("rg")
    z, x_low = az // 2, az % 2
    x, y, core = (me // 8) * 2 + x_low, (me // 2) % 4, me % 2
    chip = z * 16 + x * 4 + y
    same = x_low == core
    apart = jnp.where(same, 0, 1)
    zs = [(z + step) % 4 for step in RING]
    xs = [(x + step) % 4 for step in RING]
    ys = [(y + step) % 4 for step in RING]
    cores = [core, 1 - core]
    near = {step: (x + apart + step) % 4 for step in (0, 2)}
    far = {step: (x + 1 - apart + step) % 4 for step in (0, 2)}

    def place(z_at, x_at, y_at, core_at):
        return (z_at * 2 + x_at % 2, (x_at // 2) * 8 + y_at * 2 + core_at)

    loads = [
        pltpu.make_async_copy(source, target, load_sem.at[i])
        for i, (source, target) in enumerate(
            (
                (echo_hbm, echo),
                (range_row_hbm, range_row),
                (aperture_hbm, aperture),
                (centroid_hbm, centroid_table),
                (rate_hbm, rate_table),
                (twiddle_hbm, twiddle),
                (dense_hbm, dense),
                (inverse_hbm, inverse),
            )
        )
    ]
    forward_loads = [
        pltpu.make_async_copy(forward_hbm.at[q], forward.at[q], forward_sem.at[q])
        for q in range(CLASSES)
    ]
    for copy in loads[:1] + forward_loads[:1] + loads[1:6] + forward_loads[1:] + loads[6:]:
        copy.start()

    barrier = pltpu.get_barrier_semaphore()

    def greet(target):
        pl.semaphore_signal(barrier, inc=1, device_id=target, device_id_type=MESH)

    for dz, dx, dy, dc in HOMEWARD:
        target = place(zs[dz], near[dx], ys[dy], cores[dc])
        if (dz, dx, dy, dc) == (0, 0, 0, 0):
            pl.when(jnp.logical_not(same))(partial(greet, target))
        else:
            greet(target)
    for dz in RING:
        for dx in (0, 2):
            for dy in RING:
                greet(place(zs[dz], far[dx], ys[dy], x_low))

    loads[0].wait()
    for part in range(2):
        rows = slice(part * SEG, (part + 1) * SEG)
        pulses[0, rows, :], pulses[1, rows, :] = split(echo[part])

    def azimuth(q, carry):
        pltpu.make_async_copy(forward_hbm.at[q], forward.at[q], forward_sem.at[q]).wait()
        spectrum = (
            dot(forward[q, 0], pulses[0])
            + dot(forward[q, 1], pulses[0])
            + dot(forward[q, 0], pulses[1])
        )
        made[q] = spectrum.reshape(CHIPS, ROWS, WIDTH)

        @pl.when(q == 0)
        def _():
            pl.semaphore_wait(barrier, 96 - jnp.where(same, 1, 0))

        for dz, dx, dy in OUTWARD:
            target = place(zs[dz], xs[dx], ys[dy], x_low)
            owner = zs[dz] * 16 + xs[dx] * 4 + ys[dy]

            def send():
                pltpu.make_async_remote_copy(
                    src_ref=made.at[q, owner],
                    dst_ref=got.at[q, x_low, z, me],
                    send_sem=made_send.at[q],
                    recv_sem=made_recv.at[q],
                    device_id=target,
                    device_id_type=MESH,
                ).start()

            def keep():
                pltpu.make_async_copy(
                    made.at[q, owner], got.at[q, x_low, z, me], made_recv.at[q]
                ).start()

            if (dz, dx, dy) == (0, 0, 0):
                pl.when(jnp.logical_not(same))(send)
                pl.when(same)(keep)
            else:
                send()
        return carry

    lax.fori_loop(0, CLASSES, azimuth, 0)

    for copy in loads[1:6]:
        copy.wait()
    for g in range(GROUPS):
        here = pl.ds(g * WIDTH, WIDTH)
        centroid[g : g + 1, :] = range_row[here].reshape(1, WIDTH)
    rows = centroid[...]
    centers = jnp.zeros((GROUPS, WIDTH), jnp.int32)
    rates = jnp.zeros((GROUPS, WIDTH), F32)
    for entry in range(64):
        hit = rows == entry
        centers = jnp.where(hit, centroid_table[entry], centers)
        rates = jnp.where(hit, rate_table[entry], rates)
    centroid[...] = centers
    rate[...] = rates

    lane = lax.broadcasted_iota(jnp.int32, (ROWS, WIDTH), 1)
    line = lax.broadcasted_iota(jnp.int32, (ROWS, WIDTH), 0) % LINES

    def doppler(bins):
        fraction = bins.astype(F32) * (1.0 / LENGTH)
        squared = jnp.maximum(1.0 - 1.5 * fraction * fraction, 0.1)
        migration = jnp.sqrt(squared)
        return squared, migration, 1.0 / migration - 1.0

    def phases(q, carry):
        bins = CLASSES * (LINES * chip + line) + q
        unused, low_migration, low_scaling = doppler(bins)
        unused, high_migration, high_scaling = doppler(bins - LENGTH)
        squared, unused, zero_scaling = doppler(jnp.where(bins < LENGTH // 2, bins, bins - LENGTH))
        square_gain = squared * (150.0 / (TOTAL * TOTAL))
        linear_gain = zero_scaling * 0.05

        def each_group(g, inner):
            here = pl.ds(g, 1)
            center = centroid[here, :]
            time = (g * WIDTH + lane).astype(F32) * (1.0 / TOTAL) + (0.5 / TOTAL - 0.5)
            low = bins <= center + (LENGTH // 2 - 1)
            migration = jnp.where(low, low_migration, high_migration)
            scaling = jnp.where(low, low_scaling, high_scaling)
            offset = jnp.where(low, bins, bins - LENGTH) - center
            lagged = time - 0.2 * scaling
            cosine, sine = turn(-150.0 * scaling * lagged * lagged)
            one[0, q, g] = cosine
            one[1, q, g] = sine
            cosine, sine = turn(
                rate[here, :] * (migration - 1.0) + 150.0 * scaling * (1.0 + scaling) * time * time
            )
            wide = aperture[pl.ds(pl.multiple_of(g * WIDTH, WIDTH), WIDTH)].reshape(1, WIDTH)
            keep = jnp.where(2 * jnp.abs(offset) < wide, 1.0 / TOTAL, 0.0)
            three[0, q, g] = cosine * keep
            three[1, q, g] = sine * keep
            frequency = (GROUPS * lane + g - jnp.where(lane >= HALF, TOTAL, 0)).astype(F32)
            cosine, sine = turn((square_gain * frequency + linear_gain) * frequency)
            two[0, q, g] = cosine
            two[1, q, g] = sine
            return inner

        return lax.fori_loop(0, GROUPS, each_group, carry)

    lax.fori_loop(0, CLASSES, phases, 0)

    sibling = (az, me + 1 - 2 * core)

    def swap(q):
        return pltpu.make_async_remote_copy(
            src_ref=got.at[q, core],
            dst_ref=got.at[q, core],
            send_sem=swap_send.at[q],
            recv_sem=swap_recv.at[q],
            device_id=sibling,
            device_id_type=MESH,
        )

    def arrive(q):
        lot = got.at[q, core]
        pltpu.make_async_copy(lot, lot, made_recv.at[q]).wait()
        swap(q).start()

    upper_rows = lax.broadcasted_iota(jnp.int32, (ROWS, HALF), 0) < LINES
    flip = jnp.where(upper_rows, 1.0, -1.0).astype(F32)
    first_before = core.astype(F32)
    last_after = 1.0 - first_before

    def turned_rows(value):
        return pltpu.roll(value, LINES, 0)

    def range_work(q, carry):
        @pl.when(q < CLASSES - 1)
        def _():
            arrive(q + 1)

        swap(q).wait_recv()
        c_one, s_one = weight(q, 1, 0), weight(q, 1, 1)
        c_two, s_two = weight(q, 2, 0), weight(q, 2, 1)

        def block(segment, g, columns):
            value = got[q, core, segment, g, :, columns]
            before = got[q, 1 - core, jnp.maximum(segment - 1 + core, 0), g, :, columns]
            after = got[q, 1 - core, jnp.minimum(segment + core, 3), g, :, columns]
            if segment == 0:
                before = before * first_before
            if segment == 3:
                after = after * last_after
            value = value + c_one * (after + before)
            side = s_one * (after - before)
            if segment > 0:
                before = got[q, core, segment - 1, g, :, columns]
                value = value + c_two * before
                side = side - s_two * before
            if segment < 3:
                after = got[q, core, segment + 1, g, :, columns]
                value = value + c_two * after
                side = side + s_two * after
            return value + flip * turned_rows(side)

        for upper in range(2):
            for side in range(2):
                columns = slice(side * HALF, (side + 1) * HALF)
                values = []
                for g in range(GROUPS):
                    first, second = (block(2 * upper + i, g, columns) for i in range(2))
                    real = jnp.where(upper_rows, first, turned_rows(second))
                    imag = jnp.where(upper_rows, turned_rows(first), second)
                    cosine, sine = one[0, q, g, :, columns], one[1, q, g, :, columns]
                    values.append((real * cosine - imag * sine, real * sine + imag * cosine))
                values = sixteen(values, -1)
                for g in range(GROUPS):
                    real, imag = values[g]
                    cosine, sine = twiddle[0, g : g + 1, columns], twiddle[1, g : g + 1, columns]
                    values[g] = (real * cosine + imag * sine, imag * cosine - real * sine)
                for g in range(0, GROUPS, 2):
                    spot = slice(upper * HALF + g * 8, upper * HALF + g * 8 + 16)
                    for part in range(2):
                        both = jnp.concatenate([values[g][part], values[g + 1][part]], axis=0)
                        lanes = slice(part * WIDTH + side * HALF, part * WIDTH + (side + 1) * HALF)
                        left[0, spot, lanes], left[1, spot, lanes] = split(both)
        for upper in range(2):
            area = slice(upper * HALF, (upper + 1) * HALF)
            mixed[area, :] = (
                dot(left[0, area, :], dense[0, 0])
                + dot(left[0, area, :], dense[0, 1])
                + dot(left[1, area, :], dense[0, 0])
            )
        for upper in range(2):
            for g in range(0, GROUPS, 2):
                spot = slice(upper * HALF + g * 8, upper * HALF + g * 8 + 16)
                real, imag = mixed[spot, :WIDTH], mixed[spot, WIDTH:]
                cosine = jnp.concatenate([two[0, q, g], two[0, q, g + 1]], axis=0)
                sine = jnp.concatenate([two[1, q, g], two[1, q, g + 1]], axis=0)
                left[0, spot, :WIDTH], left[1, spot, :WIDTH] = split(real * cosine - imag * sine)
                left[0, spot, WIDTH:], left[1, spot, WIDTH:] = split(real * sine + imag * cosine)
        for upper in range(2):
            area = slice(upper * HALF, (upper + 1) * HALF)
            mixed[area, :] = (
                dot(left[0, area, :], dense[1, 0])
                + dot(left[0, area, :], dense[1, 1])
                + dot(left[1, area, :], dense[1, 0])
            )
        for upper in range(2):
            for side in range(2):
                columns = slice(side * HALF, (side + 1) * HALF)
                values = []
                for g in range(GROUPS):
                    spot = slice(upper * HALF + g * 8, upper * HALF + g * 8 + 8)
                    real = mixed[spot, side * HALF : (side + 1) * HALF]
                    imag = mixed[spot, WIDTH + side * HALF : WIDTH + (side + 1) * HALF]
                    cosine, sine = twiddle[0, g : g + 1, columns], twiddle[1, g : g + 1, columns]
                    values.append((real * cosine - imag * sine, real * sine + imag * cosine))
                values = sixteen(values, 1)
                for g in range(GROUPS):
                    real, imag = values[g]
                    cosine, sine = three[0, q, g, :, columns], three[1, q, g, :, columns]
                    real, imag = real * cosine - imag * sine, real * sine + imag * cosine
                    first = 2 * upper * GROUPS + g
                    back[q, first, :, columns] = jnp.where(upper_rows, real, turned_rows(imag))
                    back[q, first + GROUPS, :, columns] = jnp.where(
                        upper_rows, turned_rows(real), imag
                    )
        for dz, dx, dy, dc in HOMEWARD:
            target = place(zs[dz], near[dx], ys[dy], cores[dc])
            piece = zs[dz] * GROUPS + target[1]

            def send():
                pltpu.make_async_remote_copy(
                    src_ref=back.at[q, piece],
                    dst_ref=home.at[q, chip],
                    send_sem=back_send.at[q],
                    recv_sem=back_recv.at[q],
                    device_id=target,
                    device_id_type=MESH,
                ).start()

            def keep():
                pltpu.make_async_copy(
                    back.at[q, piece], home.at[q, chip], back_recv.at[q]
                ).start()

            if (dz, dx, dy, dc) == (0, 0, 0, 0):
                pl.when(jnp.logical_not(same))(send)
                pl.when(same)(keep)
            else:
                send()
        return carry

    arrive(0)
    loads[6].wait()
    lax.fori_loop(0, CLASSES, range_work, 0)

    loads[7].wait()
    total[...] = jnp.zeros_like(total)

    def focus(q, carry):
        lot = home.at[q]
        pltpu.make_async_copy(lot, lot, back_recv.at[q]).wait()
        high, low = split(home[q].reshape(CHIPS * ROWS, WIDTH))
        total[...] += (
            dot(inverse[q, 0], high) + dot(inverse[q, 1], high) + dot(inverse[q, 0], low)
        )
        return carry

    lax.fori_loop(0, CLASSES, focus, 0)
    out[0] = total[:SEG, :]
    out[1] = total[SEG:, :]

    def drain(q, carry):
        swap(q).wait_send()

        @pl.when(same)
        def _():
            for buffer, semaphore in ((made, made_send), (back, back_send)):
                lot = buffer.at[q, pl.ds(0, CHIPS - 1)]
                pltpu.make_async_copy(lot, lot, semaphore.at[q]).wait()

        @pl.when(jnp.logical_not(same))
        def _():
            for buffer, semaphore in ((made, made_send), (back, back_send)):
                lot = buffer.at[q]
                pltpu.make_async_copy(lot, lot, semaphore.at[q]).wait()

        return carry

    lax.fori_loop(0, CLASSES, drain, 0)


def per_device(tables, echo, range_row, aperture, centroid_table, rate_table):
    hbm = pl.BlockSpec(memory_space=pltpu.HBM)
    semaphore = pltpu.SemaphoreType.DMA
    return pl.pallas_call(
        kernel,
        out_shape=jax.ShapeDtypeStruct((2, SEG, WIDTH), F32),
        in_specs=[hbm] * 9,
        out_specs=pl.BlockSpec(memory_space=pltpu.VMEM),
        scratch_shapes=[
            pltpu.VMEM((2, SEG, WIDTH), F32),
            pltpu.VMEM((2, 2 * SEG, WIDTH), BF16),
            pltpu.VMEM((TOTAL,), jnp.int32),
            pltpu.VMEM((TOTAL,), jnp.int32),
            pltpu.SMEM((64,), jnp.int32),
            pltpu.SMEM((64,), F32),
            pltpu.VMEM((CLASSES, 2, 2 * SEG, 2 * SEG), BF16),
            pltpu.VMEM((CLASSES, 2, 2 * SEG, 2 * SEG), BF16),
            pltpu.VMEM((2, 2, 2 * WIDTH, 2 * WIDTH), BF16),
            pltpu.VMEM((2, GROUPS, WIDTH), F32),
            pltpu.VMEM((CLASSES, CHIPS, ROWS, WIDTH), F32),
            pltpu.VMEM((CLASSES, 2, PAIRS, GROUPS, ROWS, WIDTH), F32),
            pltpu.VMEM((CLASSES, CHIPS, ROWS, WIDTH), F32),
            pltpu.VMEM((CLASSES, CHIPS, ROWS, WIDTH), F32),
            pltpu.VMEM((2, CLASSES, GROUPS, ROWS, WIDTH), F32),
            pltpu.VMEM((2, CLASSES, GROUPS, ROWS, WIDTH), F32),
            pltpu.VMEM((2, CLASSES, GROUPS, ROWS, WIDTH), F32),
            pltpu.VMEM((GROUPS, WIDTH), jnp.int32),
            pltpu.VMEM((GROUPS, WIDTH), F32),
            pltpu.VMEM((2, 2 * HALF, 2 * WIDTH), BF16),
            pltpu.VMEM((2 * HALF, 2 * WIDTH), F32),
            pltpu.VMEM((2 * SEG, WIDTH), F32),
            semaphore((8,)),
            semaphore((CLASSES,)),
            semaphore((CLASSES,)),
            semaphore((CLASSES,)),
            semaphore((CLASSES,)),
            semaphore((CLASSES,)),
            semaphore((CLASSES,)),
            semaphore((CLASSES,)),
        ],
        compiler_params=pltpu.CompilerParams(
            collective_id=0, has_side_effects=True, vmem_limit_bytes=52 * 1024 * 1024
        ),
    )(echo, range_row, aperture, centroid_table, rate_table, *tables)


def solution(mesh):
    forward, inverse = azimuth_tables()
    dense, twiddle = range_tables()
    tables = tuple(jnp.asarray(table) for table in (forward, inverse, dense, twiddle))
    in_specs = (P(None, "az", "rg"), P(), P(), P(), P())
    out_specs = P(None, "az", "rg")
    return jax.shard_map(
        partial(per_device, tables),
        mesh=mesh,
        in_specs=in_specs,
        out_specs=out_specs,
        check_vma=False,
    )
```

```python
from functools import partial
import math

import jax
import jax.numpy as jnp
import numpy as np
from jax import lax
from jax.experimental import pallas as pl
from jax.experimental.pallas import tpu as pltpu
from jax.sharding import PartitionSpec as P
import ml_dtypes

F32 = jnp.float32
BF16 = jnp.bfloat16
MESH = pl.DeviceIdType.MESH

SEG = 256
CLASSES = 5
LENGTH = SEG * CLASSES
GROUPS = 16
WIDTH = 256
TOTAL = GROUPS * WIDTH
CHIPS = 64
LINES = SEG // CHIPS
ROWS = 2 * LINES
PAIRS = 4
HALF = 128


def links_of(step):
    load = np.zeros(6)
    for axis, hops in enumerate(step[:3]):
        load[2 * axis] += hops in (1, 2)
        load[2 * axis + 1] += hops in (2, 3)
    return load


def spread(steps):
    load, remaining, ordered = np.zeros(6), list(steps), []
    while remaining:
        levels = [
            (np.ptp(load + links_of(step)), -links_of(step).sum(), step) for step in remaining
        ]
        chosen = min(levels)[2]
        ordered.append(chosen)
        remaining.remove(chosen)
        load = load + links_of(chosen)
    return ordered


RING = range(4)
OUTWARD = spread([(dz, dx, dy) for dz in RING for dx in RING for dy in RING])
HOMEWARD = spread(
    [(dz, dx, dy, dc) for dz in RING for dx in (0, 2) for dy in RING for dc in (0, 1)]
)


def pair_split(values):
    high = values.astype(ml_dtypes.bfloat16)
    low = (values - high.astype(np.float64)).astype(ml_dtypes.bfloat16)
    return np.stack([high, low])


def azimuth_tables():
    pulse = np.arange(SEG)
    bins = np.arange(SEG)[None, :] * CLASSES + np.arange(CLASSES)[:, None]
    turns = ((2 * SEG + pulse)[None, :, None] * bins[:, None, :]) % LENGTH
    angle = turns * (2.0 * np.pi / LENGTH)
    scale = 1.0 / math.sqrt(LENGTH)
    cosine, sine = np.cos(angle) * scale, np.sin(angle) * scale
    real = np.stack([cosine, -sine]).reshape(2, CLASSES, SEG, CHIPS, LINES)
    imag = np.stack([sine, cosine]).reshape(2, CLASSES, SEG, CHIPS, LINES)
    inverse = np.stack([real, imag]).transpose(2, 0, 3, 4, 1, 5)
    inverse = inverse.reshape(CLASSES, 2 * SEG, CHIPS * ROWS)
    forward = inverse.transpose(0, 2, 1)
    return pair_split(forward).transpose(1, 0, 2, 3), pair_split(inverse).transpose(1, 0, 2, 3)


def range_tables():
    index = np.arange(WIDTH)
    angle = (index[:, None] * index[None, :] % WIDTH) * (2.0 * np.pi / WIDTH)
    cosine, sine = np.cos(angle), np.sin(angle)
    forward = np.block([[cosine, -sine], [sine, cosine]])
    inverse = np.block([[cosine, sine], [-sine, cosine]])
    fine = np.arange(GROUPS)[:, None] * index[None, :] * (2.0 * np.pi / TOTAL)
    twiddle = np.stack([np.cos(fine), np.sin(fine)]).astype(np.float32)
    return np.stack([pair_split(forward), pair_split(inverse)]), twiddle


WEIGHTS = [
    [
        (math.cos(2.0 * math.pi * q * step / CLASSES), math.sin(2.0 * math.pi * q * step / CLASSES))
        for step in (1, 2)
    ]
    for q in range(CLASSES)
]


def weight(q, step, part):
    value = jnp.float32(WEIGHTS[0][step - 1][part])
    for other in range(1, CLASSES):
        value = jnp.where(q == other, jnp.float32(WEIGHTS[other][step - 1][part]), value)
    return value


def split(value):
    high = value.astype(BF16)
    return high, (value - high.astype(F32)).astype(BF16)


def fitted(function, powers):
    nodes = np.cos((np.arange(400) + 0.5) * np.pi / 400) * 0.5
    nodes = nodes[nodes > 0]
    basis = np.stack([(2 * nodes) ** p for p in powers], axis=1)
    solved = np.linalg.lstsq(basis, function(2.0 * np.pi * nodes), rcond=None)[0]
    return [float(value * 2.0**p) for value, p in zip(solved, powers)]


SINE = fitted(np.sin, [1, 3, 5, 7, 9, 11])
COSINE = fitted(np.cos, [0, 2, 4, 6, 8, 10, 12])


def turn(cycles):
    left = cycles - jnp.floor(cycles + 0.5)
    square = left * left
    sine, cosine = SINE[-1], COSINE[-1]
    for value in SINE[-2::-1]:
        sine = sine * square + value
    for value in COSINE[-2::-1]:
        cosine = cosine * square + value
    return cosine, sine * left


def times_turn(value, quarter):
    real, imag = value
    quarter %= 4
    if quarter == 0:
        return real, imag
    if quarter == 1:
        return -imag, real
    if quarter == 2:
        return -real, -imag
    return imag, -real


def four(values, sign):
    a, b, c, d = values
    ac = (a[0] + c[0], a[1] + c[1])
    am = (a[0] - c[0], a[1] - c[1])
    bd = (b[0] + d[0], b[1] + d[1])
    bm = times_turn((b[0] - d[0], b[1] - d[1]), sign)
    return [
        (ac[0] + bd[0], ac[1] + bd[1]),
        (am[0] + bm[0], am[1] + bm[1]),
        (ac[0] - bd[0], ac[1] - bd[1]),
        (am[0] - bm[0], am[1] - bm[1]),
    ]


def sixteen(values, sign):
    inner = [four(values[low::4], sign) for low in range(4)]
    result = [None] * 16
    for first in range(4):
        column = []
        for low in range(4):
            real, imag = inner[low][first]
            step = low * first
            if step % 4 == 0:
                column.append(times_turn((real, imag), sign * (step // 4)))
            else:
                angle = sign * 2.0 * math.pi * step / 16
                cosine, sine = math.cos(angle), math.sin(angle)
                if step % 2 == 0:
                    root = math.sqrt(0.5)
                    up = 1.0 if cosine > 0 else -1.0
                    side = 1.0 if sine > 0 else -1.0
                    if up == side:
                        column.append(((real - imag) * (up * root), (real + imag) * (up * root)))
                    else:
                        column.append(((real + imag) * (up * root), (imag - real) * (up * root)))
                else:
                    column.append((real * cosine - imag * sine, real * sine + imag * cosine))
        outer = four(column, sign)
        for second in range(4):
            result[first + 4 * second] = outer[second]
    return result


def dot(left, right):
    return jnp.dot(left, right, preferred_element_type=F32)


def kernel(
    echo_hbm,
    range_row_hbm,
    aperture_hbm,
    centroid_hbm,
    rate_hbm,
    forward_hbm,
    inverse_hbm,
    dense_hbm,
    twiddle_hbm,
    out,
    echo,
    pulses,
    range_row,
    aperture,
    centroid_table,
    rate_table,
    forward,
    inverse,
    dense,
    twiddle,
    made,
    got,
    back,
    home,
    one,
    two,
    three,
    centroid,
    rate,
    left,
    mixed,
    total,
    load_sem,
    forward_sem,
    made_send,
    made_recv,
    swap_send,
    swap_recv,
    back_send,
    back_recv,
):
    az = lax.axis_index("az")
    me = lax.axis_index("rg")
    z, x_low = az // 2, az % 2
    x, y, core = (me // 8) * 2 + x_low, (me // 2) % 4, me % 2
    chip = z * 16 + x * 4 + y
    same = x_low == core
    apart = jnp.where(same, 0, 1)
    zs = [(z + step) % 4 for step in RING]
    xs = [(x + step) % 4 for step in RING]
    ys = [(y + step) % 4 for step in RING]
    cores = [core, 1 - core]
    near = {step: (x + apart + step) % 4 for step in (0, 2)}

    def place(z_at, x_at, y_at, core_at):
        return (z_at * 2 + x_at % 2, (x_at // 2) * 8 + y_at * 2 + core_at)

    loads = [
        pltpu.make_async_copy(source, target, load_sem.at[i])
        for i, (source, target) in enumerate(
            (
                (echo_hbm, echo),
                (range_row_hbm, range_row),
                (aperture_hbm, aperture),
                (centroid_hbm, centroid_table),
                (rate_hbm, rate_table),
                (twiddle_hbm, twiddle),
                (dense_hbm, dense),
                (inverse_hbm, inverse),
            )
        )
    ]
    forward_loads = [
        pltpu.make_async_copy(forward_hbm.at[q], forward.at[q], forward_sem.at[q])
        for q in range(CLASSES)
    ]
    loads[0].start()
    forward_loads[0].start()

    barrier = pltpu.get_barrier_semaphore()

    def greet(target):
        pl.semaphore_signal(barrier, inc=1, device_id=target, device_id_type=MESH)

    for dz, dx, dy, dc in HOMEWARD:
        target = place(zs[dz], near[dx], ys[dy], cores[dc])
        if (dz, dx, dy, dc) == (0, 0, 0, 0):
            pl.when(jnp.logical_not(same))(partial(greet, target))
        else:
            greet(target)

    for copy in forward_loads[1:] + loads[1:]:
        copy.start()
    loads[0].wait()
    for part in range(2):
        rows = slice(part * SEG, (part + 1) * SEG)
        pulses[0, rows, :], pulses[1, rows, :] = split(echo[part])

    def azimuth(q, carry):
        pltpu.make_async_copy(forward_hbm.at[q], forward.at[q], forward_sem.at[q]).wait()
        spectrum = (
            dot(forward[q, 0], pulses[0])
            + dot(forward[q, 1], pulses[0])
            + dot(forward[q, 0], pulses[1])
        )
        made[q] = spectrum.reshape(CHIPS, ROWS, WIDTH)

        @pl.when(q == 0)
        def _():
            pl.semaphore_wait(barrier, CHIPS - jnp.where(same, 1, 0))

        for dz, dx, dy in OUTWARD:
            target = place(zs[dz], xs[dx], ys[dy], x_low)
            owner = zs[dz] * 16 + xs[dx] * 4 + ys[dy]

            def send():
                pltpu.make_async_remote_copy(
                    src_ref=made.at[q, owner],
                    dst_ref=got.at[q, x_low, z, me],
                    send_sem=made_send.at[q],
                    recv_sem=made_recv.at[q],
                    device_id=target,
                    device_id_type=MESH,
                ).start()

            def keep():
                pltpu.make_async_copy(
                    made.at[q, owner], got.at[q, x_low, z, me], made_recv.at[q]
                ).start()

            if (dz, dx, dy) == (0, 0, 0):
                pl.when(jnp.logical_not(same))(send)
                pl.when(same)(keep)
            else:
                send()
        return carry

    lax.fori_loop(0, CLASSES, azimuth, 0)

    for copy in loads[1:6]:
        copy.wait()
    for g in range(GROUPS):
        here = pl.ds(g * WIDTH, WIDTH)
        centroid[g : g + 1, :] = range_row[here].reshape(1, WIDTH)
    rows = centroid[...]
    centers = jnp.zeros((GROUPS, WIDTH), jnp.int32)
    rates = jnp.zeros((GROUPS, WIDTH), F32)
    for entry in range(64):
        hit = rows == entry
        centers = jnp.where(hit, centroid_table[entry], centers)
        rates = jnp.where(hit, rate_table[entry], rates)
    centroid[...] = centers
    rate[...] = rates

    lane = lax.broadcasted_iota(jnp.int32, (ROWS, WIDTH), 1)
    line = lax.broadcasted_iota(jnp.int32, (ROWS, WIDTH), 0) % LINES

    def doppler(bins):
        fraction = bins.astype(F32) * (1.0 / LENGTH)
        squared = jnp.maximum(1.0 - 1.5 * fraction * fraction, 0.1)
        migration = jnp.sqrt(squared)
        return squared, migration, 1.0 / migration - 1.0

    def phases(q, carry):
        bins = CLASSES * (LINES * chip + line) + q
        unused, low_migration, low_scaling = doppler(bins)
        unused, high_migration, high_scaling = doppler(bins - LENGTH)
        squared, unused, zero_scaling = doppler(jnp.where(bins < LENGTH // 2, bins, bins - LENGTH))
        square_gain = squared * (150.0 / (TOTAL * TOTAL))
        linear_gain = zero_scaling * 0.05

        def each_group(g, inner):
            here = pl.ds(g, 1)
            center = centroid[here, :]
            time = (g * WIDTH + lane).astype(F32) * (1.0 / TOTAL) + (0.5 / TOTAL - 0.5)
            low = bins <= center + (LENGTH // 2 - 1)
            migration = jnp.where(low, low_migration, high_migration)
            scaling = jnp.where(low, low_scaling, high_scaling)
            offset = jnp.where(low, bins, bins - LENGTH) - center
            lagged = time - 0.2 * scaling
            cosine, sine = turn(-150.0 * scaling * lagged * lagged)
            one[0, q, g] = cosine
            one[1, q, g] = sine
            cosine, sine = turn(
                rate[here, :] * (migration - 1.0) + 150.0 * scaling * (1.0 + scaling) * time * time
            )
            wide = aperture[pl.ds(pl.multiple_of(g * WIDTH, WIDTH), WIDTH)].reshape(1, WIDTH)
            keep = jnp.where(2 * jnp.abs(offset) < wide, 1.0 / TOTAL, 0.0)
            three[0, q, g] = cosine * keep
            three[1, q, g] = sine * keep
            frequency = (GROUPS * lane + g - jnp.where(lane >= HALF, TOTAL, 0)).astype(F32)
            cosine, sine = turn((square_gain * frequency + linear_gain) * frequency)
            two[0, q, g] = cosine
            two[1, q, g] = sine
            return inner

        return lax.fori_loop(0, GROUPS, each_group, carry)

    lax.fori_loop(0, CLASSES, phases, 0)

    sibling = (az, me + 1 - 2 * core)

    def swap(q):
        return pltpu.make_async_remote_copy(
            src_ref=got.at[q, core],
            dst_ref=got.at[q, core],
            send_sem=swap_send.at[q],
            recv_sem=swap_recv.at[q],
            device_id=sibling,
            device_id_type=MESH,
        )

    def arrive(q):
        lot = got.at[q, core]
        pltpu.make_async_copy(lot, lot, made_recv.at[q]).wait()
        swap(q).start()

    upper_rows = lax.broadcasted_iota(jnp.int32, (ROWS, HALF), 0) < LINES
    flip = jnp.where(upper_rows, 1.0, -1.0).astype(F32)
    first_before = core.astype(F32)
    last_after = 1.0 - first_before

    def turned_rows(value):
        return pltpu.roll(value, LINES, 0)

    def range_work(q, carry):
        @pl.when(q < CLASSES - 1)
        def _():
            arrive(q + 1)

        swap(q).wait_recv()
        c_one, s_one = weight(q, 1, 0), weight(q, 1, 1)
        c_two, s_two = weight(q, 2, 0), weight(q, 2, 1)

        def block(segment, g, columns):
            value = got[q, core, segment, g, :, columns]
            before = got[q, 1 - core, jnp.maximum(segment - 1 + core, 0), g, :, columns]
            after = got[q, 1 - core, jnp.minimum(segment + core, 3), g, :, columns]
            if segment == 0:
                before = before * first_before
            if segment == 3:
                after = after * last_after
            value = value + c_one * (after + before)
            side = s_one * (after - before)
            if segment > 0:
                before = got[q, core, segment - 1, g, :, columns]
                value = value + c_two * before
                side = side - s_two * before
            if segment < 3:
                after = got[q, core, segment + 1, g, :, columns]
                value = value + c_two * after
                side = side + s_two * after
            return value + flip * turned_rows(side)

        for upper in range(2):
            for side in range(2):
                columns = slice(side * HALF, (side + 1) * HALF)
                values = []
                for g in range(GROUPS):
                    first, second = (block(2 * upper + i, g, columns) for i in range(2))
                    real = jnp.where(upper_rows, first, turned_rows(second))
                    imag = jnp.where(upper_rows, turned_rows(first), second)
                    cosine, sine = one[0, q, g, :, columns], one[1, q, g, :, columns]
                    values.append((real * cosine - imag * sine, real * sine + imag * cosine))
                values = sixteen(values, -1)
                for g in range(GROUPS):
                    real, imag = values[g]
                    cosine, sine = twiddle[0, g : g + 1, columns], twiddle[1, g : g + 1, columns]
                    values[g] = (real * cosine + imag * sine, imag * cosine - real * sine)
                for g in range(0, GROUPS, 2):
                    spot = slice(upper * HALF + g * 8, upper * HALF + g * 8 + 16)
                    for part in range(2):
                        both = jnp.concatenate([values[g][part], values[g + 1][part]], axis=0)
                        lanes = slice(part * WIDTH + side * HALF, part * WIDTH + (side + 1) * HALF)
                        left[0, spot, lanes], left[1, spot, lanes] = split(both)
        for upper in range(2):
            area = slice(upper * HALF, (upper + 1) * HALF)
            mixed[area, :] = (
                dot(left[0, area, :], dense[0, 0])
                + dot(left[0, area, :], dense[0, 1])
                + dot(left[1, area, :], dense[0, 0])
            )
        for upper in range(2):
            for g in range(0, GROUPS, 2):
                spot = slice(upper * HALF + g * 8, upper * HALF + g * 8 + 16)
                real, imag = mixed[spot, :WIDTH], mixed[spot, WIDTH:]
                cosine = jnp.concatenate([two[0, q, g], two[0, q, g + 1]], axis=0)
                sine = jnp.concatenate([two[1, q, g], two[1, q, g + 1]], axis=0)
                left[0, spot, :WIDTH], left[1, spot, :WIDTH] = split(real * cosine - imag * sine)
                left[0, spot, WIDTH:], left[1, spot, WIDTH:] = split(real * sine + imag * cosine)
        for upper in range(2):
            area = slice(upper * HALF, (upper + 1) * HALF)
            mixed[area, :] = (
                dot(left[0, area, :], dense[1, 0])
                + dot(left[0, area, :], dense[1, 1])
                + dot(left[1, area, :], dense[1, 0])
            )
        for upper in range(2):
            for side in range(2):
                columns = slice(side * HALF, (side + 1) * HALF)
                values = []
                for g in range(GROUPS):
                    spot = slice(upper * HALF + g * 8, upper * HALF + g * 8 + 8)
                    real = mixed[spot, side * HALF : (side + 1) * HALF]
                    imag = mixed[spot, WIDTH + side * HALF : WIDTH + (side + 1) * HALF]
                    cosine, sine = twiddle[0, g : g + 1, columns], twiddle[1, g : g + 1, columns]
                    values.append((real * cosine - imag * sine, real * sine + imag * cosine))
                values = sixteen(values, 1)
                for g in range(GROUPS):
                    real, imag = values[g]
                    cosine, sine = three[0, q, g, :, columns], three[1, q, g, :, columns]
                    real, imag = real * cosine - imag * sine, real * sine + imag * cosine
                    first = 2 * upper * GROUPS + g
                    back[q, first, :, columns] = jnp.where(upper_rows, real, turned_rows(imag))
                    back[q, first + GROUPS, :, columns] = jnp.where(
                        upper_rows, turned_rows(real), imag
                    )
        for dz, dx, dy, dc in HOMEWARD:
            target = place(zs[dz], near[dx], ys[dy], cores[dc])
            piece = zs[dz] * GROUPS + target[1]

            def send():
                pltpu.make_async_remote_copy(
                    src_ref=back.at[q, piece],
                    dst_ref=home.at[q, chip],
                    send_sem=back_send.at[q],
                    recv_sem=back_recv.at[q],
                    device_id=target,
                    device_id_type=MESH,
                ).start()

            def keep():
                pltpu.make_async_copy(
                    back.at[q, piece], home.at[q, chip], back_recv.at[q]
                ).start()

            if (dz, dx, dy, dc) == (0, 0, 0, 0):
                pl.when(jnp.logical_not(same))(send)
                pl.when(same)(keep)
            else:
                send()
        return carry

    arrive(0)
    loads[6].wait()
    lax.fori_loop(0, CLASSES, range_work, 0)

    def drain(buffer, semaphore, q):
        @pl.when(same)
        def _():
            lot = buffer.at[q, pl.ds(0, CHIPS - 1)]
            pltpu.make_async_copy(lot, lot, semaphore.at[q]).wait()

        @pl.when(jnp.logical_not(same))
        def _():
            lot = buffer.at[q]
            pltpu.make_async_copy(lot, lot, semaphore.at[q]).wait()

    def drain_forward(q, carry):
        swap(q).wait_send()
        drain(made, made_send, q)
        return carry

    lax.fori_loop(0, CLASSES, drain_forward, 0)

    loads[7].wait()

    def focused(q):
        lot = home.at[q]
        pltpu.make_async_copy(lot, lot, back_recv.at[q]).wait()
        high, low = split(home[q].reshape(CHIPS * ROWS, WIDTH))
        return dot(inverse[q, 0], high) + dot(inverse[q, 1], high) + dot(inverse[q, 0], low)

    total[...] = focused(0)

    def focus(q, carry):
        total[...] += focused(q)
        drain(back, back_send, q - 1)
        return carry

    lax.fori_loop(1, CLASSES - 1, focus, 0)
    drain(back, back_send, CLASSES - 2)
    result = total[...] + focused(CLASSES - 1)
    out[0] = result[:SEG, :]
    out[1] = result[SEG:, :]
    drain(back, back_send, CLASSES - 1)


def per_device(tables, echo, range_row, aperture, centroid_table, rate_table):
    hbm = pl.BlockSpec(memory_space=pltpu.HBM)
    semaphore = pltpu.SemaphoreType.DMA
    return pl.pallas_call(
        kernel,
        out_shape=jax.ShapeDtypeStruct((2, SEG, WIDTH), F32),
        in_specs=[hbm] * 9,
        out_specs=pl.BlockSpec(memory_space=pltpu.VMEM),
        scratch_shapes=[
            pltpu.VMEM((2, SEG, WIDTH), F32),
            pltpu.VMEM((2, 2 * SEG, WIDTH), BF16),
            pltpu.VMEM((TOTAL,), jnp.int32),
            pltpu.VMEM((TOTAL,), jnp.int32),
            pltpu.SMEM((64,), jnp.int32),
            pltpu.SMEM((64,), F32),
            pltpu.VMEM((CLASSES, 2, 2 * SEG, 2 * SEG), BF16),
            pltpu.VMEM((CLASSES, 2, 2 * SEG, 2 * SEG), BF16),
            pltpu.VMEM((2, 2, 2 * WIDTH, 2 * WIDTH), BF16),
            pltpu.VMEM((2, GROUPS, WIDTH), F32),
            pltpu.VMEM((CLASSES, CHIPS, ROWS, WIDTH), F32),
            pltpu.VMEM((CLASSES, 2, PAIRS, GROUPS, ROWS, WIDTH), F32),
            pltpu.VMEM((CLASSES, CHIPS, ROWS, WIDTH), F32),
            pltpu.VMEM((CLASSES, CHIPS, ROWS, WIDTH), F32),
            pltpu.VMEM((2, CLASSES, GROUPS, ROWS, WIDTH), F32),
            pltpu.VMEM((2, CLASSES, GROUPS, ROWS, WIDTH), F32),
            pltpu.VMEM((2, CLASSES, GROUPS, ROWS, WIDTH), F32),
            pltpu.VMEM((GROUPS, WIDTH), jnp.int32),
            pltpu.VMEM((GROUPS, WIDTH), F32),
            pltpu.VMEM((2, 2 * HALF, 2 * WIDTH), BF16),
            pltpu.VMEM((2 * HALF, 2 * WIDTH), F32),
            pltpu.VMEM((2 * SEG, WIDTH), F32),
            semaphore((8,)),
            semaphore((CLASSES,)),
            semaphore((CLASSES,)),
            semaphore((CLASSES,)),
            semaphore((CLASSES,)),
            semaphore((CLASSES,)),
            semaphore((CLASSES,)),
            semaphore((CLASSES,)),
        ],
        compiler_params=pltpu.CompilerParams(
            collective_id=0, has_side_effects=True, vmem_limit_bytes=63 * 1024 * 1024
        ),
    )(echo, range_row, aperture, centroid_table, rate_table, *tables)


def solution(mesh):
    forward, inverse = azimuth_tables()
    dense, twiddle = range_tables()
    tables = tuple(jnp.asarray(table) for table in (forward, inverse, dense, twiddle))
    in_specs = (P(None, "az", "rg"), P(), P(), P(), P())
    out_specs = P(None, "az", "rg")
    return jax.shard_map(
        partial(per_device, tables),
        mesh=mesh,
        in_specs=in_specs,
        out_specs=out_specs,
        check_vma=False,
    )
```

```python
from functools import partial
import math

import jax
import jax.numpy as jnp
import numpy as np
from jax import lax
from jax.experimental import pallas as pl
from jax.experimental.pallas import tpu as pltpu
from jax.sharding import PartitionSpec as P
import ml_dtypes

F32 = jnp.float32
BF16 = jnp.bfloat16
MESH = pl.DeviceIdType.MESH

SEG = 256
CLASSES = 5
LENGTH = SEG * CLASSES
GROUPS = 16
WIDTH = 256
TOTAL = GROUPS * WIDTH
CHIPS = 64
LINES = SEG // CHIPS
ROWS = 2 * LINES
PAIRS = 4
HALF = 128


def links_of(step):
    load = np.zeros(6)
    for axis, hops in enumerate(step[:3]):
        load[2 * axis] += hops in (1, 2)
        load[2 * axis + 1] += hops in (2, 3)
    return load


def hops(step):
    return sum(min(count, 4 - count) for count in step[:3])


def spread(steps):
    load, remaining, ordered = np.zeros(6), list(steps), []
    while remaining:
        levels = [
            (np.ptp(load + links_of(step)), -links_of(step).sum(), step) for step in remaining
        ]
        chosen = min(levels)[2]
        ordered.append(chosen)
        remaining.remove(chosen)
        load = load + links_of(chosen)
    return ordered


RING = range(4)
OUTWARD = spread([(dz, dx, dy) for dz in RING for dx in RING for dy in RING])
HOMEWARD = spread(
    [(dz, dx, dy, dc) for dz in RING for dx in (0, 2) for dy in RING for dc in (0, 1)]
)


def pair_split(values):
    high = values.astype(ml_dtypes.bfloat16)
    low = (values - high.astype(np.float64)).astype(ml_dtypes.bfloat16)
    return np.stack([high, low])


def azimuth_tables():
    pulse = np.arange(SEG)
    bins = np.arange(SEG)[None, :] * CLASSES + np.arange(CLASSES)[:, None]
    turns = ((2 * SEG + pulse)[None, :, None] * bins[:, None, :]) % LENGTH
    angle = turns * (2.0 * np.pi / LENGTH)
    scale = 1.0 / math.sqrt(LENGTH)
    cosine, sine = np.cos(angle) * scale, np.sin(angle) * scale
    real = np.stack([cosine, -sine]).reshape(2, CLASSES, SEG, CHIPS, LINES)
    imag = np.stack([sine, cosine]).reshape(2, CLASSES, SEG, CHIPS, LINES)
    inverse = np.stack([real, imag]).transpose(2, 0, 3, 4, 1, 5)
    inverse = inverse.reshape(CLASSES, 2 * SEG, CHIPS * ROWS)
    forward = inverse.transpose(0, 2, 1)
    return pair_split(forward).transpose(1, 0, 2, 3), pair_split(inverse).transpose(1, 0, 2, 3)


def range_tables():
    index = np.arange(WIDTH)
    angle = (index[:, None] * index[None, :] % WIDTH) * (2.0 * np.pi / WIDTH)
    cosine, sine = np.cos(angle), np.sin(angle)
    forward = np.block([[cosine, -sine], [sine, cosine]])
    inverse = np.block([[cosine, sine], [-sine, cosine]])
    fine = np.arange(GROUPS)[:, None] * index[None, :] * (2.0 * np.pi / TOTAL)
    twiddle = np.stack([np.cos(fine), np.sin(fine)]).astype(np.float32)
    return np.stack([pair_split(forward), pair_split(inverse)]), twiddle


WEIGHTS = [
    [
        (math.cos(2.0 * math.pi * q * step / CLASSES), math.sin(2.0 * math.pi * q * step / CLASSES))
        for step in (1, 2)
    ]
    for q in range(CLASSES)
]


def weight(q, step, part):
    value = jnp.float32(WEIGHTS[0][step - 1][part])
    for other in range(1, CLASSES):
        value = jnp.where(q == other, jnp.float32(WEIGHTS[other][step - 1][part]), value)
    return value


def split(value):
    high = value.astype(BF16)
    return high, (value - high.astype(F32)).astype(BF16)


def fitted(function, powers):
    nodes = np.cos((np.arange(400) + 0.5) * np.pi / 400) * 0.5
    nodes = nodes[nodes > 0]
    basis = np.stack([(2 * nodes) ** p for p in powers], axis=1)
    solved = np.linalg.lstsq(basis, function(2.0 * np.pi * nodes), rcond=None)[0]
    return [float(value * 2.0**p) for value, p in zip(solved, powers)]


SINE = fitted(np.sin, [1, 3, 5, 7, 9, 11])
COSINE = fitted(np.cos, [0, 2, 4, 6, 8, 10, 12])


def turn(cycles):
    left = cycles - jnp.floor(cycles + 0.5)
    square = left * left
    sine, cosine = SINE[-1], COSINE[-1]
    for value in SINE[-2::-1]:
        sine = sine * square + value
    for value in COSINE[-2::-1]:
        cosine = cosine * square + value
    return cosine, sine * left


def times_turn(value, quarter):
    real, imag = value
    quarter %= 4
    if quarter == 0:
        return real, imag
    if quarter == 1:
        return -imag, real
    if quarter == 2:
        return -real, -imag
    return imag, -real


def four(values, sign):
    a, b, c, d = values
    ac = (a[0] + c[0], a[1] + c[1])
    am = (a[0] - c[0], a[1] - c[1])
    bd = (b[0] + d[0], b[1] + d[1])
    bm = times_turn((b[0] - d[0], b[1] - d[1]), sign)
    return [
        (ac[0] + bd[0], ac[1] + bd[1]),
        (am[0] + bm[0], am[1] + bm[1]),
        (ac[0] - bd[0], ac[1] - bd[1]),
        (am[0] - bm[0], am[1] - bm[1]),
    ]


def sixteen(values, sign):
    inner = [four(values[low::4], sign) for low in range(4)]
    result = [None] * 16
    for first in range(4):
        column = []
        for low in range(4):
            real, imag = inner[low][first]
            step = low * first
            if step % 4 == 0:
                column.append(times_turn((real, imag), sign * (step // 4)))
            else:
                angle = sign * 2.0 * math.pi * step / 16
                cosine, sine = math.cos(angle), math.sin(angle)
                if step % 2 == 0:
                    root = math.sqrt(0.5)
                    up = 1.0 if cosine > 0 else -1.0
                    side = 1.0 if sine > 0 else -1.0
                    if up == side:
                        column.append(((real - imag) * (up * root), (real + imag) * (up * root)))
                    else:
                        column.append(((real + imag) * (up * root), (imag - real) * (up * root)))
                else:
                    column.append((real * cosine - imag * sine, real * sine + imag * cosine))
        outer = four(column, sign)
        for second in range(4):
            result[first + 4 * second] = outer[second]
    return result


def dot(left, right):
    return jnp.dot(left, right, preferred_element_type=F32)


def kernel(
    echo_hbm,
    range_row_hbm,
    aperture_hbm,
    centroid_hbm,
    rate_hbm,
    forward_hbm,
    inverse_hbm,
    dense_hbm,
    twiddle_hbm,
    out,
    echo,
    pulses,
    range_row,
    aperture,
    centroid_table,
    rate_table,
    forward,
    inverse,
    dense,
    twiddle,
    made,
    got,
    back,
    home,
    one,
    two,
    three,
    centroid,
    rate,
    left,
    mixed,
    total,
    load_sem,
    forward_sem,
    made_send,
    made_recv,
    swap_send,
    swap_recv,
    back_send,
    back_recv,
):
    az = lax.axis_index("az")
    me = lax.axis_index("rg")
    z, x_low = az // 2, az % 2
    x, y, core = (me // 8) * 2 + x_low, (me // 2) % 4, me % 2
    chip = z * 16 + x * 4 + y
    same = x_low == core
    apart = jnp.where(same, 0, 1)
    zs = [(z + step) % 4 for step in RING]
    xs = [(x + step) % 4 for step in RING]
    ys = [(y + step) % 4 for step in RING]
    cores = [core, 1 - core]
    near = {step: (x + apart + step) % 4 for step in (0, 2)}

    def place(z_at, x_at, y_at, core_at):
        return (z_at * 2 + x_at % 2, (x_at // 2) * 8 + y_at * 2 + core_at)

    loads = [
        pltpu.make_async_copy(source, target, load_sem.at[i])
        for i, (source, target) in enumerate(
            (
                (echo_hbm, echo),
                (range_row_hbm, range_row),
                (aperture_hbm, aperture),
                (centroid_hbm, centroid_table),
                (rate_hbm, rate_table),
                (twiddle_hbm, twiddle),
                (dense_hbm, dense),
                (inverse_hbm, inverse),
            )
        )
    ]
    forward_loads = [
        pltpu.make_async_copy(forward_hbm.at[q], forward.at[q], forward_sem.at[q])
        for q in range(CLASSES)
    ]
    loads[0].start()
    forward_loads[0].start()

    barrier = pltpu.get_barrier_semaphore()

    def greet(target):
        pl.semaphore_signal(barrier, inc=1, device_id=target, device_id_type=MESH)

    for dz, dx, dy, dc in sorted(HOMEWARD, key=hops, reverse=True):
        target = place(zs[dz], near[dx], ys[dy], cores[dc])
        if (dz, dx, dy, dc) == (0, 0, 0, 0):
            pl.when(jnp.logical_not(same))(partial(greet, target))
        else:
            greet(target)

    for copy in forward_loads[1:] + loads[1:]:
        copy.start()
    loads[0].wait()
    for part in range(2):
        rows = slice(part * SEG, (part + 1) * SEG)
        pulses[0, rows, :], pulses[1, rows, :] = split(echo[part])

    def azimuth(q, carry):
        pltpu.make_async_copy(forward_hbm.at[q], forward.at[q], forward_sem.at[q]).wait()
        spectrum = (
            dot(forward[q, 0], pulses[0])
            + dot(forward[q, 1], pulses[0])
            + dot(forward[q, 0], pulses[1])
        )
        made[q] = spectrum.reshape(CHIPS, ROWS, WIDTH)

        @pl.when(q == 0)
        def _():
            pl.semaphore_wait(barrier, CHIPS - jnp.where(same, 1, 0))

        for dz, dx, dy in OUTWARD:
            target = place(zs[dz], xs[dx], ys[dy], x_low)
            owner = zs[dz] * 16 + xs[dx] * 4 + ys[dy]

            def send():
                pltpu.make_async_remote_copy(
                    src_ref=made.at[q, owner],
                    dst_ref=got.at[q, x_low, z, me],
                    send_sem=made_send.at[q],
                    recv_sem=made_recv.at[q],
                    device_id=target,
                    device_id_type=MESH,
                ).start()

            def keep():
                pltpu.make_async_copy(
                    made.at[q, owner], got.at[q, x_low, z, me], made_recv.at[q]
                ).start()

            if (dz, dx, dy) == (0, 0, 0):
                pl.when(jnp.logical_not(same))(send)
                pl.when(same)(keep)
            else:
                send()
        return carry

    lax.fori_loop(0, CLASSES, azimuth, 0)

    for copy in loads[1:6]:
        copy.wait()
    for g in range(GROUPS):
        here = pl.ds(g * WIDTH, WIDTH)
        centroid[g : g + 1, :] = range_row[here].reshape(1, WIDTH)
    rows = centroid[...]
    centers = jnp.zeros((GROUPS, WIDTH), jnp.int32)
    rates = jnp.zeros((GROUPS, WIDTH), F32)
    for entry in range(64):
        hit = rows == entry
        centers = jnp.where(hit, centroid_table[entry], centers)
        rates = jnp.where(hit, rate_table[entry], rates)
    centroid[...] = centers
    rate[...] = rates

    lane = lax.broadcasted_iota(jnp.int32, (ROWS, WIDTH), 1)
    line = lax.broadcasted_iota(jnp.int32, (ROWS, WIDTH), 0) % LINES

    def doppler(bins):
        fraction = bins.astype(F32) * (1.0 / LENGTH)
        squared = jnp.maximum(1.0 - 1.5 * fraction * fraction, 0.1)
        migration = jnp.sqrt(squared)
        return squared, migration, 1.0 / migration - 1.0

    def phases(q, carry):
        bins = CLASSES * (LINES * chip + line) + q
        unused, low_migration, low_scaling = doppler(bins)
        unused, high_migration, high_scaling = doppler(bins - LENGTH)
        squared, unused, zero_scaling = doppler(jnp.where(bins < LENGTH // 2, bins, bins - LENGTH))
        square_gain = squared * (150.0 / (TOTAL * TOTAL))
        linear_gain = zero_scaling * 0.05

        def each_group(g, inner):
            here = pl.ds(g, 1)
            center = centroid[here, :]
            time = (g * WIDTH + lane).astype(F32) * (1.0 / TOTAL) + (0.5 / TOTAL - 0.5)
            low = bins <= center + (LENGTH // 2 - 1)
            migration = jnp.where(low, low_migration, high_migration)
            scaling = jnp.where(low, low_scaling, high_scaling)
            offset = jnp.where(low, bins, bins - LENGTH) - center
            lagged = time - 0.2 * scaling
            cosine, sine = turn(-150.0 * scaling * lagged * lagged)
            one[0, q, g] = cosine
            one[1, q, g] = sine
            cosine, sine = turn(
                rate[here, :] * (migration - 1.0) + 150.0 * scaling * (1.0 + scaling) * time * time
            )
            wide = aperture[pl.ds(pl.multiple_of(g * WIDTH, WIDTH), WIDTH)].reshape(1, WIDTH)
            keep = jnp.where(2 * jnp.abs(offset) < wide, 1.0 / TOTAL, 0.0)
            three[0, q, g] = cosine * keep
            three[1, q, g] = sine * keep
            frequency = (GROUPS * lane + g - jnp.where(lane >= HALF, TOTAL, 0)).astype(F32)
            cosine, sine = turn((square_gain * frequency + linear_gain) * frequency)
            two[0, q, g] = cosine
            two[1, q, g] = sine
            return inner

        return lax.fori_loop(0, GROUPS, each_group, carry)

    lax.fori_loop(0, CLASSES, phases, 0)

    sibling = (az, me + 1 - 2 * core)

    def swap(q):
        return pltpu.make_async_remote_copy(
            src_ref=got.at[q, core],
            dst_ref=got.at[q, core],
            send_sem=swap_send.at[q],
            recv_sem=swap_recv.at[q],
            device_id=sibling,
            device_id_type=MESH,
        )

    def arrive(q):
        lot = got.at[q, core]
        pltpu.make_async_copy(lot, lot, made_recv.at[q]).wait()
        swap(q).start()

    upper_rows = lax.broadcasted_iota(jnp.int32, (ROWS, HALF), 0) < LINES
    flip = jnp.where(upper_rows, 1.0, -1.0).astype(F32)
    first_before = core.astype(F32)
    last_after = 1.0 - first_before

    def turned_rows(value):
        return pltpu.roll(value, LINES, 0)

    def range_work(q, carry):
        @pl.when(q < CLASSES - 1)
        def _():
            arrive(q + 1)

        swap(q).wait_recv()
        c_one, s_one = weight(q, 1, 0), weight(q, 1, 1)
        c_two, s_two = weight(q, 2, 0), weight(q, 2, 1)

        def block(segment, g, columns):
            value = got[q, core, segment, g, :, columns]
            before = got[q, 1 - core, jnp.maximum(segment - 1 + core, 0), g, :, columns]
            after = got[q, 1 - core, jnp.minimum(segment + core, 3), g, :, columns]
            if segment == 0:
                before = before * first_before
            if segment == 3:
                after = after * last_after
            value = value + c_one * (after + before)
            side = s_one * (after - before)
            if segment > 0:
                before = got[q, core, segment - 1, g, :, columns]
                value = value + c_two * before
                side = side - s_two * before
            if segment < 3:
                after = got[q, core, segment + 1, g, :, columns]
                value = value + c_two * after
                side = side + s_two * after
            return value + flip * turned_rows(side)

        for upper in range(2):
            for side in range(2):
                columns = slice(side * HALF, (side + 1) * HALF)
                values = []
                for g in range(GROUPS):
                    first, second = (block(2 * upper + i, g, columns) for i in range(2))
                    real = jnp.where(upper_rows, first, turned_rows(second))
                    imag = jnp.where(upper_rows, turned_rows(first), second)
                    cosine, sine = one[0, q, g, :, columns], one[1, q, g, :, columns]
                    values.append((real * cosine - imag * sine, real * sine + imag * cosine))
                values = sixteen(values, -1)
                for g in range(GROUPS):
                    real, imag = values[g]
                    cosine, sine = twiddle[0, g : g + 1, columns], twiddle[1, g : g + 1, columns]
                    values[g] = (real * cosine + imag * sine, imag * cosine - real * sine)
                for g in range(0, GROUPS, 2):
                    spot = slice(upper * HALF + g * 8, upper * HALF + g * 8 + 16)
                    for part in range(2):
                        both = jnp.concatenate([values[g][part], values[g + 1][part]], axis=0)
                        lanes = slice(part * WIDTH + side * HALF, part * WIDTH + (side + 1) * HALF)
                        left[0, spot, lanes], left[1, spot, lanes] = split(both)
        for upper in range(2):
            area = slice(upper * HALF, (upper + 1) * HALF)
            mixed[area, :] = (
                dot(left[0, area, :], dense[0, 0])
                + dot(left[0, area, :], dense[0, 1])
                + dot(left[1, area, :], dense[0, 0])
            )
        for upper in range(2):
            for g in range(0, GROUPS, 2):
                spot = slice(upper * HALF + g * 8, upper * HALF + g * 8 + 16)
                real, imag = mixed[spot, :WIDTH], mixed[spot, WIDTH:]
                cosine = jnp.concatenate([two[0, q, g], two[0, q, g + 1]], axis=0)
                sine = jnp.concatenate([two[1, q, g], two[1, q, g + 1]], axis=0)
                left[0, spot, :WIDTH], left[1, spot, :WIDTH] = split(real * cosine - imag * sine)
                left[0, spot, WIDTH:], left[1, spot, WIDTH:] = split(real * sine + imag * cosine)
        for upper in range(2):
            area = slice(upper * HALF, (upper + 1) * HALF)
            mixed[area, :] = (
                dot(left[0, area, :], dense[1, 0])
                + dot(left[0, area, :], dense[1, 1])
                + dot(left[1, area, :], dense[1, 0])
            )
        for upper in range(2):
            for side in range(2):
                columns = slice(side * HALF, (side + 1) * HALF)
                values = []
                for g in range(GROUPS):
                    spot = slice(upper * HALF + g * 8, upper * HALF + g * 8 + 8)
                    real = mixed[spot, side * HALF : (side + 1) * HALF]
                    imag = mixed[spot, WIDTH + side * HALF : WIDTH + (side + 1) * HALF]
                    cosine, sine = twiddle[0, g : g + 1, columns], twiddle[1, g : g + 1, columns]
                    values.append((real * cosine - imag * sine, real * sine + imag * cosine))
                values = sixteen(values, 1)
                for g in range(GROUPS):
                    real, imag = values[g]
                    cosine, sine = three[0, q, g, :, columns], three[1, q, g, :, columns]
                    real, imag = real * cosine - imag * sine, real * sine + imag * cosine
                    first = 2 * upper * GROUPS + g
                    back[q, first, :, columns] = jnp.where(upper_rows, real, turned_rows(imag))
                    back[q, first + GROUPS, :, columns] = jnp.where(
                        upper_rows, turned_rows(real), imag
                    )
        for dz, dx, dy, dc in HOMEWARD:
            target = place(zs[dz], near[dx], ys[dy], cores[dc])
            piece = zs[dz] * GROUPS + target[1]

            def send():
                pltpu.make_async_remote_copy(
                    src_ref=back.at[q, piece],
                    dst_ref=home.at[q, chip],
                    send_sem=back_send.at[q],
                    recv_sem=back_recv.at[q],
                    device_id=target,
                    device_id_type=MESH,
                ).start()

            def keep():
                pltpu.make_async_copy(
                    back.at[q, piece], home.at[q, chip], back_recv.at[q]
                ).start()

            if (dz, dx, dy, dc) == (0, 0, 0, 0):
                pl.when(jnp.logical_not(same))(send)
                pl.when(same)(keep)
            else:
                send()
        return carry

    arrive(0)
    loads[6].wait()
    lax.fori_loop(0, CLASSES, range_work, 0)

    def drain(buffer, semaphore, q):
        @pl.when(same)
        def _():
            lot = buffer.at[q, pl.ds(0, CHIPS - 1)]
            pltpu.make_async_copy(lot, lot, semaphore.at[q]).wait()

        @pl.when(jnp.logical_not(same))
        def _():
            lot = buffer.at[q]
            pltpu.make_async_copy(lot, lot, semaphore.at[q]).wait()

    def drain_forward(q, carry):
        swap(q).wait_send()
        drain(made, made_send, q)
        return carry

    lax.fori_loop(0, CLASSES, drain_forward, 0)

    loads[7].wait()

    def focused(q):
        lot = home.at[q]
        pltpu.make_async_copy(lot, lot, back_recv.at[q]).wait()
        high, low = split(home[q].reshape(CHIPS * ROWS, WIDTH))
        return dot(inverse[q, 0], high) + dot(inverse[q, 1], high) + dot(inverse[q, 0], low)

    total[...] = focused(0)

    def focus(q, carry):
        total[...] += focused(q)
        drain(back, back_send, q - 1)
        return carry

    lax.fori_loop(1, CLASSES - 1, focus, 0)
    drain(back, back_send, CLASSES - 2)
    result = total[...] + focused(CLASSES - 1)
    out[0] = result[:SEG, :]
    out[1] = result[SEG:, :]
    drain(back, back_send, CLASSES - 1)


def per_device(tables, echo, range_row, aperture, centroid_table, rate_table):
    hbm = pl.BlockSpec(memory_space=pltpu.HBM)
    semaphore = pltpu.SemaphoreType.DMA
    return pl.pallas_call(
        kernel,
        out_shape=pltpu.VMEM((2, SEG, WIDTH), F32),
        in_specs=[hbm] * 9,
        out_specs=pl.BlockSpec(memory_space=pltpu.VMEM),
        scratch_shapes=[
            pltpu.VMEM((2, SEG, WIDTH), F32),
            pltpu.VMEM((2, 2 * SEG, WIDTH), BF16),
            pltpu.VMEM((TOTAL,), jnp.int32),
            pltpu.VMEM((TOTAL,), jnp.int32),
            pltpu.SMEM((64,), jnp.int32),
            pltpu.SMEM((64,), F32),
            pltpu.VMEM((CLASSES, 2, 2 * SEG, 2 * SEG), BF16),
            pltpu.VMEM((CLASSES, 2, 2 * SEG, 2 * SEG), BF16),
            pltpu.VMEM((2, 2, 2 * WIDTH, 2 * WIDTH), BF16),
            pltpu.VMEM((2, GROUPS, WIDTH), F32),
            pltpu.VMEM((CLASSES, CHIPS, ROWS, WIDTH), F32),
            pltpu.VMEM((CLASSES, 2, PAIRS, GROUPS, ROWS, WIDTH), F32),
            pltpu.VMEM((CLASSES, CHIPS, ROWS, WIDTH), F32),
            pltpu.VMEM((CLASSES, CHIPS, ROWS, WIDTH), F32),
            pltpu.VMEM((2, CLASSES, GROUPS, ROWS, WIDTH), F32),
            pltpu.VMEM((2, CLASSES, GROUPS, ROWS, WIDTH), F32),
            pltpu.VMEM((2, CLASSES, GROUPS, ROWS, WIDTH), F32),
            pltpu.VMEM((GROUPS, WIDTH), jnp.int32),
            pltpu.VMEM((GROUPS, WIDTH), F32),
            pltpu.VMEM((2, 2 * HALF, 2 * WIDTH), BF16),
            pltpu.VMEM((2 * HALF, 2 * WIDTH), F32),
            pltpu.VMEM((2 * SEG, WIDTH), F32),
            semaphore((8,)),
            semaphore((CLASSES,)),
            semaphore((CLASSES,)),
            semaphore((CLASSES,)),
            semaphore((CLASSES,)),
            semaphore((CLASSES,)),
            semaphore((CLASSES,)),
            semaphore((CLASSES,)),
        ],
        compiler_params=pltpu.CompilerParams(
            collective_id=0, has_side_effects=True, vmem_limit_bytes=52 * 1024 * 1024
        ),
    )(
        *(
            pltpu.with_memory_space_constraint(operand, pltpu.HBM)
            for operand in (echo, range_row, aperture, centroid_table, rate_table, *tables)
        )
    )


def solution(mesh):
    forward, inverse = azimuth_tables()
    dense, twiddle = range_tables()
    tables = tuple(jnp.asarray(table) for table in (forward, inverse, dense, twiddle))
    in_specs = (P(None, "az", "rg"), P(), P(), P(), P())
    out_specs = P(None, "az", "rg")
    return jax.shard_map(
        partial(per_device, tables),
        mesh=mesh,
        in_specs=in_specs,
        out_specs=out_specs,
        check_vma=False,
    )
```

```python
from functools import partial
import math

import jax
import jax.numpy as jnp
import numpy as np
from jax import lax
from jax.experimental import pallas as pl
from jax.experimental.pallas import tpu as pltpu
from jax.sharding import PartitionSpec as P
import ml_dtypes

F32 = jnp.float32
BF16 = jnp.bfloat16
MESH = pl.DeviceIdType.MESH

SEG = 256
CLASSES = 5
LENGTH = SEG * CLASSES
GROUPS = 16
WIDTH = 256
TOTAL = GROUPS * WIDTH
CHIPS = 64
LINES = SEG // CHIPS
ROWS = 2 * LINES
PAIRS = 4
HALF = 128


def links_of(step):
    load = np.zeros(6)
    for axis, hops in enumerate(step[:3]):
        load[2 * axis] += hops in (1, 2)
        load[2 * axis + 1] += hops in (2, 3)
    return load


def hops(step):
    return sum(min(count, 4 - count) for count in step[:3])


def spread(steps):
    load, remaining, ordered = np.zeros(6), list(steps), []
    while remaining:
        levels = [
            (np.ptp(load + links_of(step)), -links_of(step).sum(), step) for step in remaining
        ]
        chosen = min(levels)[2]
        ordered.append(chosen)
        remaining.remove(chosen)
        load = load + links_of(chosen)
    return ordered


RING = range(4)
OUTWARD = spread([(dz, dx, dy) for dz in RING for dx in RING for dy in RING])
HOMEWARD = spread(
    [(dz, dx, dy, dc) for dz in RING for dx in (0, 2) for dy in RING for dc in (0, 1)]
)


def pair_split(values):
    high = values.astype(ml_dtypes.bfloat16)
    low = (values - high.astype(np.float64)).astype(ml_dtypes.bfloat16)
    return np.stack([high, low])


def azimuth_tables():
    pulse = np.arange(SEG)
    bins = np.arange(SEG)[None, :] * CLASSES + np.arange(CLASSES)[:, None]
    turns = ((2 * SEG + pulse)[None, :, None] * bins[:, None, :]) % LENGTH
    angle = turns * (2.0 * np.pi / LENGTH)
    scale = 1.0 / math.sqrt(LENGTH)
    cosine, sine = np.cos(angle) * scale, np.sin(angle) * scale
    real = np.stack([cosine, -sine]).reshape(2, CLASSES, SEG, CHIPS, LINES)
    imag = np.stack([sine, cosine]).reshape(2, CLASSES, SEG, CHIPS, LINES)
    inverse = np.stack([real, imag]).transpose(2, 0, 3, 4, 1, 5)
    inverse = inverse.reshape(CLASSES, 2 * SEG, CHIPS * ROWS)
    forward = inverse.transpose(0, 2, 1)
    return pair_split(forward).transpose(1, 0, 2, 3), pair_split(inverse).transpose(1, 0, 2, 3)


def range_tables():
    index = np.arange(WIDTH)
    angle = (index[:, None] * index[None, :] % WIDTH) * (2.0 * np.pi / WIDTH)
    cosine, sine = np.cos(angle), np.sin(angle)
    forward = np.block([[cosine, -sine], [sine, cosine]])
    inverse = np.block([[cosine, sine], [-sine, cosine]])
    fine = np.arange(GROUPS)[:, None] * index[None, :] * (2.0 * np.pi / TOTAL)
    twiddle = np.stack([np.cos(fine), np.sin(fine)]).astype(np.float32)
    return np.stack([pair_split(forward), pair_split(inverse)]), twiddle


WEIGHTS = [
    [
        (math.cos(2.0 * math.pi * q * step / CLASSES), math.sin(2.0 * math.pi * q * step / CLASSES))
        for step in (1, 2)
    ]
    for q in range(CLASSES)
]


def weight(q, step, part):
    value = jnp.float32(WEIGHTS[0][step - 1][part])
    for other in range(1, CLASSES):
        value = jnp.where(q == other, jnp.float32(WEIGHTS[other][step - 1][part]), value)
    return value


def split(value):
    high = value.astype(BF16)
    return high, (value - high.astype(F32)).astype(BF16)


def fitted(function, powers):
    nodes = np.cos((np.arange(400) + 0.5) * np.pi / 400) * 0.5
    nodes = nodes[nodes > 0]
    basis = np.stack([(2 * nodes) ** p for p in powers], axis=1)
    solved = np.linalg.lstsq(basis, function(2.0 * np.pi * nodes), rcond=None)[0]
    return [float(value * 2.0**p) for value, p in zip(solved, powers)]


SINE = fitted(np.sin, [1, 3, 5, 7, 9, 11])
COSINE = fitted(np.cos, [0, 2, 4, 6, 8, 10, 12])


def turn(cycles):
    left = cycles - jnp.floor(cycles + 0.5)
    square = left * left
    sine, cosine = SINE[-1], COSINE[-1]
    for value in SINE[-2::-1]:
        sine = sine * square + value
    for value in COSINE[-2::-1]:
        cosine = cosine * square + value
    return cosine, sine * left


def times_turn(value, quarter):
    real, imag = value
    quarter %= 4
    if quarter == 0:
        return real, imag
    if quarter == 1:
        return -imag, real
    if quarter == 2:
        return -real, -imag
    return imag, -real


def four(values, sign):
    a, b, c, d = values
    ac = (a[0] + c[0], a[1] + c[1])
    am = (a[0] - c[0], a[1] - c[1])
    bd = (b[0] + d[0], b[1] + d[1])
    bm = times_turn((b[0] - d[0], b[1] - d[1]), sign)
    return [
        (ac[0] + bd[0], ac[1] + bd[1]),
        (am[0] + bm[0], am[1] + bm[1]),
        (ac[0] - bd[0], ac[1] - bd[1]),
        (am[0] - bm[0], am[1] - bm[1]),
    ]


def sixteen(values, sign):
    inner = [four(values[low::4], sign) for low in range(4)]
    result = [None] * 16
    for first in range(4):
        column = []
        for low in range(4):
            real, imag = inner[low][first]
            step = low * first
            if step % 4 == 0:
                column.append(times_turn((real, imag), sign * (step // 4)))
            else:
                angle = sign * 2.0 * math.pi * step / 16
                cosine, sine = math.cos(angle), math.sin(angle)
                if step % 2 == 0:
                    root = math.sqrt(0.5)
                    up = 1.0 if cosine > 0 else -1.0
                    side = 1.0 if sine > 0 else -1.0
                    if up == side:
                        column.append(((real - imag) * (up * root), (real + imag) * (up * root)))
                    else:
                        column.append(((real + imag) * (up * root), (imag - real) * (up * root)))
                else:
                    column.append((real * cosine - imag * sine, real * sine + imag * cosine))
        outer = four(column, sign)
        for second in range(4):
            result[first + 4 * second] = outer[second]
    return result


def dot(left, right):
    return jnp.dot(left, right, preferred_element_type=F32)


def kernel(
    echo_hbm,
    range_row_hbm,
    aperture_hbm,
    centroid_hbm,
    rate_hbm,
    forward_hbm,
    inverse_hbm,
    dense_hbm,
    twiddle_hbm,
    total,
    last,
    last_table,
    echo,
    pulses,
    range_row,
    aperture,
    centroid_table,
    rate_table,
    forward,
    inverse,
    dense,
    twiddle,
    made,
    got,
    back,
    home,
    one,
    two,
    three,
    centroid,
    rate,
    left,
    mixed,
    load_sem,
    forward_sem,
    made_send,
    made_recv,
    swap_send,
    swap_recv,
    back_send,
    back_recv,
):
    az = lax.axis_index("az")
    me = lax.axis_index("rg")
    z, x_low = az // 2, az % 2
    x, y, core = (me // 8) * 2 + x_low, (me // 2) % 4, me % 2
    chip = z * 16 + x * 4 + y
    same = x_low == core
    apart = jnp.where(same, 0, 1)
    zs = [(z + step) % 4 for step in RING]
    xs = [(x + step) % 4 for step in RING]
    ys = [(y + step) % 4 for step in RING]
    cores = [core, 1 - core]
    near = {step: (x + apart + step) % 4 for step in (0, 2)}

    def place(z_at, x_at, y_at, core_at):
        return (z_at * 2 + x_at % 2, (x_at // 2) * 8 + y_at * 2 + core_at)

    loads = [
        pltpu.make_async_copy(source, target, load_sem.at[i])
        for i, (source, target) in enumerate(
            (
                (echo_hbm, echo),
                (range_row_hbm, range_row),
                (aperture_hbm, aperture),
                (centroid_hbm, centroid_table),
                (rate_hbm, rate_table),
                (twiddle_hbm, twiddle),
                (dense_hbm, dense),
                (inverse_hbm, inverse),
                (inverse_hbm.at[CLASSES - 1], last_table),
            )
        )
    ]
    forward_loads = [
        pltpu.make_async_copy(forward_hbm.at[q], forward.at[q], forward_sem.at[q])
        for q in range(CLASSES)
    ]
    loads[0].start()
    forward_loads[0].start()

    barrier = pltpu.get_barrier_semaphore()

    def greet(target):
        pl.semaphore_signal(barrier, inc=1, device_id=target, device_id_type=MESH)

    for dz, dx, dy, dc in sorted(HOMEWARD, key=hops, reverse=True):
        target = place(zs[dz], near[dx], ys[dy], cores[dc])
        if (dz, dx, dy, dc) == (0, 0, 0, 0):
            pl.when(jnp.logical_not(same))(partial(greet, target))
        else:
            greet(target)

    for copy in forward_loads[1:] + loads[1:]:
        copy.start()
    loads[0].wait()
    for part in range(2):
        rows = slice(part * SEG, (part + 1) * SEG)
        pulses[0, rows, :], pulses[1, rows, :] = split(echo[part])

    def azimuth(q, carry):
        pltpu.make_async_copy(forward_hbm.at[q], forward.at[q], forward_sem.at[q]).wait()
        spectrum = (
            dot(forward[q, 0], pulses[0])
            + dot(forward[q, 1], pulses[0])
            + dot(forward[q, 0], pulses[1])
        )
        made[q] = spectrum.reshape(CHIPS, ROWS, WIDTH)

        @pl.when(q == 0)
        def _():
            pl.semaphore_wait(barrier, CHIPS - jnp.where(same, 1, 0))

        for dz, dx, dy in OUTWARD:
            target = place(zs[dz], xs[dx], ys[dy], x_low)
            owner = zs[dz] * 16 + xs[dx] * 4 + ys[dy]

            def send():
                pltpu.make_async_remote_copy(
                    src_ref=made.at[q, owner],
                    dst_ref=got.at[q, x_low, z, me],
                    send_sem=made_send.at[q],
                    recv_sem=made_recv.at[q],
                    device_id=target,
                    device_id_type=MESH,
                ).start()

            def keep():
                pltpu.make_async_copy(
                    made.at[q, owner], got.at[q, x_low, z, me], made_recv.at[q]
                ).start()

            if (dz, dx, dy) == (0, 0, 0):
                pl.when(jnp.logical_not(same))(send)
                pl.when(same)(keep)
            else:
                send()
        return carry

    lax.fori_loop(0, CLASSES, azimuth, 0)

    for copy in loads[1:6]:
        copy.wait()
    for g in range(GROUPS):
        here = pl.ds(g * WIDTH, WIDTH)
        centroid[g : g + 1, :] = range_row[here].reshape(1, WIDTH)
    rows = centroid[...]
    centers = jnp.zeros((GROUPS, WIDTH), jnp.int32)
    rates = jnp.zeros((GROUPS, WIDTH), F32)
    for entry in range(64):
        hit = rows == entry
        centers = jnp.where(hit, centroid_table[entry], centers)
        rates = jnp.where(hit, rate_table[entry], rates)
    centroid[...] = centers
    rate[...] = rates

    lane = lax.broadcasted_iota(jnp.int32, (ROWS, WIDTH), 1)
    line = lax.broadcasted_iota(jnp.int32, (ROWS, WIDTH), 0) % LINES

    def doppler(bins):
        fraction = bins.astype(F32) * (1.0 / LENGTH)
        squared = jnp.maximum(1.0 - 1.5 * fraction * fraction, 0.1)
        migration = jnp.sqrt(squared)
        return squared, migration, 1.0 / migration - 1.0

    def phases(q, carry):
        bins = CLASSES * (LINES * chip + line) + q
        unused, low_migration, low_scaling = doppler(bins)
        unused, high_migration, high_scaling = doppler(bins - LENGTH)
        squared, unused, zero_scaling = doppler(jnp.where(bins < LENGTH // 2, bins, bins - LENGTH))
        square_gain = squared * (150.0 / (TOTAL * TOTAL))
        linear_gain = zero_scaling * 0.05

        def each_group(g, inner):
            here = pl.ds(g, 1)
            center = centroid[here, :]
            time = (g * WIDTH + lane).astype(F32) * (1.0 / TOTAL) + (0.5 / TOTAL - 0.5)
            low = bins <= center + (LENGTH // 2 - 1)
            migration = jnp.where(low, low_migration, high_migration)
            scaling = jnp.where(low, low_scaling, high_scaling)
            offset = jnp.where(low, bins, bins - LENGTH) - center
            lagged = time - 0.2 * scaling
            cosine, sine = turn(-150.0 * scaling * lagged * lagged)
            one[0, q, g] = cosine
            one[1, q, g] = sine
            cosine, sine = turn(
                rate[here, :] * (migration - 1.0) + 150.0 * scaling * (1.0 + scaling) * time * time
            )
            wide = aperture[pl.ds(pl.multiple_of(g * WIDTH, WIDTH), WIDTH)].reshape(1, WIDTH)
            keep = jnp.where(2 * jnp.abs(offset) < wide, 1.0 / TOTAL, 0.0)
            three[0, q, g] = cosine * keep
            three[1, q, g] = sine * keep
            frequency = (GROUPS * lane + g - jnp.where(lane >= HALF, TOTAL, 0)).astype(F32)
            cosine, sine = turn((square_gain * frequency + linear_gain) * frequency)
            two[0, q, g] = cosine
            two[1, q, g] = sine
            return inner

        return lax.fori_loop(0, GROUPS, each_group, carry)

    lax.fori_loop(0, CLASSES, phases, 0)

    sibling = (az, me + 1 - 2 * core)

    def swap(q):
        return pltpu.make_async_remote_copy(
            src_ref=got.at[q, core],
            dst_ref=got.at[q, core],
            send_sem=swap_send.at[q],
            recv_sem=swap_recv.at[q],
            device_id=sibling,
            device_id_type=MESH,
        )

    def arrive(q):
        lot = got.at[q, core]
        pltpu.make_async_copy(lot, lot, made_recv.at[q]).wait()
        swap(q).start()

    upper_rows = lax.broadcasted_iota(jnp.int32, (ROWS, HALF), 0) < LINES
    flip = jnp.where(upper_rows, 1.0, -1.0).astype(F32)
    first_before = core.astype(F32)
    last_after = 1.0 - first_before

    def turned_rows(value):
        return pltpu.roll(value, LINES, 0)

    def range_work(q, carry):
        @pl.when(q < CLASSES - 1)
        def _():
            arrive(q + 1)

        swap(q).wait_recv()
        c_one, s_one = weight(q, 1, 0), weight(q, 1, 1)
        c_two, s_two = weight(q, 2, 0), weight(q, 2, 1)

        def block(segment, g, columns):
            value = got[q, core, segment, g, :, columns]
            before = got[q, 1 - core, jnp.maximum(segment - 1 + core, 0), g, :, columns]
            after = got[q, 1 - core, jnp.minimum(segment + core, 3), g, :, columns]
            if segment == 0:
                before = before * first_before
            if segment == 3:
                after = after * last_after
            value = value + c_one * (after + before)
            side = s_one * (after - before)
            if segment > 0:
                before = got[q, core, segment - 1, g, :, columns]
                value = value + c_two * before
                side = side - s_two * before
            if segment < 3:
                after = got[q, core, segment + 1, g, :, columns]
                value = value + c_two * after
                side = side + s_two * after
            return value + flip * turned_rows(side)

        for upper in range(2):
            for side in range(2):
                columns = slice(side * HALF, (side + 1) * HALF)
                values = []
                for g in range(GROUPS):
                    first, second = (block(2 * upper + i, g, columns) for i in range(2))
                    real = jnp.where(upper_rows, first, turned_rows(second))
                    imag = jnp.where(upper_rows, turned_rows(first), second)
                    cosine, sine = one[0, q, g, :, columns], one[1, q, g, :, columns]
                    values.append((real * cosine - imag * sine, real * sine + imag * cosine))
                values = sixteen(values, -1)
                for g in range(GROUPS):
                    real, imag = values[g]
                    cosine, sine = twiddle[0, g : g + 1, columns], twiddle[1, g : g + 1, columns]
                    values[g] = (real * cosine + imag * sine, imag * cosine - real * sine)
                for g in range(0, GROUPS, 2):
                    spot = slice(upper * HALF + g * 8, upper * HALF + g * 8 + 16)
                    for part in range(2):
                        both = jnp.concatenate([values[g][part], values[g + 1][part]], axis=0)
                        lanes = slice(part * WIDTH + side * HALF, part * WIDTH + (side + 1) * HALF)
                        left[0, spot, lanes], left[1, spot, lanes] = split(both)
        for upper in range(2):
            area = slice(upper * HALF, (upper + 1) * HALF)
            mixed[area, :] = (
                dot(left[0, area, :], dense[0, 0])
                + dot(left[0, area, :], dense[0, 1])
                + dot(left[1, area, :], dense[0, 0])
            )
        for upper in range(2):
            for g in range(0, GROUPS, 2):
                spot = slice(upper * HALF + g * 8, upper * HALF + g * 8 + 16)
                real, imag = mixed[spot, :WIDTH], mixed[spot, WIDTH:]
                cosine = jnp.concatenate([two[0, q, g], two[0, q, g + 1]], axis=0)
                sine = jnp.concatenate([two[1, q, g], two[1, q, g + 1]], axis=0)
                left[0, spot, :WIDTH], left[1, spot, :WIDTH] = split(real * cosine - imag * sine)
                left[0, spot, WIDTH:], left[1, spot, WIDTH:] = split(real * sine + imag * cosine)
        for upper in range(2):
            area = slice(upper * HALF, (upper + 1) * HALF)
            mixed[area, :] = (
                dot(left[0, area, :], dense[1, 0])
                + dot(left[0, area, :], dense[1, 1])
                + dot(left[1, area, :], dense[1, 0])
            )
        for upper in range(2):
            for side in range(2):
                columns = slice(side * HALF, (side + 1) * HALF)
                values = []
                for g in range(GROUPS):
                    spot = slice(upper * HALF + g * 8, upper * HALF + g * 8 + 8)
                    real = mixed[spot, side * HALF : (side + 1) * HALF]
                    imag = mixed[spot, WIDTH + side * HALF : WIDTH + (side + 1) * HALF]
                    cosine, sine = twiddle[0, g : g + 1, columns], twiddle[1, g : g + 1, columns]
                    values.append((real * cosine - imag * sine, real * sine + imag * cosine))
                values = sixteen(values, 1)
                for g in range(GROUPS):
                    real, imag = values[g]
                    cosine, sine = three[0, q, g, :, columns], three[1, q, g, :, columns]
                    real, imag = real * cosine - imag * sine, real * sine + imag * cosine
                    first = 2 * upper * GROUPS + g
                    back[q, first, :, columns] = jnp.where(upper_rows, real, turned_rows(imag))
                    back[q, first + GROUPS, :, columns] = jnp.where(
                        upper_rows, turned_rows(real), imag
                    )
        for dz, dx, dy, dc in HOMEWARD:
            target = place(zs[dz], near[dx], ys[dy], cores[dc])
            piece = zs[dz] * GROUPS + target[1]

            def send():
                pltpu.make_async_remote_copy(
                    src_ref=back.at[q, piece],
                    dst_ref=home.at[q, chip],
                    send_sem=back_send.at[q],
                    recv_sem=back_recv.at[q],
                    device_id=target,
                    device_id_type=MESH,
                ).start()

            def keep():
                pltpu.make_async_copy(
                    back.at[q, piece], home.at[q, chip], back_recv.at[q]
                ).start()

            if (dz, dx, dy, dc) == (0, 0, 0, 0):
                pl.when(jnp.logical_not(same))(send)
                pl.when(same)(keep)
            else:
                send()
        return carry

    arrive(0)
    loads[6].wait()
    lax.fori_loop(0, CLASSES, range_work, 0)

    def drain(buffer, semaphore, q):
        @pl.when(same)
        def _():
            lot = buffer.at[q, pl.ds(0, CHIPS - 1)]
            pltpu.make_async_copy(lot, lot, semaphore.at[q]).wait()

        @pl.when(jnp.logical_not(same))
        def _():
            lot = buffer.at[q]
            pltpu.make_async_copy(lot, lot, semaphore.at[q]).wait()

    def drain_forward(q, carry):
        swap(q).wait_send()
        drain(made, made_send, q)
        return carry

    lax.fori_loop(0, CLASSES, drain_forward, 0)

    loads[7].wait()

    loads[8].wait()

    def received(q):
        lot = home.at[q]
        pltpu.make_async_copy(lot, lot, back_recv.at[q]).wait()
        return split(home[q].reshape(CHIPS * ROWS, WIDTH))

    def focused(q):
        high, low = received(q)
        return dot(inverse[q, 0], high) + dot(inverse[q, 1], high) + dot(inverse[q, 0], low)

    total[...] = focused(0)

    def focus(q, carry):
        total[...] += focused(q)
        drain(back, back_send, q - 1)
        return carry

    lax.fori_loop(1, CLASSES - 1, focus, 0)
    drain(back, back_send, CLASSES - 2)
    last[0], last[1] = received(CLASSES - 1)
    drain(back, back_send, CLASSES - 1)


def finish(total, last, table, out, result, sent):
    copies = []
    for block in range(4):
        rows = slice(block * HALF, (block + 1) * HALF)
        result[block] = total[rows, :] + (
            dot(table[0, rows, :], last[0])
            + dot(table[1, rows, :], last[0])
            + dot(table[0, rows, :], last[1])
        )
        place = out.at[block // 2, pl.ds(block % 2 * HALF, HALF), :]
        copy = pltpu.make_async_copy(result.at[block], place, sent.at[block])
        copy.start()
        copies.append(copy)
    for copy in copies:
        copy.wait()


def per_device(tables, echo, range_row, aperture, centroid_table, rate_table):
    hbm = pl.BlockSpec(memory_space=pltpu.HBM)
    semaphore = pltpu.SemaphoreType.DMA
    parts = pl.pallas_call(
        kernel,
        out_shape=[
            pltpu.VMEM((2 * SEG, WIDTH), F32),
            pltpu.VMEM((2, CHIPS * ROWS, WIDTH), BF16),
            pltpu.VMEM((2, 2 * SEG, CHIPS * ROWS), BF16),
        ],
        in_specs=[hbm] * 9,
        out_specs=[pl.BlockSpec(memory_space=pltpu.VMEM)] * 3,
        scratch_shapes=[
            pltpu.VMEM((2, SEG, WIDTH), F32),
            pltpu.VMEM((2, 2 * SEG, WIDTH), BF16),
            pltpu.VMEM((TOTAL,), jnp.int32),
            pltpu.VMEM((TOTAL,), jnp.int32),
            pltpu.SMEM((64,), jnp.int32),
            pltpu.SMEM((64,), F32),
            pltpu.VMEM((CLASSES, 2, 2 * SEG, 2 * SEG), BF16),
            pltpu.VMEM((CLASSES, 2, 2 * SEG, 2 * SEG), BF16),
            pltpu.VMEM((2, 2, 2 * WIDTH, 2 * WIDTH), BF16),
            pltpu.VMEM((2, GROUPS, WIDTH), F32),
            pltpu.VMEM((CLASSES, CHIPS, ROWS, WIDTH), F32),
            pltpu.VMEM((CLASSES, 2, PAIRS, GROUPS, ROWS, WIDTH), F32),
            pltpu.VMEM((CLASSES, CHIPS, ROWS, WIDTH), F32),
            pltpu.VMEM((CLASSES, CHIPS, ROWS, WIDTH), F32),
            pltpu.VMEM((2, CLASSES, GROUPS, ROWS, WIDTH), F32),
            pltpu.VMEM((2, CLASSES, GROUPS, ROWS, WIDTH), F32),
            pltpu.VMEM((2, CLASSES, GROUPS, ROWS, WIDTH), F32),
            pltpu.VMEM((GROUPS, WIDTH), jnp.int32),
            pltpu.VMEM((GROUPS, WIDTH), F32),
            pltpu.VMEM((2, 2 * HALF, 2 * WIDTH), BF16),
            pltpu.VMEM((2 * HALF, 2 * WIDTH), F32),
            semaphore((9,)),
            semaphore((CLASSES,)),
            semaphore((CLASSES,)),
            semaphore((CLASSES,)),
            semaphore((CLASSES,)),
            semaphore((CLASSES,)),
            semaphore((CLASSES,)),
            semaphore((CLASSES,)),
        ],
        compiler_params=pltpu.CompilerParams(
            collective_id=0, has_side_effects=True, vmem_limit_bytes=52 * 1024 * 1024
        ),
    )(
        *(
            pltpu.with_memory_space_constraint(operand, pltpu.HBM)
            for operand in (echo, range_row, aperture, centroid_table, rate_table, *tables)
        )
    )
    return pl.pallas_call(
        finish,
        out_shape=jax.ShapeDtypeStruct((2, SEG, WIDTH), F32),
        in_specs=[pl.BlockSpec(memory_space=pltpu.VMEM)] * 3,
        out_specs=pl.BlockSpec(memory_space=pl.ANY),
        scratch_shapes=[pltpu.VMEM((4, HALF, WIDTH), F32), semaphore((4,))],
        compiler_params=pltpu.CompilerParams(vmem_limit_bytes=16 * 1024 * 1024),
    )(*(pltpu.with_memory_space_constraint(part, pltpu.VMEM) for part in parts))


def solution(mesh):
    forward, inverse = azimuth_tables()
    dense, twiddle = range_tables()
    tables = tuple(jnp.asarray(table) for table in (forward, inverse, dense, twiddle))
    in_specs = (P(None, "az", "rg"), P(), P(), P(), P())
    out_specs = P(None, "az", "rg")
    return jax.shard_map(
        partial(per_device, tables),
        mesh=mesh,
        in_specs=in_specs,
        out_specs=out_specs,
        check_vma=False,
    )
```

```python
from functools import partial
import math

import jax
import jax.numpy as jnp
import numpy as np
from jax import lax
from jax.experimental import pallas as pl
from jax.experimental.pallas import tpu as pltpu
from jax.sharding import PartitionSpec as P
import ml_dtypes

F32 = jnp.float32
BF16 = jnp.bfloat16
MESH = pl.DeviceIdType.MESH

SEG = 256
CLASSES = 5
LENGTH = SEG * CLASSES
GROUPS = 16
WIDTH = 256
TOTAL = GROUPS * WIDTH
CHIPS = 64
LINES = SEG // CHIPS
ROWS = 2 * LINES
PAIRS = 4
HALF = 128


def links_of(step):
    load = np.zeros(6)
    for axis, hops in enumerate(step[:3]):
        load[2 * axis] += hops in (1, 2)
        load[2 * axis + 1] += hops in (2, 3)
    return load


def hops(step):
    return sum(min(count, 4 - count) for count in step[:3])


def spread(steps):
    load, remaining, ordered = np.zeros(6), list(steps), []
    while remaining:
        levels = [
            (np.ptp(load + links_of(step)), -links_of(step).sum(), step) for step in remaining
        ]
        chosen = min(levels)[2]
        ordered.append(chosen)
        remaining.remove(chosen)
        load = load + links_of(chosen)
    return ordered


RING = range(4)
OUTWARD = spread([(dz, dx, dy) for dz in RING for dx in RING for dy in RING])
HOMEWARD = spread(
    [(dz, dx, dy, dc) for dz in RING for dx in (0, 2) for dy in RING for dc in (0, 1)]
)


def pair_split(values):
    high = values.astype(ml_dtypes.bfloat16)
    low = (values - high.astype(np.float64)).astype(ml_dtypes.bfloat16)
    return np.stack([high, low])


def azimuth_tables():
    pulse = np.arange(SEG)
    bins = np.arange(SEG)[None, :] * CLASSES + np.arange(CLASSES)[:, None]
    turns = ((2 * SEG + pulse)[None, :, None] * bins[:, None, :]) % LENGTH
    angle = turns * (2.0 * np.pi / LENGTH)
    scale = 1.0 / math.sqrt(LENGTH)
    cosine, sine = np.cos(angle) * scale, np.sin(angle) * scale
    real = np.stack([cosine, -sine]).reshape(2, CLASSES, SEG, CHIPS, LINES)
    imag = np.stack([sine, cosine]).reshape(2, CLASSES, SEG, CHIPS, LINES)
    inverse = np.stack([real, imag]).transpose(2, 0, 3, 4, 1, 5)
    inverse = inverse.reshape(CLASSES, 2 * SEG, CHIPS * ROWS)
    forward = inverse.transpose(0, 2, 1)
    return pair_split(forward).transpose(1, 0, 2, 3), pair_split(inverse).transpose(1, 0, 2, 3)


def range_tables():
    index = np.arange(WIDTH)
    angle = (index[:, None] * index[None, :] % WIDTH) * (2.0 * np.pi / WIDTH)
    cosine, sine = np.cos(angle), np.sin(angle)
    forward = np.block([[cosine, -sine], [sine, cosine]])
    inverse = np.block([[cosine, sine], [-sine, cosine]])
    fine = np.arange(GROUPS)[:, None] * index[None, :] * (2.0 * np.pi / TOTAL)
    twiddle = np.stack([np.cos(fine), np.sin(fine)]).astype(np.float32)
    return np.stack([pair_split(forward), pair_split(inverse)]), twiddle


WEIGHTS = [
    [
        (math.cos(2.0 * math.pi * q * step / CLASSES), math.sin(2.0 * math.pi * q * step / CLASSES))
        for step in (1, 2)
    ]
    for q in range(CLASSES)
]


def weight(q, step, part):
    value = jnp.float32(WEIGHTS[0][step - 1][part])
    for other in range(1, CLASSES):
        value = jnp.where(q == other, jnp.float32(WEIGHTS[other][step - 1][part]), value)
    return value


def split(value):
    high = value.astype(BF16)
    return high, (value - high.astype(F32)).astype(BF16)


def fitted(function, powers):
    nodes = np.cos((np.arange(400) + 0.5) * np.pi / 400) * 0.5
    nodes = nodes[nodes > 0]
    basis = np.stack([(2 * nodes) ** p for p in powers], axis=1)
    solved = np.linalg.lstsq(basis, function(2.0 * np.pi * nodes), rcond=None)[0]
    return [float(value * 2.0**p) for value, p in zip(solved, powers)]


SINE = fitted(np.sin, [1, 3, 5, 7, 9, 11])
COSINE = fitted(np.cos, [0, 2, 4, 6, 8, 10, 12])


def turn(cycles):
    left = cycles - jnp.floor(cycles + 0.5)
    square = left * left
    sine, cosine = SINE[-1], COSINE[-1]
    for value in SINE[-2::-1]:
        sine = sine * square + value
    for value in COSINE[-2::-1]:
        cosine = cosine * square + value
    return cosine, sine * left


def times_turn(value, quarter):
    real, imag = value
    quarter %= 4
    if quarter == 0:
        return real, imag
    if quarter == 1:
        return -imag, real
    if quarter == 2:
        return -real, -imag
    return imag, -real


def four(values, sign):
    a, b, c, d = values
    ac = (a[0] + c[0], a[1] + c[1])
    am = (a[0] - c[0], a[1] - c[1])
    bd = (b[0] + d[0], b[1] + d[1])
    bm = times_turn((b[0] - d[0], b[1] - d[1]), sign)
    return [
        (ac[0] + bd[0], ac[1] + bd[1]),
        (am[0] + bm[0], am[1] + bm[1]),
        (ac[0] - bd[0], ac[1] - bd[1]),
        (am[0] - bm[0], am[1] - bm[1]),
    ]


def sixteen(values, sign):
    inner = [four(values[low::4], sign) for low in range(4)]
    result = [None] * 16
    for first in range(4):
        column = []
        for low in range(4):
            real, imag = inner[low][first]
            step = low * first
            if step % 4 == 0:
                column.append(times_turn((real, imag), sign * (step // 4)))
            else:
                angle = sign * 2.0 * math.pi * step / 16
                cosine, sine = math.cos(angle), math.sin(angle)
                if step % 2 == 0:
                    root = math.sqrt(0.5)
                    up = 1.0 if cosine > 0 else -1.0
                    side = 1.0 if sine > 0 else -1.0
                    if up == side:
                        column.append(((real - imag) * (up * root), (real + imag) * (up * root)))
                    else:
                        column.append(((real + imag) * (up * root), (imag - real) * (up * root)))
                else:
                    column.append((real * cosine - imag * sine, real * sine + imag * cosine))
        outer = four(column, sign)
        for second in range(4):
            result[first + 4 * second] = outer[second]
    return result


def dot(left, right):
    return jnp.dot(left, right, preferred_element_type=F32)


def kernel(
    echo_hbm,
    range_row_hbm,
    aperture_hbm,
    centroid_hbm,
    rate_hbm,
    forward_hbm,
    inverse_hbm,
    dense_hbm,
    twiddle_hbm,
    out,
    echo,
    pulses,
    range_row,
    aperture,
    centroid_table,
    rate_table,
    forward,
    inverse,
    dense,
    twiddle,
    made,
    got,
    back,
    home,
    one,
    two,
    three,
    centroid,
    rate,
    left,
    mixed,
    total,
    load_sem,
    forward_sem,
    made_send,
    made_recv,
    swap_send,
    swap_recv,
    back_send,
    back_recv,
):
    az = lax.axis_index("az")
    me = lax.axis_index("rg")
    z, x_low = az // 2, az % 2
    x, y, core = (me // 8) * 2 + x_low, (me // 2) % 4, me % 2
    chip = z * 16 + x * 4 + y
    same = x_low == core
    apart = jnp.where(same, 0, 1)
    zs = [(z + step + 2 * core) % 4 for step in RING]
    own_plane = [jnp.logical_and(same, core == side) for side in range(2)]
    xs = [(x + step) % 4 for step in RING]
    ys = [(y + step) % 4 for step in RING]
    cores = [core, 1 - core]
    near = {step: (x + apart + step) % 4 for step in (0, 2)}

    def place(z_at, x_at, y_at, core_at):
        return (z_at * 2 + x_at % 2, (x_at // 2) * 8 + y_at * 2 + core_at)

    loads = [
        pltpu.make_async_copy(source, target, load_sem.at[i])
        for i, (source, target) in enumerate(
            (
                (echo_hbm, echo),
                (range_row_hbm, range_row),
                (aperture_hbm, aperture),
                (centroid_hbm, centroid_table),
                (rate_hbm, rate_table),
                (twiddle_hbm, twiddle),
                (dense_hbm, dense),
                (inverse_hbm, inverse),
            )
        )
    ]
    forward_loads = [
        pltpu.make_async_copy(forward_hbm.at[q], forward.at[q], forward_sem.at[q])
        for q in range(CLASSES)
    ]
    loads[0].start()
    forward_loads[0].start()

    barrier = pltpu.get_barrier_semaphore()

    def greet(target):
        pl.semaphore_signal(barrier, inc=1, device_id=target, device_id_type=MESH)

    for dz, dx, dy, dc in sorted(HOMEWARD, key=hops, reverse=True):
        target = place(zs[dz], near[dx], ys[dy], cores[dc])
        if (dx, dy, dc) == (0, 0, 0) and dz in (0, 2):
            pl.when(jnp.logical_not(own_plane[dz // 2]))(partial(greet, target))
        else:
            greet(target)

    for copy in forward_loads[1:] + loads[1:]:
        copy.start()
    loads[0].wait()
    for part in range(2):
        rows = slice(part * SEG, (part + 1) * SEG)
        pulses[0, rows, :], pulses[1, rows, :] = split(echo[part])

    def azimuth(q, carry):
        pltpu.make_async_copy(forward_hbm.at[q], forward.at[q], forward_sem.at[q]).wait()
        spectrum = (
            dot(forward[q, 0], pulses[0])
            + dot(forward[q, 1], pulses[0])
            + dot(forward[q, 0], pulses[1])
        )
        made[q] = spectrum.reshape(CHIPS, ROWS, WIDTH)

        @pl.when(q == 0)
        def _():
            pl.semaphore_wait(barrier, CHIPS - jnp.where(same, 1, 0))

        for dz, dx, dy in OUTWARD:
            target = place(zs[dz], xs[dx], ys[dy], x_low)
            owner = zs[dz] * 16 + xs[dx] * 4 + ys[dy]

            def send():
                pltpu.make_async_remote_copy(
                    src_ref=made.at[q, owner],
                    dst_ref=got.at[q, x_low, z, me],
                    send_sem=made_send.at[q],
                    recv_sem=made_recv.at[q],
                    device_id=target,
                    device_id_type=MESH,
                ).start()

            def keep():
                pltpu.make_async_copy(
                    made.at[q, owner], got.at[q, x_low, z, me], made_recv.at[q]
                ).start()

            if (dx, dy) == (0, 0) and dz in (0, 2):
                pl.when(jnp.logical_not(own_plane[dz // 2]))(send)
                pl.when(own_plane[dz // 2])(keep)
            else:
                send()
        return carry

    lax.fori_loop(0, CLASSES, azimuth, 0)

    for copy in loads[1:6]:
        copy.wait()
    for g in range(GROUPS):
        here = pl.ds(g * WIDTH, WIDTH)
        centroid[g : g + 1, :] = range_row[here].reshape(1, WIDTH)
    rows = centroid[...]
    centers = jnp.zeros((GROUPS, WIDTH), jnp.int32)
    rates = jnp.zeros((GROUPS, WIDTH), F32)
    for entry in range(64):
        hit = rows == entry
        centers = jnp.where(hit, centroid_table[entry], centers)
        rates = jnp.where(hit, rate_table[entry], rates)
    centroid[...] = centers
    rate[...] = rates

    lane = lax.broadcasted_iota(jnp.int32, (ROWS, WIDTH), 1)
    line = lax.broadcasted_iota(jnp.int32, (ROWS, WIDTH), 0) % LINES

    def doppler(bins):
        fraction = bins.astype(F32) * (1.0 / LENGTH)
        squared = jnp.maximum(1.0 - 1.5 * fraction * fraction, 0.1)
        migration = jnp.sqrt(squared)
        return squared, migration, 1.0 / migration - 1.0

    def phases(q, carry):
        bins = CLASSES * (LINES * chip + line) + q
        unused, low_migration, low_scaling = doppler(bins)
        unused, high_migration, high_scaling = doppler(bins - LENGTH)
        squared, unused, zero_scaling = doppler(jnp.where(bins < LENGTH // 2, bins, bins - LENGTH))
        square_gain = squared * (150.0 / (TOTAL * TOTAL))
        linear_gain = zero_scaling * 0.05

        def each_group(g, inner):
            here = pl.ds(g, 1)
            center = centroid[here, :]
            time = (g * WIDTH + lane).astype(F32) * (1.0 / TOTAL) + (0.5 / TOTAL - 0.5)
            low = bins <= center + (LENGTH // 2 - 1)
            migration = jnp.where(low, low_migration, high_migration)
            scaling = jnp.where(low, low_scaling, high_scaling)
            offset = jnp.where(low, bins, bins - LENGTH) - center
            lagged = time - 0.2 * scaling
            cosine, sine = turn(-150.0 * scaling * lagged * lagged)
            one[0, q, g] = cosine
            one[1, q, g] = sine
            cosine, sine = turn(
                rate[here, :] * (migration - 1.0) + 150.0 * scaling * (1.0 + scaling) * time * time
            )
            wide = aperture[pl.ds(pl.multiple_of(g * WIDTH, WIDTH), WIDTH)].reshape(1, WIDTH)
            keep = jnp.where(2 * jnp.abs(offset) < wide, 1.0 / TOTAL, 0.0)
            three[0, q, g] = cosine * keep
            three[1, q, g] = sine * keep
            frequency = (GROUPS * lane + g - jnp.where(lane >= HALF, TOTAL, 0)).astype(F32)
            cosine, sine = turn((square_gain * frequency + linear_gain) * frequency)
            two[0, q, g] = cosine
            two[1, q, g] = sine
            return inner

        return lax.fori_loop(0, GROUPS, each_group, carry)

    lax.fori_loop(0, CLASSES, phases, 0)

    sibling = (az, me + 1 - 2 * core)

    def swap(q):
        return pltpu.make_async_remote_copy(
            src_ref=got.at[q, core],
            dst_ref=got.at[q, core],
            send_sem=swap_send.at[q],
            recv_sem=swap_recv.at[q],
            device_id=sibling,
            device_id_type=MESH,
        )

    def arrive(q):
        lot = got.at[q, core]
        pltpu.make_async_copy(lot, lot, made_recv.at[q]).wait()
        swap(q).start()

    upper_rows = lax.broadcasted_iota(jnp.int32, (ROWS, HALF), 0) < LINES
    flip = jnp.where(upper_rows, 1.0, -1.0).astype(F32)
    first_before = core.astype(F32)
    last_after = 1.0 - first_before

    def turned_rows(value):
        return pltpu.roll(value, LINES, 0)

    def range_work(q, carry):
        @pl.when(q < CLASSES - 1)
        def _():
            arrive(q + 1)

        swap(q).wait_recv()
        c_one, s_one = weight(q, 1, 0), weight(q, 1, 1)
        c_two, s_two = weight(q, 2, 0), weight(q, 2, 1)

        def block(segment, g, columns):
            value = got[q, core, segment, g, :, columns]
            before = got[q, 1 - core, jnp.maximum(segment - 1 + core, 0), g, :, columns]
            after = got[q, 1 - core, jnp.minimum(segment + core, 3), g, :, columns]
            if segment == 0:
                before = before * first_before
            if segment == 3:
                after = after * last_after
            value = value + c_one * (after + before)
            side = s_one * (after - before)
            if segment > 0:
                before = got[q, core, segment - 1, g, :, columns]
                value = value + c_two * before
                side = side - s_two * before
            if segment < 3:
                after = got[q, core, segment + 1, g, :, columns]
                value = value + c_two * after
                side = side + s_two * after
            return value + flip * turned_rows(side)

        for upper in range(2):
            for side in range(2):
                columns = slice(side * HALF, (side + 1) * HALF)
                values = []
                for g in range(GROUPS):
                    first, second = (block(2 * upper + i, g, columns) for i in range(2))
                    real = jnp.where(upper_rows, first, turned_rows(second))
                    imag = jnp.where(upper_rows, turned_rows(first), second)
                    cosine, sine = one[0, q, g, :, columns], one[1, q, g, :, columns]
                    values.append((real * cosine - imag * sine, real * sine + imag * cosine))
                values = sixteen(values, -1)
                for g in range(GROUPS):
                    real, imag = values[g]
                    cosine, sine = twiddle[0, g : g + 1, columns], twiddle[1, g : g + 1, columns]
                    values[g] = (real * cosine + imag * sine, imag * cosine - real * sine)
                for g in range(0, GROUPS, 2):
                    spot = slice(upper * HALF + g * 8, upper * HALF + g * 8 + 16)
                    for part in range(2):
                        both = jnp.concatenate([values[g][part], values[g + 1][part]], axis=0)
                        lanes = slice(part * WIDTH + side * HALF, part * WIDTH + (side + 1) * HALF)
                        left[0, spot, lanes], left[1, spot, lanes] = split(both)
        for upper in range(2):
            area = slice(upper * HALF, (upper + 1) * HALF)
            mixed[area, :] = (
                dot(left[0, area, :], dense[0, 0])
                + dot(left[0, area, :], dense[0, 1])
                + dot(left[1, area, :], dense[0, 0])
            )
        for upper in range(2):
            for g in range(0, GROUPS, 2):
                spot = slice(upper * HALF + g * 8, upper * HALF + g * 8 + 16)
                real, imag = mixed[spot, :WIDTH], mixed[spot, WIDTH:]
                cosine = jnp.concatenate([two[0, q, g], two[0, q, g + 1]], axis=0)
                sine = jnp.concatenate([two[1, q, g], two[1, q, g + 1]], axis=0)
                left[0, spot, :WIDTH], left[1, spot, :WIDTH] = split(real * cosine - imag * sine)
                left[0, spot, WIDTH:], left[1, spot, WIDTH:] = split(real * sine + imag * cosine)
        for upper in range(2):
            area = slice(upper * HALF, (upper + 1) * HALF)
            mixed[area, :] = (
                dot(left[0, area, :], dense[1, 0])
                + dot(left[0, area, :], dense[1, 1])
                + dot(left[1, area, :], dense[1, 0])
            )
        for upper in range(2):
            for side in range(2):
                columns = slice(side * HALF, (side + 1) * HALF)
                values = []
                for g in range(GROUPS):
                    spot = slice(upper * HALF + g * 8, upper * HALF + g * 8 + 8)
                    real = mixed[spot, side * HALF : (side + 1) * HALF]
                    imag = mixed[spot, WIDTH + side * HALF : WIDTH + (side + 1) * HALF]
                    cosine, sine = twiddle[0, g : g + 1, columns], twiddle[1, g : g + 1, columns]
                    values.append((real * cosine - imag * sine, real * sine + imag * cosine))
                values = sixteen(values, 1)
                for g in range(GROUPS):
                    real, imag = values[g]
                    cosine, sine = three[0, q, g, :, columns], three[1, q, g, :, columns]
                    real, imag = real * cosine - imag * sine, real * sine + imag * cosine
                    first = 2 * upper * GROUPS + g
                    back[q, first, :, columns] = jnp.where(upper_rows, real, turned_rows(imag))
                    back[q, first + GROUPS, :, columns] = jnp.where(
                        upper_rows, turned_rows(real), imag
                    )
        for dz, dx, dy, dc in HOMEWARD:
            target = place(zs[dz], near[dx], ys[dy], cores[dc])
            piece = zs[dz] * GROUPS + target[1]

            def send():
                pltpu.make_async_remote_copy(
                    src_ref=back.at[q, piece],
                    dst_ref=home.at[q, chip],
                    send_sem=back_send.at[q],
                    recv_sem=back_recv.at[q],
                    device_id=target,
                    device_id_type=MESH,
                ).start()

            def keep():
                pltpu.make_async_copy(
                    back.at[q, piece], home.at[q, chip], back_recv.at[q]
                ).start()

            if (dx, dy, dc) == (0, 0, 0) and dz in (0, 2):
                pl.when(jnp.logical_not(own_plane[dz // 2]))(send)
                pl.when(own_plane[dz // 2])(keep)
            else:
                send()
        return carry

    arrive(0)
    loads[6].wait()
    lax.fori_loop(0, CLASSES, range_work, 0)

    def drain(buffer, semaphore, q):
        @pl.when(same)
        def _():
            lot = buffer.at[q, pl.ds(0, CHIPS - 1)]
            pltpu.make_async_copy(lot, lot, semaphore.at[q]).wait()

        @pl.when(jnp.logical_not(same))
        def _():
            lot = buffer.at[q]
            pltpu.make_async_copy(lot, lot, semaphore.at[q]).wait()

    def drain_forward(q, carry):
        swap(q).wait_send()
        drain(made, made_send, q)
        return carry

    lax.fori_loop(0, CLASSES, drain_forward, 0)

    loads[7].wait()

    def focused(q):
        lot = home.at[q]
        pltpu.make_async_copy(lot, lot, back_recv.at[q]).wait()
        high, low = split(home[q].reshape(CHIPS * ROWS, WIDTH))
        return dot(inverse[q, 0], high) + dot(inverse[q, 1], high) + dot(inverse[q, 0], low)

    total[...] = focused(0)

    def focus(q, carry):
        total[...] += focused(q)
        drain(back, back_send, q - 1)
        return carry

    lax.fori_loop(1, CLASSES - 1, focus, 0)
    drain(back, back_send, CLASSES - 2)
    result = total[...] + focused(CLASSES - 1)
    out[0] = result[:SEG, :]
    out[1] = result[SEG:, :]
    drain(back, back_send, CLASSES - 1)


def per_device(tables, echo, range_row, aperture, centroid_table, rate_table):
    hbm = pl.BlockSpec(memory_space=pltpu.HBM)
    semaphore = pltpu.SemaphoreType.DMA
    return pl.pallas_call(
        kernel,
        out_shape=pltpu.VMEM((2, SEG, WIDTH), F32),
        in_specs=[hbm] * 9,
        out_specs=pl.BlockSpec(memory_space=pltpu.VMEM),
        scratch_shapes=[
            pltpu.VMEM((2, SEG, WIDTH), F32),
            pltpu.VMEM((2, 2 * SEG, WIDTH), BF16),
            pltpu.VMEM((TOTAL,), jnp.int32),
            pltpu.VMEM((TOTAL,), jnp.int32),
            pltpu.SMEM((64,), jnp.int32),
            pltpu.SMEM((64,), F32),
            pltpu.VMEM((CLASSES, 2, 2 * SEG, 2 * SEG), BF16),
            pltpu.VMEM((CLASSES, 2, 2 * SEG, 2 * SEG), BF16),
            pltpu.VMEM((2, 2, 2 * WIDTH, 2 * WIDTH), BF16),
            pltpu.VMEM((2, GROUPS, WIDTH), F32),
            pltpu.VMEM((CLASSES, CHIPS, ROWS, WIDTH), F32),
            pltpu.VMEM((CLASSES, 2, PAIRS, GROUPS, ROWS, WIDTH), F32),
            pltpu.VMEM((CLASSES, CHIPS, ROWS, WIDTH), F32),
            pltpu.VMEM((CLASSES, CHIPS, ROWS, WIDTH), F32),
            pltpu.VMEM((2, CLASSES, GROUPS, ROWS, WIDTH), F32),
            pltpu.VMEM((2, CLASSES, GROUPS, ROWS, WIDTH), F32),
            pltpu.VMEM((2, CLASSES, GROUPS, ROWS, WIDTH), F32),
            pltpu.VMEM((GROUPS, WIDTH), jnp.int32),
            pltpu.VMEM((GROUPS, WIDTH), F32),
            pltpu.VMEM((2, 2 * HALF, 2 * WIDTH), BF16),
            pltpu.VMEM((2 * HALF, 2 * WIDTH), F32),
            pltpu.VMEM((2 * SEG, WIDTH), F32),
            semaphore((8,)),
            semaphore((CLASSES,)),
            semaphore((CLASSES,)),
            semaphore((CLASSES,)),
            semaphore((CLASSES,)),
            semaphore((CLASSES,)),
            semaphore((CLASSES,)),
            semaphore((CLASSES,)),
        ],
        compiler_params=pltpu.CompilerParams(
            collective_id=0, has_side_effects=True, vmem_limit_bytes=52 * 1024 * 1024
        ),
    )(
        *(
            pltpu.with_memory_space_constraint(operand, pltpu.HBM)
            for operand in (echo, range_row, aperture, centroid_table, rate_table, *tables)
        )
    )


def solution(mesh):
    forward, inverse = azimuth_tables()
    dense, twiddle = range_tables()
    tables = tuple(jnp.asarray(table) for table in (forward, inverse, dense, twiddle))
    in_specs = (P(None, "az", "rg"), P(), P(), P(), P())
    out_specs = P(None, "az", "rg")
    return jax.shard_map(
        partial(per_device, tables),
        mesh=mesh,
        in_specs=in_specs,
        out_specs=out_specs,
        check_vma=False,
    )
```

```python
from functools import partial
import math

import jax
import jax.numpy as jnp
import numpy as np
from jax import lax
from jax.experimental import pallas as pl
from jax.experimental.pallas import tpu as pltpu
from jax.sharding import PartitionSpec as P
import ml_dtypes

F32 = jnp.float32
BF16 = jnp.bfloat16
MESH = pl.DeviceIdType.MESH

SEG = 256
CLASSES = 5
LENGTH = SEG * CLASSES
GROUPS = 16
WIDTH = 256
TOTAL = GROUPS * WIDTH
CHIPS = 64
LINES = SEG // CHIPS
ROWS = 2 * LINES
PAIRS = 4
HALF = 128


def links_of(step):
    load = np.zeros(6)
    for axis, hops in enumerate(step[:3]):
        load[2 * axis] += hops in (1, 2)
        load[2 * axis + 1] += hops in (2, 3)
    return load


def hops(step):
    return sum(min(count, 4 - count) for count in step[:3])


def spread(steps):
    load, remaining, ordered = np.zeros(6), list(steps), []
    while remaining:
        levels = [
            (np.ptp(load + links_of(step)), -links_of(step).sum(), step) for step in remaining
        ]
        chosen = min(levels)[2]
        ordered.append(chosen)
        remaining.remove(chosen)
        load = load + links_of(chosen)
    return ordered


RING = range(4)
OUTWARD = spread([(dz, dx, dy) for dz in RING for dx in RING for dy in RING])
HOMEWARD = spread(
    [(dz, dx, dy, dc) for dz in RING for dx in (0, 2) for dy in RING for dc in (0, 1)]
)


def pair_split(values):
    high = values.astype(ml_dtypes.bfloat16)
    low = (values - high.astype(np.float64)).astype(ml_dtypes.bfloat16)
    return np.stack([high, low])


def azimuth_tables():
    pulse = np.arange(SEG)
    bins = np.arange(SEG)[None, :] * CLASSES + np.arange(CLASSES)[:, None]
    turns = ((2 * SEG + pulse)[None, :, None] * bins[:, None, :]) % LENGTH
    angle = turns * (2.0 * np.pi / LENGTH)
    scale = 1.0 / math.sqrt(LENGTH)
    cosine, sine = np.cos(angle) * scale, np.sin(angle) * scale
    real = np.stack([cosine, -sine]).reshape(2, CLASSES, SEG, CHIPS, LINES)
    imag = np.stack([sine, cosine]).reshape(2, CLASSES, SEG, CHIPS, LINES)
    inverse = np.stack([real, imag]).transpose(2, 0, 3, 4, 1, 5)
    inverse = inverse.reshape(CLASSES, 2 * SEG, CHIPS * ROWS)
    forward = inverse.transpose(0, 2, 1)
    return pair_split(forward).transpose(1, 0, 2, 3), pair_split(inverse).transpose(1, 0, 2, 3)


def range_tables():
    index = np.arange(WIDTH)
    angle = (index[:, None] * index[None, :] % WIDTH) * (2.0 * np.pi / WIDTH)
    cosine, sine = np.cos(angle), np.sin(angle)
    forward = np.block([[cosine, -sine], [sine, cosine]])
    inverse = np.block([[cosine, sine], [-sine, cosine]])
    fine = np.arange(GROUPS)[:, None] * index[None, :] * (2.0 * np.pi / TOTAL)
    twiddle = np.stack([np.cos(fine), np.sin(fine)]).astype(np.float32)
    return np.stack([pair_split(forward), pair_split(inverse)]), twiddle


WEIGHTS = [
    [
        (math.cos(2.0 * math.pi * q * step / CLASSES), math.sin(2.0 * math.pi * q * step / CLASSES))
        for step in (1, 2)
    ]
    for q in range(CLASSES)
]


def weight(q, step, part):
    value = jnp.float32(WEIGHTS[0][step - 1][part])
    for other in range(1, CLASSES):
        value = jnp.where(q == other, jnp.float32(WEIGHTS[other][step - 1][part]), value)
    return value


def split(value):
    high = value.astype(BF16)
    return high, (value - high.astype(F32)).astype(BF16)


def fitted(function, powers):
    nodes = np.cos((np.arange(400) + 0.5) * np.pi / 400) * 0.5
    nodes = nodes[nodes > 0]
    basis = np.stack([(2 * nodes) ** p for p in powers], axis=1)
    solved = np.linalg.lstsq(basis, function(2.0 * np.pi * nodes), rcond=None)[0]
    return [float(value * 2.0**p) for value, p in zip(solved, powers)]


SINE = fitted(np.sin, [1, 3, 5, 7, 9, 11])
COSINE = fitted(np.cos, [0, 2, 4, 6, 8, 10, 12])


def turn(cycles):
    left = cycles - jnp.floor(cycles + 0.5)
    square = left * left
    sine, cosine = SINE[-1], COSINE[-1]
    for value in SINE[-2::-1]:
        sine = sine * square + value
    for value in COSINE[-2::-1]:
        cosine = cosine * square + value
    return cosine, sine * left


def times_turn(value, quarter):
    real, imag = value
    quarter %= 4
    if quarter == 0:
        return real, imag
    if quarter == 1:
        return -imag, real
    if quarter == 2:
        return -real, -imag
    return imag, -real


def four(values, sign):
    a, b, c, d = values
    ac = (a[0] + c[0], a[1] + c[1])
    am = (a[0] - c[0], a[1] - c[1])
    bd = (b[0] + d[0], b[1] + d[1])
    bm = times_turn((b[0] - d[0], b[1] - d[1]), sign)
    return [
        (ac[0] + bd[0], ac[1] + bd[1]),
        (am[0] + bm[0], am[1] + bm[1]),
        (ac[0] - bd[0], ac[1] - bd[1]),
        (am[0] - bm[0], am[1] - bm[1]),
    ]


def sixteen(values, sign):
    inner = [four(values[low::4], sign) for low in range(4)]
    result = [None] * 16
    for first in range(4):
        column = []
        for low in range(4):
            real, imag = inner[low][first]
            step = low * first
            if step % 4 == 0:
                column.append(times_turn((real, imag), sign * (step // 4)))
            else:
                angle = sign * 2.0 * math.pi * step / 16
                cosine, sine = math.cos(angle), math.sin(angle)
                if step % 2 == 0:
                    root = math.sqrt(0.5)
                    up = 1.0 if cosine > 0 else -1.0
                    side = 1.0 if sine > 0 else -1.0
                    if up == side:
                        column.append(((real - imag) * (up * root), (real + imag) * (up * root)))
                    else:
                        column.append(((real + imag) * (up * root), (imag - real) * (up * root)))
                else:
                    column.append((real * cosine - imag * sine, real * sine + imag * cosine))
        outer = four(column, sign)
        for second in range(4):
            result[first + 4 * second] = outer[second]
    return result


def dot(left, right):
    return jnp.dot(left, right, preferred_element_type=F32)


def kernel(
    echo_hbm,
    range_row_hbm,
    aperture_hbm,
    centroid_hbm,
    rate_hbm,
    forward_hbm,
    inverse_hbm,
    dense_hbm,
    twiddle_hbm,
    out,
    echo,
    pulses,
    range_row,
    aperture,
    centroid_table,
    rate_table,
    forward,
    inverse,
    dense,
    twiddle,
    made,
    got,
    back,
    home,
    one,
    two,
    three,
    centroid,
    rate,
    left,
    mixed,
    total,
    both_sem,
    load_sem,
    forward_sem,
    made_send,
    made_recv,
    swap_send,
    swap_recv,
    back_send,
    back_recv,
):
    az = lax.axis_index("az")
    me = lax.axis_index("rg")
    z, x_low = az // 2, az % 2
    x, y, core = (me // 8) * 2 + x_low, (me // 2) % 4, me % 2
    chip = z * 16 + x * 4 + y
    same = x_low == core
    apart = jnp.where(same, 0, 1)
    zs = [(z + step) % 4 for step in RING]
    xs = [(x + step) % 4 for step in RING]
    ys = [(y + step) % 4 for step in RING]
    cores = [core, 1 - core]
    near = {step: (x + apart + step) % 4 for step in (0, 2)}

    def place(z_at, x_at, y_at, core_at):
        return (z_at * 2 + x_at % 2, (x_at // 2) * 8 + y_at * 2 + core_at)

    loads = [
        pltpu.make_async_copy(source, target, load_sem.at[i])
        for i, (source, target) in enumerate(
            (
                (echo_hbm, echo),
                (range_row_hbm, range_row),
                (aperture_hbm, aperture),
                (centroid_hbm, centroid_table),
                (rate_hbm, rate_table),
                (twiddle_hbm, twiddle),
                (dense_hbm, dense),
                (inverse_hbm, inverse),
            )
        )
    ]
    forward_loads = [
        pltpu.make_async_copy(forward_hbm.at[q], forward.at[q], forward_sem.at[q])
        for q in range(CLASSES)
    ]
    loads[0].start()
    forward_loads[0].start()

    barrier = pltpu.get_barrier_semaphore()
    sibling = (az, me + 1 - 2 * core)
    told = lax.rem(y, 2)

    def greet(target):
        pl.semaphore_signal(barrier, inc=1, device_id=target, device_id_type=MESH)

    own_turn = jnp.logical_and(same, told == core)
    for dz, dx, dy, dc in sorted(HOMEWARD, key=hops, reverse=True):
        if dc == 0:
            target = place(zs[dz], near[dx], ys[dy], told)
            if (dz, dx, dy) == (0, 0, 0):
                pl.when(jnp.logical_not(own_turn))(partial(greet, target))
            else:
                greet(target)
    greet(sibling)

    loads[0].wait()
    for part in range(2):
        rows = slice(part * SEG, (part + 1) * SEG)
        pulses[0, rows, :], pulses[1, rows, :] = split(echo[part])

    def azimuth(q, carry):
        pltpu.make_async_copy(forward_hbm.at[q], forward.at[q], forward_sem.at[q]).wait()
        spectrum = (
            dot(forward[q, 0], pulses[0])
            + dot(forward[q, 1], pulses[0])
            + dot(forward[q, 0], pulses[1])
        )
        made[q] = spectrum.reshape(CHIPS, ROWS, WIDTH)

        @pl.when(q == 0)
        def _():
            pl.semaphore_wait(barrier, CHIPS // 2 + 1 - jnp.where(own_turn, 1, 0))
            pl.semaphore_signal(both_sem, inc=1, device_id=sibling, device_id_type=MESH)
            pl.semaphore_wait(both_sem, 1)

        for dz, dx, dy in OUTWARD:
            target = place(zs[dz], xs[dx], ys[dy], x_low)
            owner = zs[dz] * 16 + xs[dx] * 4 + ys[dy]

            def send():
                pltpu.make_async_remote_copy(
                    src_ref=made.at[q, owner],
                    dst_ref=got.at[q, x_low, z, me],
                    send_sem=made_send.at[q],
                    recv_sem=made_recv.at[q],
                    device_id=target,
                    device_id_type=MESH,
                ).start()

            def keep():
                pltpu.make_async_copy(
                    made.at[q, owner], got.at[q, x_low, z, me], made_recv.at[q]
                ).start()

            if (dz, dx, dy) == (0, 0, 0):
                pl.when(jnp.logical_not(same))(send)
                pl.when(same)(keep)
            else:
                send()

        @pl.when(q == 0)
        def _():
            for copy in forward_loads[1:] + loads[1:]:
                copy.start()

        return carry

    lax.fori_loop(0, CLASSES, azimuth, 0)

    for copy in loads[1:6]:
        copy.wait()
    for g in range(GROUPS):
        here = pl.ds(g * WIDTH, WIDTH)
        centroid[g : g + 1, :] = range_row[here].reshape(1, WIDTH)
    rows = centroid[...]
    centers = jnp.zeros((GROUPS, WIDTH), jnp.int32)
    rates = jnp.zeros((GROUPS, WIDTH), F32)
    for entry in range(64):
        hit = rows == entry
        centers = jnp.where(hit, centroid_table[entry], centers)
        rates = jnp.where(hit, rate_table[entry], rates)
    centroid[...] = centers
    rate[...] = rates

    lane = lax.broadcasted_iota(jnp.int32, (ROWS, WIDTH), 1)
    line = lax.broadcasted_iota(jnp.int32, (ROWS, WIDTH), 0) % LINES

    def doppler(bins):
        fraction = bins.astype(F32) * (1.0 / LENGTH)
        squared = jnp.maximum(1.0 - 1.5 * fraction * fraction, 0.1)
        migration = jnp.sqrt(squared)
        return squared, migration, 1.0 / migration - 1.0

    def phases(q, carry):
        bins = CLASSES * (LINES * chip + line) + q
        unused, low_migration, low_scaling = doppler(bins)
        unused, high_migration, high_scaling = doppler(bins - LENGTH)
        squared, unused, zero_scaling = doppler(jnp.where(bins < LENGTH // 2, bins, bins - LENGTH))
        square_gain = squared * (150.0 / (TOTAL * TOTAL))
        linear_gain = zero_scaling * 0.05

        def each_group(g, inner):
            here = pl.ds(g, 1)
            center = centroid[here, :]
            time = (g * WIDTH + lane).astype(F32) * (1.0 / TOTAL) + (0.5 / TOTAL - 0.5)
            low = bins <= center + (LENGTH // 2 - 1)
            migration = jnp.where(low, low_migration, high_migration)
            scaling = jnp.where(low, low_scaling, high_scaling)
            offset = jnp.where(low, bins, bins - LENGTH) - center
            lagged = time - 0.2 * scaling
            cosine, sine = turn(-150.0 * scaling * lagged * lagged)
            one[0, q, g] = cosine
            one[1, q, g] = sine
            cosine, sine = turn(
                rate[here, :] * (migration - 1.0) + 150.0 * scaling * (1.0 + scaling) * time * time
            )
            wide = aperture[pl.ds(pl.multiple_of(g * WIDTH, WIDTH), WIDTH)].reshape(1, WIDTH)
            keep = jnp.where(2 * jnp.abs(offset) < wide, 1.0 / TOTAL, 0.0)
            three[0, q, g] = cosine * keep
            three[1, q, g] = sine * keep
            frequency = (GROUPS * lane + g - jnp.where(lane >= HALF, TOTAL, 0)).astype(F32)
            cosine, sine = turn((square_gain * frequency + linear_gain) * frequency)
            two[0, q, g] = cosine
            two[1, q, g] = sine
            return inner

        return lax.fori_loop(0, GROUPS, each_group, carry)

    lax.fori_loop(0, CLASSES, phases, 0)

    def swap(q):
        return pltpu.make_async_remote_copy(
            src_ref=got.at[q, core],
            dst_ref=got.at[q, core],
            send_sem=swap_send.at[q],
            recv_sem=swap_recv.at[q],
            device_id=sibling,
            device_id_type=MESH,
        )

    def arrive(q):
        lot = got.at[q, core]
        pltpu.make_async_copy(lot, lot, made_recv.at[q]).wait()
        swap(q).start()

    upper_rows = lax.broadcasted_iota(jnp.int32, (ROWS, HALF), 0) < LINES
    flip = jnp.where(upper_rows, 1.0, -1.0).astype(F32)
    first_before = core.astype(F32)
    last_after = 1.0 - first_before

    def turned_rows(value):
        return pltpu.roll(value, LINES, 0)

    def range_work(q, carry):
        @pl.when(q < CLASSES - 1)
        def _():
            arrive(q + 1)

        swap(q).wait_recv()
        c_one, s_one = weight(q, 1, 0), weight(q, 1, 1)
        c_two, s_two = weight(q, 2, 0), weight(q, 2, 1)

        def block(segment, g, columns):
            value = got[q, core, segment, g, :, columns]
            before = got[q, 1 - core, jnp.maximum(segment - 1 + core, 0), g, :, columns]
            after = got[q, 1 - core, jnp.minimum(segment + core, 3), g, :, columns]
            if segment == 0:
                before = before * first_before
            if segment == 3:
                after = after * last_after
            value = value + c_one * (after + before)
            side = s_one * (after - before)
            if segment > 0:
                before = got[q, core, segment - 1, g, :, columns]
                value = value + c_two * before
                side = side - s_two * before
            if segment < 3:
                after = got[q, core, segment + 1, g, :, columns]
                value = value + c_two * after
                side = side + s_two * after
            return value + flip * turned_rows(side)

        for upper in range(2):
            for side in range(2):
                columns = slice(side * HALF, (side + 1) * HALF)
                values = []
                for g in range(GROUPS):
                    first, second = (block(2 * upper + i, g, columns) for i in range(2))
                    real = jnp.where(upper_rows, first, turned_rows(second))
                    imag = jnp.where(upper_rows, turned_rows(first), second)
                    cosine, sine = one[0, q, g, :, columns], one[1, q, g, :, columns]
                    values.append((real * cosine - imag * sine, real * sine + imag * cosine))
                values = sixteen(values, -1)
                for g in range(GROUPS):
                    real, imag = values[g]
                    cosine, sine = twiddle[0, g : g + 1, columns], twiddle[1, g : g + 1, columns]
                    values[g] = (real * cosine + imag * sine, imag * cosine - real * sine)
                for g in range(0, GROUPS, 2):
                    spot = slice(upper * HALF + g * 8, upper * HALF + g * 8 + 16)
                    for part in range(2):
                        both = jnp.concatenate([values[g][part], values[g + 1][part]], axis=0)
                        lanes = slice(part * WIDTH + side * HALF, part * WIDTH + (side + 1) * HALF)
                        left[0, spot, lanes], left[1, spot, lanes] = split(both)
        for upper in range(2):
            area = slice(upper * HALF, (upper + 1) * HALF)
            mixed[area, :] = (
                dot(left[0, area, :], dense[0, 0])
                + dot(left[0, area, :], dense[0, 1])
                + dot(left[1, area, :], dense[0, 0])
            )
        for upper in range(2):
            for g in range(0, GROUPS, 2):
                spot = slice(upper * HALF + g * 8, upper * HALF + g * 8 + 16)
                real, imag = mixed[spot, :WIDTH], mixed[spot, WIDTH:]
                cosine = jnp.concatenate([two[0, q, g], two[0, q, g + 1]], axis=0)
                sine = jnp.concatenate([two[1, q, g], two[1, q, g + 1]], axis=0)
                left[0, spot, :WIDTH], left[1, spot, :WIDTH] = split(real * cosine - imag * sine)
                left[0, spot, WIDTH:], left[1, spot, WIDTH:] = split(real * sine + imag * cosine)
        for upper in range(2):
            area = slice(upper * HALF, (upper + 1) * HALF)
            mixed[area, :] = (
                dot(left[0, area, :], dense[1, 0])
                + dot(left[0, area, :], dense[1, 1])
                + dot(left[1, area, :], dense[1, 0])
            )
        for upper in range(2):
            for side in range(2):
                columns = slice(side * HALF, (side + 1) * HALF)
                values = []
                for g in range(GROUPS):
                    spot = slice(upper * HALF + g * 8, upper * HALF + g * 8 + 8)
                    real = mixed[spot, side * HALF : (side + 1) * HALF]
                    imag = mixed[spot, WIDTH + side * HALF : WIDTH + (side + 1) * HALF]
                    cosine, sine = twiddle[0, g : g + 1, columns], twiddle[1, g : g + 1, columns]
                    values.append((real * cosine - imag * sine, real * sine + imag * cosine))
                values = sixteen(values, 1)
                for g in range(GROUPS):
                    real, imag = values[g]
                    cosine, sine = three[0, q, g, :, columns], three[1, q, g, :, columns]
                    real, imag = real * cosine - imag * sine, real * sine + imag * cosine
                    first = 2 * upper * GROUPS + g
                    back[q, first, :, columns] = jnp.where(upper_rows, real, turned_rows(imag))
                    back[q, first + GROUPS, :, columns] = jnp.where(
                        upper_rows, turned_rows(real), imag
                    )
        for dz, dx, dy, dc in HOMEWARD:
            target = place(zs[dz], near[dx], ys[dy], cores[dc])
            piece = zs[dz] * GROUPS + target[1]

            def send():
                pltpu.make_async_remote_copy(
                    src_ref=back.at[q, piece],
                    dst_ref=home.at[q, chip],
                    send_sem=back_send.at[q],
                    recv_sem=back_recv.at[q],
                    device_id=target,
                    device_id_type=MESH,
                ).start()

            def keep():
                pltpu.make_async_copy(
                    back.at[q, piece], home.at[q, chip], back_recv.at[q]
                ).start()

            if (dz, dx, dy, dc) == (0, 0, 0, 0):
                pl.when(jnp.logical_not(same))(send)
                pl.when(same)(keep)
            else:
                send()
        return carry

    arrive(0)
    loads[6].wait()
    lax.fori_loop(0, CLASSES, range_work, 0)

    def drain(buffer, semaphore, q):
        @pl.when(same)
        def _():
            lot = buffer.at[q, pl.ds(0, CHIPS - 1)]
            pltpu.make_async_copy(lot, lot, semaphore.at[q]).wait()

        @pl.when(jnp.logical_not(same))
        def _():
            lot = buffer.at[q]
            pltpu.make_async_copy(lot, lot, semaphore.at[q]).wait()

    def drain_forward(q, carry):
        swap(q).wait_send()
        drain(made, made_send, q)
        return carry

    lax.fori_loop(0, CLASSES, drain_forward, 0)

    loads[7].wait()

    def focused(q):
        lot = home.at[q]
        pltpu.make_async_copy(lot, lot, back_recv.at[q]).wait()
        high, low = split(home[q].reshape(CHIPS * ROWS, WIDTH))
        return dot(inverse[q, 0], high) + dot(inverse[q, 1], high) + dot(inverse[q, 0], low)

    total[...] = focused(0)

    def focus(q, carry):
        total[...] += focused(q)
        drain(back, back_send, q - 1)
        return carry

    lax.fori_loop(1, CLASSES - 1, focus, 0)
    drain(back, back_send, CLASSES - 2)
    result = total[...] + focused(CLASSES - 1)
    out[0] = result[:SEG, :]
    out[1] = result[SEG:, :]
    drain(back, back_send, CLASSES - 1)


def per_device(tables, echo, range_row, aperture, centroid_table, rate_table):
    hbm = pl.BlockSpec(memory_space=pltpu.HBM)
    semaphore = pltpu.SemaphoreType.DMA
    return pl.pallas_call(
        kernel,
        out_shape=pltpu.VMEM((2, SEG, WIDTH), F32),
        in_specs=[hbm] * 9,
        out_specs=pl.BlockSpec(memory_space=pltpu.VMEM),
        scratch_shapes=[
            pltpu.VMEM((2, SEG, WIDTH), F32),
            pltpu.VMEM((2, 2 * SEG, WIDTH), BF16),
            pltpu.VMEM((TOTAL,), jnp.int32),
            pltpu.VMEM((TOTAL,), jnp.int32),
            pltpu.SMEM((64,), jnp.int32),
            pltpu.SMEM((64,), F32),
            pltpu.VMEM((CLASSES, 2, 2 * SEG, 2 * SEG), BF16),
            pltpu.VMEM((CLASSES, 2, 2 * SEG, 2 * SEG), BF16),
            pltpu.VMEM((2, 2, 2 * WIDTH, 2 * WIDTH), BF16),
            pltpu.VMEM((2, GROUPS, WIDTH), F32),
            pltpu.VMEM((CLASSES, CHIPS, ROWS, WIDTH), F32),
            pltpu.VMEM((CLASSES, 2, PAIRS, GROUPS, ROWS, WIDTH), F32),
            pltpu.VMEM((CLASSES, CHIPS, ROWS, WIDTH), F32),
            pltpu.VMEM((CLASSES, CHIPS, ROWS, WIDTH), F32),
            pltpu.VMEM((2, CLASSES, GROUPS, ROWS, WIDTH), F32),
            pltpu.VMEM((2, CLASSES, GROUPS, ROWS, WIDTH), F32),
            pltpu.VMEM((2, CLASSES, GROUPS, ROWS, WIDTH), F32),
            pltpu.VMEM((GROUPS, WIDTH), jnp.int32),
            pltpu.VMEM((GROUPS, WIDTH), F32),
            pltpu.VMEM((2, 2 * HALF, 2 * WIDTH), BF16),
            pltpu.VMEM((2 * HALF, 2 * WIDTH), F32),
            pltpu.VMEM((2 * SEG, WIDTH), F32),
            pltpu.SemaphoreType.REGULAR,
            semaphore((8,)),
            semaphore((CLASSES,)),
            semaphore((CLASSES,)),
            semaphore((CLASSES,)),
            semaphore((CLASSES,)),
            semaphore((CLASSES,)),
            semaphore((CLASSES,)),
            semaphore((CLASSES,)),
        ],
        compiler_params=pltpu.CompilerParams(
            collective_id=0, has_side_effects=True, vmem_limit_bytes=52 * 1024 * 1024
        ),
    )(
        *(
            pltpu.with_memory_space_constraint(operand, pltpu.HBM)
            for operand in (echo, range_row, aperture, centroid_table, rate_table, *tables)
        )
    )


def solution(mesh):
    forward, inverse = azimuth_tables()
    dense, twiddle = range_tables()
    tables = tuple(jnp.asarray(table) for table in (forward, inverse, dense, twiddle))
    in_specs = (P(None, "az", "rg"), P(), P(), P(), P())
    out_specs = P(None, "az", "rg")
    return jax.shard_map(
        partial(per_device, tables),
        mesh=mesh,
        in_specs=in_specs,
        out_specs=out_specs,
        check_vma=False,
    )
```

```python
from functools import partial
import math

import jax
import jax.numpy as jnp
import numpy as np
from jax import lax
from jax.experimental import pallas as pl
from jax.experimental.pallas import tpu as pltpu
from jax.sharding import PartitionSpec as P
import ml_dtypes

F32 = jnp.float32
BF16 = jnp.bfloat16
MESH = pl.DeviceIdType.MESH

SEG = 256
CLASSES = 5
LENGTH = SEG * CLASSES
GROUPS = 16
WIDTH = 256
TOTAL = GROUPS * WIDTH
CHIPS = 64
LINES = SEG // CHIPS
ROWS = 2 * LINES
PAIRS = 4
HALF = 128


def links_of(step):
    load = np.zeros(6)
    for axis, hops in enumerate(step[:3]):
        load[2 * axis] += hops in (1, 2)
        load[2 * axis + 1] += hops in (2, 3)
    return load


def hops(step):
    return sum(min(count, 4 - count) for count in step[:3])


def spread(steps):
    load, remaining, ordered = np.zeros(6), list(steps), []
    while remaining:
        levels = [
            (-hops(step), np.ptp(load + links_of(step)), step) for step in remaining
        ]
        chosen = min(levels)[2]
        ordered.append(chosen)
        remaining.remove(chosen)
        load = load + links_of(chosen)
    return ordered


RING = range(4)
OUTWARD = spread([(dz, dx, dy) for dz in RING for dx in RING for dy in RING])
HOMEWARD = spread(
    [(dz, dx, dy, dc) for dz in RING for dx in (0, 2) for dy in RING for dc in (0, 1)]
)


def pair_split(values):
    high = values.astype(ml_dtypes.bfloat16)
    low = (values - high.astype(np.float64)).astype(ml_dtypes.bfloat16)
    return np.stack([high, low])


def azimuth_tables():
    pulse = np.arange(SEG)
    bins = np.arange(SEG)[None, :] * CLASSES + np.arange(CLASSES)[:, None]
    turns = ((2 * SEG + pulse)[None, :, None] * bins[:, None, :]) % LENGTH
    angle = turns * (2.0 * np.pi / LENGTH)
    scale = 1.0 / math.sqrt(LENGTH)
    cosine, sine = np.cos(angle) * scale, np.sin(angle) * scale
    real = np.stack([cosine, -sine]).reshape(2, CLASSES, SEG, CHIPS, LINES)
    imag = np.stack([sine, cosine]).reshape(2, CLASSES, SEG, CHIPS, LINES)
    inverse = np.stack([real, imag]).transpose(2, 0, 3, 4, 1, 5)
    inverse = inverse.reshape(CLASSES, 2 * SEG, CHIPS * ROWS)
    forward = inverse.transpose(0, 2, 1)
    return pair_split(forward).transpose(1, 0, 2, 3), pair_split(inverse).transpose(1, 0, 2, 3)


def range_tables():
    index = np.arange(WIDTH)
    angle = (index[:, None] * index[None, :] % WIDTH) * (2.0 * np.pi / WIDTH)
    cosine, sine = np.cos(angle), np.sin(angle)
    forward = np.block([[cosine, -sine], [sine, cosine]])
    inverse = np.block([[cosine, sine], [-sine, cosine]])
    fine = np.arange(GROUPS)[:, None] * index[None, :] * (2.0 * np.pi / TOTAL)
    twiddle = np.stack([np.cos(fine), np.sin(fine)]).astype(np.float32)
    return np.stack([pair_split(forward), pair_split(inverse)]), twiddle


WEIGHTS = [
    [
        (math.cos(2.0 * math.pi * q * step / CLASSES), math.sin(2.0 * math.pi * q * step / CLASSES))
        for step in (1, 2)
    ]
    for q in range(CLASSES)
]


def weight(q, step, part):
    value = jnp.float32(WEIGHTS[0][step - 1][part])
    for other in range(1, CLASSES):
        value = jnp.where(q == other, jnp.float32(WEIGHTS[other][step - 1][part]), value)
    return value


def split(value):
    high = value.astype(BF16)
    return high, (value - high.astype(F32)).astype(BF16)


def fitted(function, powers):
    nodes = np.cos((np.arange(400) + 0.5) * np.pi / 400) * 0.5
    nodes = nodes[nodes > 0]
    basis = np.stack([(2 * nodes) ** p for p in powers], axis=1)
    solved = np.linalg.lstsq(basis, function(2.0 * np.pi * nodes), rcond=None)[0]
    return [float(value * 2.0**p) for value, p in zip(solved, powers)]


SINE = fitted(np.sin, [1, 3, 5, 7, 9, 11])
COSINE = fitted(np.cos, [0, 2, 4, 6, 8, 10, 12])


def turn(cycles):
    left = cycles - jnp.floor(cycles + 0.5)
    square = left * left
    sine, cosine = SINE[-1], COSINE[-1]
    for value in SINE[-2::-1]:
        sine = sine * square + value
    for value in COSINE[-2::-1]:
        cosine = cosine * square + value
    return cosine, sine * left


def times_turn(value, quarter):
    real, imag = value
    quarter %= 4
    if quarter == 0:
        return real, imag
    if quarter == 1:
        return -imag, real
    if quarter == 2:
        return -real, -imag
    return imag, -real


def four(values, sign):
    a, b, c, d = values
    ac = (a[0] + c[0], a[1] + c[1])
    am = (a[0] - c[0], a[1] - c[1])
    bd = (b[0] + d[0], b[1] + d[1])
    bm = times_turn((b[0] - d[0], b[1] - d[1]), sign)
    return [
        (ac[0] + bd[0], ac[1] + bd[1]),
        (am[0] + bm[0], am[1] + bm[1]),
        (ac[0] - bd[0], ac[1] - bd[1]),
        (am[0] - bm[0], am[1] - bm[1]),
    ]


def sixteen(values, sign):
    inner = [four(values[low::4], sign) for low in range(4)]
    result = [None] * 16
    for first in range(4):
        column = []
        for low in range(4):
            real, imag = inner[low][first]
            step = low * first
            if step % 4 == 0:
                column.append(times_turn((real, imag), sign * (step // 4)))
            else:
                angle = sign * 2.0 * math.pi * step / 16
                cosine, sine = math.cos(angle), math.sin(angle)
                if step % 2 == 0:
                    root = math.sqrt(0.5)
                    up = 1.0 if cosine > 0 else -1.0
                    side = 1.0 if sine > 0 else -1.0
                    if up == side:
                        column.append(((real - imag) * (up * root), (real + imag) * (up * root)))
                    else:
                        column.append(((real + imag) * (up * root), (imag - real) * (up * root)))
                else:
                    column.append((real * cosine - imag * sine, real * sine + imag * cosine))
        outer = four(column, sign)
        for second in range(4):
            result[first + 4 * second] = outer[second]
    return result


def dot(left, right):
    return jnp.dot(left, right, preferred_element_type=F32)


def kernel(
    echo_hbm,
    range_row_hbm,
    aperture_hbm,
    centroid_hbm,
    rate_hbm,
    forward_hbm,
    inverse_hbm,
    dense_hbm,
    twiddle_hbm,
    out,
    echo,
    pulses,
    range_row,
    aperture,
    centroid_table,
    rate_table,
    forward,
    inverse,
    dense,
    twiddle,
    made,
    got,
    back,
    home,
    one,
    two,
    three,
    centroid,
    rate,
    left,
    mixed,
    total,
    load_sem,
    forward_sem,
    made_send,
    made_recv,
    swap_send,
    swap_recv,
    back_send,
    back_recv,
):
    az = lax.axis_index("az")
    me = lax.axis_index("rg")
    z, x_low = az // 2, az % 2
    x, y, core = (me // 8) * 2 + x_low, (me // 2) % 4, me % 2
    chip = z * 16 + x * 4 + y
    same = x_low == core
    apart = jnp.where(same, 0, 1)
    zs = [(z + step) % 4 for step in RING]
    xs = [(x + step) % 4 for step in RING]
    ys = [(y + step) % 4 for step in RING]
    cores = [core, 1 - core]
    near = {step: (x + apart + step) % 4 for step in (0, 2)}

    def place(z_at, x_at, y_at, core_at):
        return (z_at * 2 + x_at % 2, (x_at // 2) * 8 + y_at * 2 + core_at)

    loads = [
        pltpu.make_async_copy(source, target, load_sem.at[i])
        for i, (source, target) in enumerate(
            (
                (echo_hbm, echo),
                (range_row_hbm, range_row),
                (aperture_hbm, aperture),
                (centroid_hbm, centroid_table),
                (rate_hbm, rate_table),
                (twiddle_hbm, twiddle),
                (dense_hbm, dense),
                (inverse_hbm, inverse),
            )
        )
    ]
    forward_loads = [
        pltpu.make_async_copy(forward_hbm.at[q], forward.at[q], forward_sem.at[q])
        for q in range(CLASSES)
    ]
    loads[0].start()
    forward_loads[0].start()

    barrier = pltpu.get_barrier_semaphore()

    def greet(target):
        pl.semaphore_signal(barrier, inc=1, device_id=target, device_id_type=MESH)

    for dz, dx, dy, dc in sorted(HOMEWARD, key=hops, reverse=True):
        target = place(zs[dz], near[dx], ys[dy], cores[dc])
        if (dz, dx, dy, dc) == (0, 0, 0, 0):
            pl.when(jnp.logical_not(same))(partial(greet, target))
        else:
            greet(target)

    loads[0].wait()
    for part in range(2):
        rows = slice(part * SEG, (part + 1) * SEG)
        pulses[0, rows, :], pulses[1, rows, :] = split(echo[part])

    def azimuth(q, carry):
        pltpu.make_async_copy(forward_hbm.at[q], forward.at[q], forward_sem.at[q]).wait()
        spectrum = (
            dot(forward[q, 0], pulses[0])
            + dot(forward[q, 1], pulses[0])
            + dot(forward[q, 0], pulses[1])
        )
        made[q] = spectrum.reshape(CHIPS, ROWS, WIDTH)

        @pl.when(q == 0)
        def _():
            pl.semaphore_wait(barrier, CHIPS - jnp.where(same, 1, 0))

        for dz, dx, dy in OUTWARD:
            target = place(zs[dz], xs[dx], ys[dy], x_low)
            owner = zs[dz] * 16 + xs[dx] * 4 + ys[dy]

            def send():
                pltpu.make_async_remote_copy(
                    src_ref=made.at[q, owner],
                    dst_ref=got.at[q, x_low, z, me],
                    send_sem=made_send.at[q],
                    recv_sem=made_recv.at[q],
                    device_id=target,
                    device_id_type=MESH,
                ).start()

            def keep():
                pltpu.make_async_copy(
                    made.at[q, owner], got.at[q, x_low, z, me], made_recv.at[q]
                ).start()

            if (dz, dx, dy) == (0, 0, 0):
                pl.when(jnp.logical_not(same))(send)
                pl.when(same)(keep)
            else:
                send()

        @pl.when(q == 0)
        def _():
            for copy in forward_loads[1:] + loads[1:]:
                copy.start()

        return carry

    lax.fori_loop(0, CLASSES, azimuth, 0)

    for copy in loads[1:6]:
        copy.wait()
    for g in range(GROUPS):
        here = pl.ds(g * WIDTH, WIDTH)
        centroid[g : g + 1, :] = range_row[here].reshape(1, WIDTH)
    rows = centroid[...]
    centers = jnp.zeros((GROUPS, WIDTH), jnp.int32)
    rates = jnp.zeros((GROUPS, WIDTH), F32)
    for entry in range(64):
        hit = rows == entry
        centers = jnp.where(hit, centroid_table[entry], centers)
        rates = jnp.where(hit, rate_table[entry], rates)
    centroid[...] = centers
    rate[...] = rates

    lane = lax.broadcasted_iota(jnp.int32, (ROWS, WIDTH), 1)
    line = lax.broadcasted_iota(jnp.int32, (ROWS, WIDTH), 0) % LINES

    def doppler(bins):
        fraction = bins.astype(F32) * (1.0 / LENGTH)
        squared = jnp.maximum(1.0 - 1.5 * fraction * fraction, 0.1)
        migration = jnp.sqrt(squared)
        return squared, migration, 1.0 / migration - 1.0

    def phases(q, carry):
        bins = CLASSES * (LINES * chip + line) + q
        unused, low_migration, low_scaling = doppler(bins)
        unused, high_migration, high_scaling = doppler(bins - LENGTH)
        squared, unused, zero_scaling = doppler(jnp.where(bins < LENGTH // 2, bins, bins - LENGTH))
        square_gain = squared * (150.0 / (TOTAL * TOTAL))
        linear_gain = zero_scaling * 0.05

        def each_group(g, inner):
            here = pl.ds(g, 1)
            center = centroid[here, :]
            time = (g * WIDTH + lane).astype(F32) * (1.0 / TOTAL) + (0.5 / TOTAL - 0.5)
            low = bins <= center + (LENGTH // 2 - 1)
            migration = jnp.where(low, low_migration, high_migration)
            scaling = jnp.where(low, low_scaling, high_scaling)
            offset = jnp.where(low, bins, bins - LENGTH) - center
            lagged = time - 0.2 * scaling
            cosine, sine = turn(-150.0 * scaling * lagged * lagged)
            one[0, q, g] = cosine
            one[1, q, g] = sine
            cosine, sine = turn(
                rate[here, :] * (migration - 1.0) + 150.0 * scaling * (1.0 + scaling) * time * time
            )
            wide = aperture[pl.ds(pl.multiple_of(g * WIDTH, WIDTH), WIDTH)].reshape(1, WIDTH)
            keep = jnp.where(2 * jnp.abs(offset) < wide, 1.0 / TOTAL, 0.0)
            three[0, q, g] = cosine * keep
            three[1, q, g] = sine * keep
            frequency = (GROUPS * lane + g - jnp.where(lane >= HALF, TOTAL, 0)).astype(F32)
            cosine, sine = turn((square_gain * frequency + linear_gain) * frequency)
            two[0, q, g] = cosine
            two[1, q, g] = sine
            return inner

        return lax.fori_loop(0, GROUPS, each_group, carry)

    lax.fori_loop(0, CLASSES, phases, 0)

    sibling = (az, me + 1 - 2 * core)

    def swap(q):
        return pltpu.make_async_remote_copy(
            src_ref=got.at[q, core],
            dst_ref=got.at[q, core],
            send_sem=swap_send.at[q],
            recv_sem=swap_recv.at[q],
            device_id=sibling,
            device_id_type=MESH,
        )

    def arrive(q):
        lot = got.at[q, core]
        pltpu.make_async_copy(lot, lot, made_recv.at[q]).wait()
        swap(q).start()

    upper_rows = lax.broadcasted_iota(jnp.int32, (ROWS, HALF), 0) < LINES
    flip = jnp.where(upper_rows, 1.0, -1.0).astype(F32)
    first_before = core.astype(F32)
    last_after = 1.0 - first_before

    def turned_rows(value):
        return pltpu.roll(value, LINES, 0)

    def range_work(q, carry):
        @pl.when(q < CLASSES - 1)
        def _():
            arrive(q + 1)

        swap(q).wait_recv()
        c_one, s_one = weight(q, 1, 0), weight(q, 1, 1)
        c_two, s_two = weight(q, 2, 0), weight(q, 2, 1)

        def block(segment, g, columns):
            value = got[q, core, segment, g, :, columns]
            before = got[q, 1 - core, jnp.maximum(segment - 1 + core, 0), g, :, columns]
            after = got[q, 1 - core, jnp.minimum(segment + core, 3), g, :, columns]
            if segment == 0:
                before = before * first_before
            if segment == 3:
                after = after * last_after
            value = value + c_one * (after + before)
            side = s_one * (after - before)
            if segment > 0:
                before = got[q, core, segment - 1, g, :, columns]
                value = value + c_two * before
                side = side - s_two * before
            if segment < 3:
                after = got[q, core, segment + 1, g, :, columns]
                value = value + c_two * after
                side = side + s_two * after
            return value + flip * turned_rows(side)

        for upper in range(2):
            for side in range(2):
                columns = slice(side * HALF, (side + 1) * HALF)
                values = []
                for g in range(GROUPS):
                    first, second = (block(2 * upper + i, g, columns) for i in range(2))
                    real = jnp.where(upper_rows, first, turned_rows(second))
                    imag = jnp.where(upper_rows, turned_rows(first), second)
                    cosine, sine = one[0, q, g, :, columns], one[1, q, g, :, columns]
                    values.append((real * cosine - imag * sine, real * sine + imag * cosine))
                values = sixteen(values, -1)
                for g in range(GROUPS):
                    real, imag = values[g]
                    cosine, sine = twiddle[0, g : g + 1, columns], twiddle[1, g : g + 1, columns]
                    values[g] = (real * cosine + imag * sine, imag * cosine - real * sine)
                for g in range(0, GROUPS, 2):
                    spot = slice(upper * HALF + g * 8, upper * HALF + g * 8 + 16)
                    for part in range(2):
                        both = jnp.concatenate([values[g][part], values[g + 1][part]], axis=0)
                        lanes = slice(part * WIDTH + side * HALF, part * WIDTH + (side + 1) * HALF)
                        left[0, spot, lanes], left[1, spot, lanes] = split(both)
        for upper in range(2):
            area = slice(upper * HALF, (upper + 1) * HALF)
            mixed[area, :] = (
                dot(left[0, area, :], dense[0, 0])
                + dot(left[0, area, :], dense[0, 1])
                + dot(left[1, area, :], dense[0, 0])
            )
        for upper in range(2):
            for g in range(0, GROUPS, 2):
                spot = slice(upper * HALF + g * 8, upper * HALF + g * 8 + 16)
                real, imag = mixed[spot, :WIDTH], mixed[spot, WIDTH:]
                cosine = jnp.concatenate([two[0, q, g], two[0, q, g + 1]], axis=0)
                sine = jnp.concatenate([two[1, q, g], two[1, q, g + 1]], axis=0)
                left[0, spot, :WIDTH], left[1, spot, :WIDTH] = split(real * cosine - imag * sine)
                left[0, spot, WIDTH:], left[1, spot, WIDTH:] = split(real * sine + imag * cosine)
        for upper in range(2):
            area = slice(upper * HALF, (upper + 1) * HALF)
            mixed[area, :] = (
                dot(left[0, area, :], dense[1, 0])
                + dot(left[0, area, :], dense[1, 1])
                + dot(left[1, area, :], dense[1, 0])
            )
        for upper in range(2):
            for side in range(2):
                columns = slice(side * HALF, (side + 1) * HALF)
                values = []
                for g in range(GROUPS):
                    spot = slice(upper * HALF + g * 8, upper * HALF + g * 8 + 8)
                    real = mixed[spot, side * HALF : (side + 1) * HALF]
                    imag = mixed[spot, WIDTH + side * HALF : WIDTH + (side + 1) * HALF]
                    cosine, sine = twiddle[0, g : g + 1, columns], twiddle[1, g : g + 1, columns]
                    values.append((real * cosine - imag * sine, real * sine + imag * cosine))
                values = sixteen(values, 1)
                for g in range(GROUPS):
                    real, imag = values[g]
                    cosine, sine = three[0, q, g, :, columns], three[1, q, g, :, columns]
                    real, imag = real * cosine - imag * sine, real * sine + imag * cosine
                    first = 2 * upper * GROUPS + g
                    back[q, first, :, columns] = jnp.where(upper_rows, real, turned_rows(imag))
                    back[q, first + GROUPS, :, columns] = jnp.where(
                        upper_rows, turned_rows(real), imag
                    )
        for dz, dx, dy, dc in HOMEWARD:
            target = place(zs[dz], near[dx], ys[dy], cores[dc])
            piece = zs[dz] * GROUPS + target[1]

            def send():
                pltpu.make_async_remote_copy(
                    src_ref=back.at[q, piece],
                    dst_ref=home.at[q, chip],
                    send_sem=back_send.at[q],
                    recv_sem=back_recv.at[q],
                    device_id=target,
                    device_id_type=MESH,
                ).start()

            def keep():
                pltpu.make_async_copy(
                    back.at[q, piece], home.at[q, chip], back_recv.at[q]
                ).start()

            if (dz, dx, dy, dc) == (0, 0, 0, 0):
                pl.when(jnp.logical_not(same))(send)
                pl.when(same)(keep)
            else:
                send()
        return carry

    arrive(0)
    loads[6].wait()
    lax.fori_loop(0, CLASSES, range_work, 0)

    def drain(buffer, semaphore, q):
        @pl.when(same)
        def _():
            lot = buffer.at[q, pl.ds(0, CHIPS - 1)]
            pltpu.make_async_copy(lot, lot, semaphore.at[q]).wait()

        @pl.when(jnp.logical_not(same))
        def _():
            lot = buffer.at[q]
            pltpu.make_async_copy(lot, lot, semaphore.at[q]).wait()

    def drain_forward(q, carry):
        swap(q).wait_send()
        drain(made, made_send, q)
        return carry

    lax.fori_loop(0, CLASSES, drain_forward, 0)

    loads[7].wait()

    def focused(q):
        lot = home.at[q]
        pltpu.make_async_copy(lot, lot, back_recv.at[q]).wait()
        high, low = split(home[q].reshape(CHIPS * ROWS, WIDTH))
        return dot(inverse[q, 0], high) + dot(inverse[q, 1], high) + dot(inverse[q, 0], low)

    total[...] = focused(0)

    def focus(q, carry):
        total[...] += focused(q)
        drain(back, back_send, q - 1)
        return carry

    lax.fori_loop(1, CLASSES - 1, focus, 0)
    drain(back, back_send, CLASSES - 2)
    result = total[...] + focused(CLASSES - 1)
    out[0] = result[:SEG, :]
    out[1] = result[SEG:, :]
    drain(back, back_send, CLASSES - 1)


def per_device(tables, echo, range_row, aperture, centroid_table, rate_table):
    hbm = pl.BlockSpec(memory_space=pltpu.HBM)
    semaphore = pltpu.SemaphoreType.DMA
    return pl.pallas_call(
        kernel,
        out_shape=pltpu.VMEM((2, SEG, WIDTH), F32),
        in_specs=[hbm] * 9,
        out_specs=pl.BlockSpec(memory_space=pltpu.VMEM),
        scratch_shapes=[
            pltpu.VMEM((2, SEG, WIDTH), F32),
            pltpu.VMEM((2, 2 * SEG, WIDTH), BF16),
            pltpu.VMEM((TOTAL,), jnp.int32),
            pltpu.VMEM((TOTAL,), jnp.int32),
            pltpu.SMEM((64,), jnp.int32),
            pltpu.SMEM((64,), F32),
            pltpu.VMEM((CLASSES, 2, 2 * SEG, 2 * SEG), BF16),
            pltpu.VMEM((CLASSES, 2, 2 * SEG, 2 * SEG), BF16),
            pltpu.VMEM((2, 2, 2 * WIDTH, 2 * WIDTH), BF16),
            pltpu.VMEM((2, GROUPS, WIDTH), F32),
            pltpu.VMEM((CLASSES, CHIPS, ROWS, WIDTH), F32),
            pltpu.VMEM((CLASSES, 2, PAIRS, GROUPS, ROWS, WIDTH), F32),
            pltpu.VMEM((CLASSES, CHIPS, ROWS, WIDTH), F32),
            pltpu.VMEM((CLASSES, CHIPS, ROWS, WIDTH), F32),
            pltpu.VMEM((2, CLASSES, GROUPS, ROWS, WIDTH), F32),
            pltpu.VMEM((2, CLASSES, GROUPS, ROWS, WIDTH), F32),
            pltpu.VMEM((2, CLASSES, GROUPS, ROWS, WIDTH), F32),
            pltpu.VMEM((GROUPS, WIDTH), jnp.int32),
            pltpu.VMEM((GROUPS, WIDTH), F32),
            pltpu.VMEM((2, 2 * HALF, 2 * WIDTH), BF16),
            pltpu.VMEM((2 * HALF, 2 * WIDTH), F32),
            pltpu.VMEM((2 * SEG, WIDTH), F32),
            semaphore((8,)),
            semaphore((CLASSES,)),
            semaphore((CLASSES,)),
            semaphore((CLASSES,)),
            semaphore((CLASSES,)),
            semaphore((CLASSES,)),
            semaphore((CLASSES,)),
            semaphore((CLASSES,)),
        ],
        compiler_params=pltpu.CompilerParams(
            collective_id=0, has_side_effects=True, vmem_limit_bytes=52 * 1024 * 1024
        ),
    )(
        *(
            pltpu.with_memory_space_constraint(operand, pltpu.HBM)
            for operand in (echo, range_row, aperture, centroid_table, rate_table, *tables)
        )
    )


def solution(mesh):
    forward, inverse = azimuth_tables()
    dense, twiddle = range_tables()
    tables = tuple(jnp.asarray(table) for table in (forward, inverse, dense, twiddle))
    in_specs = (P(None, "az", "rg"), P(), P(), P(), P())
    out_specs = P(None, "az", "rg")
    return jax.shard_map(
        partial(per_device, tables),
        mesh=mesh,
        in_specs=in_specs,
        out_specs=out_specs,
        check_vma=False,
    )
```
